32 devices in a mesh: dp: 16 (over z, x, core), head: 2 (over y).
Axes of the slice: x: 2, y: 2, z: 4, core: 2. Of those that a mesh axis runs over, the one named last changes fastest.
Arguments:
- stream_x: bfloat16 [32768, 512], P(('dp', 'head')), may hold values from -6 to 6
- stream_y: bfloat16 [32768, 512], P(('dp', 'head')), may hold values from -6 to 6
- segments: int32 [32768], P('dp'), may hold values from 0 to 8, as said below
- keep_mask: int32 [32768], P('dp'), may hold values 0 or 1
- query_weight: bfloat16 [512, 512], P(None, 'head'), may hold values from -0.25 to 0.25
- key_weight: bfloat16 [512, 512], P(None, 'head'), may hold values from -0.25 to 0.25
- value_weight: bfloat16 [512, 512], P(None, 'head'), may hold values from -0.25 to 0.25
- output_weight: bfloat16 [512, 512], P('head'), may hold values from -1.5 to 1.5
- first_gain: float32 [512], replicated, may hold values from 0.5 to 1.5
- first_shift: float32 [512], replicated, may hold values from -2 to 2
- up_weight: bfloat16 [2048, 512], P(('dp', 'head')), may hold values from -0.25 to 0.25
- down_weight: bfloat16 [2048, 512], P(('dp', 'head')), may hold values from -0.125 to 0.125
- second_gain: float32 [512], replicated, may hold values from 0.5 to 1.5
- second_shift: float32 [512], replicated, may hold values from -2 to 2
- grad_stream: bfloat16 [32768, 512], P(('dp', 'head')), may hold values from -6 to 6
- grad_dual: bfloat16 [32768, 512], P(('dp', 'head')), may hold values from -6 to 6
Outputs:
- new_stream: bfloat16 [32768, 512], P(('dp', 'head'))
- new_dual: bfloat16 [32768, 512], P(('dp', 'head'))
- stream_grad: float32 [32768, 512], P(('dp', 'head'))
- query_grad: float32 [512, 512], P(None, 'head')
- key_grad: float32 [512, 512], P(None, 'head')
- value_grad: float32 [512, 512], P(None, 'head')
- output_grad: float32 [512, 512], P('head')
- first_gain_grad: float32 [512], replicated
- first_shift_grad: float32 [512], replicated
- up_grad: float32 [2048, 512], P(('dp', 'head'))
- down_grad: float32 [2048, 512], P(('dp', 'head'))
- second_gain_grad: float32 [512], replicated
- second_shift_grad: float32 [512], replicated
The draws below stay inside these ranges and needn't reach their ends.
Inputs may be any that keep to these rules, and one draw needn't show every extreme that they name: `segments`: within each sequence of 1024 tokens the ids never fall; equal ids mark one document. Each sequence begins with id 0 and ends with the largest id.
All inputs are finite; a program needn't handle non-finite values. No bound on the sum of `keep_mask` on one device may be relied on, other than what follows from the above.
Results may differ from the reference program's by a relative error of at most 0.018.
Values may be sent and summed in bfloat16 or wider, within the bound.
No kernel may reach another device: no remote copies, remote signals or barrier semaphores. Data moves between devices by JAX's collectives and lax.ppermute only.
A program may use at most 128 MiB of HBM per device.

```python
import math
from functools import partial
import jax
import jax.numpy as jnp
from jax import lax

D = 512
HEADS = 8
FF = 2048
SEQ = 1024
TOKENS = 32768


def draw_segments(key, part):
    key = jax.random.fold_in(key, 11)
    groups = TOKENS // SEQ
    quarter = SEQ // 4
    first_key, second_key, third_key, fourth_key = jax.random.split(key, 4)
    big_start = jax.random.randint(first_key, (groups, 1), 1, quarter)
    big_end = jax.random.randint(second_key, (groups, 1), SEQ - quarter + 1, SEQ - quarter // 2)
    early_cuts = jnp.minimum(jax.random.randint(third_key, (groups, 3), 1, quarter), big_start)
    later_cuts = jax.random.randint(fourth_key, (groups, 3), SEQ - quarter // 2, SEQ)
    cut_points = jnp.concatenate([big_start, big_end, early_cuts, later_cuts], axis=1)
    position = jnp.arange(SEQ, dtype=jnp.int32)
    doc_ids = jnp.sum((position[None, :, None] >= cut_points[:, None, :]).astype(jnp.int32), axis=-1)
    return doc_ids.reshape(TOKENS).astype(jnp.int32)


def with_ends(entries, rng, low, largest):
    longest = entries.shape.index(max(entries.shape))
    spots = []
    for shift in (0, 1):
        where = [jax.random.randint(jax.random.fold_in(rng, axis), (), 0, length) for axis, length in enumerate(entries.shape)]
        where[longest] = (where[longest] + shift) % entries.shape[longest]
        spots.append(tuple(where))
    return entries.at[spots[0]].set(low).at[spots[1]].set(largest)


def level_of(key, extent, pieces, least, largest):
    loudness = 1.0
    for dim, blocks in pieces:
        draws = jax.random.uniform(jax.random.fold_in(jax.random.fold_in(key, 6), dim), (blocks,), jnp.float32, least / len(pieces), largest / len(pieces))
        loudness = loudness * jnp.repeat(jnp.exp(draws), extent[dim] // blocks).reshape((-1,) + (1,) * (len(extent) - 1 - dim))
    return loudness


def bell_draw(rng, shape, spread, limit, cuts=(), kind=jnp.bfloat16):
    result = spread * jax.random.normal(rng, shape, jnp.float32)
    if cuts:
        result = result * level_of(rng, shape, cuts, -0.22, 0.18)
    return jnp.clip(result, -limit, limit).astype(kind)


def setup_inputs(seed: int = 0) -> dict:
    key_of = jax.random.split(jax.random.key(seed), 17)
    stream_x = bell_draw(key_of[0], (TOKENS, D), 1.0, 6.0, ((0, 32),))
    stream_y = bell_draw(key_of[1], (TOKENS, D), 1.0, 6.0, ((0, 32),))
    segments = draw_segments(jax.random.fold_in(key_of[16], 71), 0)
    keep_mask = with_ends((jax.random.randint(key_of[3], (TOKENS,), 0, 4) < 3).astype(jnp.int32), jax.random.fold_in(key_of[3], 1), 0, 1)
    query_weight = bell_draw(key_of[4], (D, D), D ** -0.5, 0.25, ((1, 2),))
    key_weight = bell_draw(key_of[5], (D, D), D ** -0.5, 0.25, ((1, 2),))
    value_weight = bell_draw(key_of[6], (D, D), D ** -0.5, 0.25, ((1, 2),))
    output_weight = bell_draw(key_of[7], (D, D), (D // 32) ** -0.5, 1.5, ((0, 2),))
    first_gain = jnp.clip(1.0 + 0.1 * jax.random.normal(key_of[8], (D,), jnp.float32), 0.5, 1.5)
    first_shift = bell_draw(key_of[9], (D,), 0.3, 2.0, (), jnp.float32)
    up_weight = bell_draw(key_of[10], (FF, D), D ** -0.5, 0.25, ((0, 32),))
    down_weight = bell_draw(key_of[11], (FF, D), FF ** -0.5, 0.125, ((0, 32),))
    second_gain = jnp.clip(1.0 + 0.1 * jax.random.normal(key_of[12], (D,), jnp.float32), 0.5, 1.5)
    second_shift = bell_draw(key_of[13], (D,), 0.3, 2.0, (), jnp.float32)
    grad_stream = bell_draw(key_of[14], (TOKENS, D), 1.0, 6.0, ((0, 32),))
    grad_dual = bell_draw(key_of[15], (TOKENS, D), 1.0, 6.0, ((0, 32),))
    return dict(stream_x=stream_x, stream_y=stream_y, segments=segments, keep_mask=keep_mask, query_weight=query_weight, key_weight=key_weight, value_weight=value_weight, output_weight=output_weight, first_gain=first_gain, first_shift=first_shift, up_weight=up_weight, down_weight=down_weight, second_gain=second_gain, second_shift=second_shift, grad_stream=grad_stream, grad_dual=grad_dual)


@jax.custom_vjp
def low(v):
    return lax.optimization_barrier(v.astype(jnp.bfloat16)).astype(jnp.float32)

@jax.custom_vjp
def low_back(v):
    return v

def low_keep(v):
    return (low(v), None)

def low_pass(kept, grad):
    return (grad,)

def back_keep(v):
    return (v, None)

def back_low(kept, grad):
    return (low(grad),)
low.defvjp(low_keep, low_pass)
low_back.defvjp(back_keep, back_low)
highest = lax.Precision.HIGHEST
epsilon = 1e-05

def layer_norm(values, gain_vec, shift_vec):
    row_mean = lax.optimization_barrier(jnp.mean(values, axis=-1, keepdims=True))
    centred = values - row_mean
    variance = lax.optimization_barrier(jnp.mean(centred * centred, axis=-1, keepdims=True))
    return centred * lax.rsqrt(variance + epsilon) * gain_vec + shift_vec

def allowed_mask(offset, length, seg_ids, keep_ids):
    query_pos = offset + jnp.arange(length, dtype=jnp.int32)
    key_pos = jnp.arange(seg_ids.shape[0], dtype=jnp.int32)
    query_seg = lax.dynamic_slice_in_dim(seg_ids, offset, length)
    same_doc = query_seg[:, None] == seg_ids[None, :]
    causal = key_pos[None, :] <= query_pos[:, None]
    visible = (keep_ids[None, :] == 1) | (key_pos[None, :] == query_pos[:, None])
    return same_doc & causal & visible

def attend_block(queries, key_rows, values, seg_ids, keep_ids, block_len, offset):
    score_scale = 1.0 / math.sqrt(queries.shape[-1])
    query_block = lax.dynamic_slice_in_dim(queries, offset, block_len, 1)
    scores = low_back(jnp.einsum('hqd,hkd->hqk', query_block, key_rows, precision=highest) * score_scale)
    allowed = allowed_mask(offset, block_len, seg_ids, keep_ids)[None]
    scores = jnp.where(allowed, scores, -1e+30)
    row_max = lax.optimization_barrier(jnp.max(scores, axis=-1, keepdims=True))
    exp_terms = jnp.exp(scores - row_max)
    probability = exp_terms / lax.optimization_barrier(jnp.sum(exp_terms, axis=-1, keepdims=True))
    return jnp.einsum('hqk,hkd->hqd', low(probability), values, precision=highest)

def layer_forward(seg_ids, keep_ids, stream, dual_in, params):
    query_weight, key_weight, value_weight, output_weight, first_gain, first_shift, up_weight, down_weight, second_gain, second_shift = params
    seq_tokens, model_width = stream.shape
    head_dim = model_width // HEADS

    def heads_of(matrix):
        projected = low(low_back(jnp.dot(stream, matrix, precision=highest)))
        return projected.reshape(seq_tokens, HEADS, head_dim).transpose(1, 0, 2)
    queries = heads_of(query_weight)
    key_rows = heads_of(key_weight)
    values = heads_of(value_weight)
    block_len = min(512, seq_tokens)
    starts = jnp.arange(seq_tokens // block_len, dtype=jnp.int32) * block_len
    attend = jax.checkpoint(partial(attend_block, queries, key_rows, values, seg_ids, keep_ids, block_len))
    attended = lax.map(attend, starts)
    attended = attended.transpose(0, 2, 1, 3).reshape(seq_tokens, model_width)
    attended = low(low_back(attended))
    branch = low_back(jnp.dot(attended, output_weight, precision=highest))
    first_out = layer_norm(stream + branch, first_gain, first_shift)
    hidden = low_back(jnp.dot(low(first_out), up_weight.T, precision=highest))
    activated = low(jax.nn.gelu(hidden, approximate=False))
    ffn_out = low_back(jnp.dot(activated, down_weight, precision=highest))
    new_stream = layer_norm(first_out + ffn_out, second_gain, second_shift)
    new_dual = dual_in + branch + ffn_out
    return (new_stream, new_dual)

def reference(stream_x, stream_y, segments, keep_mask, query_weight, key_weight, value_weight, output_weight, first_gain, first_shift, up_weight, down_weight, second_gain, second_shift, grad_stream, grad_dual):
    groups = TOKENS // SEQ
    params = tuple((member.astype(jnp.float32) for member in (query_weight, key_weight, value_weight, output_weight, first_gain, first_shift, up_weight, down_weight, second_gain, second_shift)))

    def by_sequence(array):
        return array.reshape((groups, SEQ) + array.shape[1:])
    inputs = (by_sequence(stream_x.astype(jnp.float32)), by_sequence(stream_y.astype(jnp.float32)), by_sequence(segments), by_sequence(keep_mask), by_sequence(grad_stream.astype(jnp.float32)), by_sequence(grad_dual.astype(jnp.float32)))

    def one_sequence(totals, items):
        stream, dual_in, seg_ids, keep_ids, cot_stream, cot_dual = items
        results, pullback = jax.vjp(partial(layer_forward, seg_ids, keep_ids), stream, dual_in, params)
        grad_in, grad_other, grad_params = pullback((cot_stream, cot_dual))
        totals = jax.tree.map(lambda running, member: running + member, totals, grad_params)
        return (totals, (results[0], results[1], grad_in))
    initial = tuple((jnp.zeros(member.shape, jnp.float32) for member in params))
    totals, outputs = lax.scan(one_sequence, initial, inputs)
    new_stream, new_dual, stream_grad = outputs
    return (new_stream.reshape(TOKENS, D).astype(jnp.bfloat16), new_dual.reshape(TOKENS, D).astype(jnp.bfloat16), stream_grad.reshape(TOKENS, D), totals[0], totals[1], totals[2], totals[3], totals[4], totals[5], totals[6], totals[7], totals[8], totals[9])
```

```python
import math
import functools
import jax
import jax.numpy as jnp
from jax import lax
from jax.experimental import pallas as pl
from jax.experimental.pallas import tpu as pltpu
from jax.sharding import PartitionSpec as P

HEADS = 8

BF = jnp.bfloat16
F32 = jnp.float32
LOG2E = 1.4426950408889634
NEG = -1e30
BLK = 256
MIB = 1 << 20

def nn(a, b):
    return lax.dot_general(a, b, (((1,), (0,)), ((), ())), preferred_element_type=F32)
def nt(a, b):
    return lax.dot_general(a, b, (((1,), (1,)), ((), ())), preferred_element_type=F32)
def tn(a, b):
    return lax.dot_general(a, b, (((0,), (0,)), ((), ())), preferred_element_type=F32)

def fill_mask(seg_ref, keep_ref, mask_ref):
    seq = mask_ref.shape[0]
    seg = seg_ref[...]
    code = jnp.where(keep_ref[...] == 1, seg, -1)
    code_col = jnp.broadcast_to(code.astype(F32), (128, seq)).T
    seg_row = seg.astype(F32)
    for kb in range(seq // BLK):
        rows = slice(kb * BLK, (kb + 1) * BLK)
        width = seq - kb * BLK
        same = jnp.concatenate([code_col[rows]] * (width // 128), axis=1) == seg_row[:, kb * BLK:]
        key = lax.broadcasted_iota(jnp.int32, (BLK, width), 0)
        query = lax.broadcasted_iota(jnp.int32, (BLK, width), 1)
        ok = (same & (key <= query)) | (key == query)
        mask_ref[rows, kb * BLK:] = jnp.where(ok, 0.0, NEG)

def lane_half(arr, h):
    lane = lax.broadcasted_iota(jnp.int32, arr.shape, 1)
    return jnp.where((lane < 64) if h == 0 else (lane >= 64), arr, jnp.zeros_like(arr))

def attn_fwd_kernel(scale, x_ref, wq_ref, wk_ref, wv_ref, seg_ref, keep_ref,
                    q_ref, k_ref, v_ref, att_ref, lse_ref, mask_ref):
    seq = x_ref.shape[0]
    @pl.when(pl.program_id(0) == 0)
    def _():
        fill_mask(seg_ref, keep_ref, mask_ref)
    x = x_ref[...]
    q_ref[...] = nn(x, wq_ref[...]).astype(BF)
    k_ref[...] = nn(x, wk_ref[...]).astype(BF)
    v = nn(x, wv_ref[...]).astype(BF)
    v_ref[...] = v
    v_t = v.T
    for qb in range(seq // BLK):
        cols = slice(qb * BLK, (qb + 1) * BLK)
        length = (qb + 1) * BLK
        outs = []
        for h in range(2):
            qm = lane_half(q_ref[cols, :], h)
            s = nt(k_ref[:length, :], qm) * (scale * LOG2E) + mask_ref[:length, cols]
            m = jnp.max(s, axis=0, keepdims=True)
            p = jnp.exp2(s - m)
            l = jnp.sum(p, axis=0, keepdims=True)
            o = nn(v_t[64 * h:64 * h + 64, :length], p.astype(BF))
            outs.append(o / l)
            lse_ref[0, h:h + 1, cols] = m + jnp.log2(l)
        att_ref[cols, :] = jnp.concatenate(outs, axis=0).T.astype(BF)

def proj_spec(width, which):
    return pl.BlockSpec((None, width, 128), lambda p: (which, 0, p))

def attn_fwd(x, proj, seg, keep, scale):
    seq, width = x.shape
    pairs = proj.shape[2] // 128
    ospec = pl.BlockSpec((seq, 128), lambda p: (0, p))
    full = lambda shape: pl.BlockSpec(shape, lambda p: (0,) * len(shape))
    o = jax.ShapeDtypeStruct((seq, 128 * pairs), BF)
    return pl.pallas_call(
        functools.partial(attn_fwd_kernel, scale),
        grid=(pairs,),
        in_specs=[full((seq, width)), proj_spec(width, 0), proj_spec(width, 1), proj_spec(width, 2), full((1, seq)), full((1, seq))],
        out_specs=[ospec, ospec, ospec, ospec, pl.BlockSpec((1, 2, seq), lambda p: (p, 0, 0))],
        out_shape=[o, o, o, o, jax.ShapeDtypeStruct((pairs, 2, seq), F32)],
        scratch_shapes=[pltpu.VMEM((seq, seq), F32)],
        compiler_params=pltpu.CompilerParams(vmem_limit_bytes=56 * MIB),
        cost_estimate=pl.CostEstimate(flops=10**10, bytes_accessed=10**7, transcendentals=0),
        name="attn_fwd",
    )(x, proj, proj, proj, seg, keep)

def attn_bwd_kernel(scale, pairs, x_ref, wq_ref, wk_ref, wv_ref, q_ref, k_ref, v_ref, att_ref, do_ref, lse_ref, seg_ref, keep_ref, gm_ref,
                    sg_ref, dw_ref, mask_ref, xt_ref, dqt_ref, dkv_ref, acc_ref):
    seq = x_ref.shape[0]
    step = pl.program_id(0)
    @pl.when(step == 0)
    def _():
        fill_mask(seg_ref, keep_ref, mask_ref)
        xt_ref[...] = x_ref[...].T
        acc_ref[...] = gm_ref[...]
    prod = (do_ref[...].astype(F32) * att_ref[...].astype(F32)).T
    k_t = k_ref[...].T
    nb = seq // BLK
    for h in range(2):
        delta = jnp.sum(prod[64 * h:64 * h + 64], axis=0, keepdims=True)
        lse = lse_ref[0, h:h + 1, :]
        for kb in range(nb):
            rows = slice(kb * BLK, (kb + 1) * BLK)
            lo = kb * BLK
            qm = lane_half(q_ref[lo:, :], h)
            dom = lane_half(do_ref[lo:, :], h)
            s = nt(k_ref[rows, :], qm) * (scale * LOG2E) + mask_ref[rows, lo:]
            p = jnp.exp2(s - lse[:, lo:])
            dp = nt(v_ref[rows, :], dom)
            ds = (p * (dp - delta[:, lo:])).astype(BF)
            dv = nn(p.astype(BF), dom)
            dk = nn(ds, qm) * scale
            dq = nn(k_t[64 * h:64 * h + 64, rows], ds)
            if h == 0:
                dkv_ref[rows, 0:128] = dk
                dkv_ref[rows, 128:256] = dv
            else:
                dkv_ref[rows, 0:128] += dk
                dkv_ref[rows, 128:256] += dv
            if kb == 0:
                dqt_ref[64 * h:64 * h + 64, :] = dq
            else:
                dqt_ref[64 * h:64 * h + 64, lo:] += dq
    dq = (dqt_ref[...] * scale).T.astype(BF)
    g = jnp.concatenate([dq, dkv_ref[...].astype(BF)], axis=1)
    dw_ref[0] = nn(xt_ref[...], g).astype(BF)
    w = jnp.concatenate([wq_ref[...], wk_ref[...], wv_ref[...]], axis=1)
    acc_ref[...] += nt(g, w)
    @pl.when(step == pairs - 1)
    def _():
        sg_ref[...] = acc_ref[...]

def attn_bwd(x, proj, q, k, v, att, do, lse, seg, keep, gm, scale):
    seq, width = x.shape
    pairs = proj.shape[2] // 128
    ospec = pl.BlockSpec((seq, 128), lambda p: (0, p))
    full = lambda shape: pl.BlockSpec(shape, lambda p: (0,) * len(shape))
    return pl.pallas_call(
        functools.partial(attn_bwd_kernel, scale, pairs),
        grid=(pairs,),
        in_specs=[full((seq, width)), proj_spec(width, 0), proj_spec(width, 1), proj_spec(width, 2), ospec, ospec, ospec, ospec, ospec, pl.BlockSpec((1, 2, seq), lambda p: (p, 0, 0)), full((1, seq)), full((1, seq)), full((seq, width))],
        out_specs=[full((seq, width)), pl.BlockSpec((1, width, 384), lambda p: (p, 0, 0))],
        out_shape=[jax.ShapeDtypeStruct((seq, width), F32), jax.ShapeDtypeStruct((pairs, width, 384), BF)],
        scratch_shapes=[pltpu.VMEM((seq, seq), F32), pltpu.VMEM((width, seq), BF), pltpu.VMEM((128, seq), F32), pltpu.VMEM((seq, 256), F32), pltpu.VMEM((seq, width), F32)],
        compiler_params=pltpu.CompilerParams(vmem_limit_bytes=56 * MIB),
        cost_estimate=pl.CostEstimate(flops=10**10, bytes_accessed=10**7, transcendentals=0),
        name="attn_bwd",
    )(x, proj, proj, proj, q, k, v, att, do, lse, seg, keep, gm)

def gelu_parts(h):
    e = jnp.exp2(h * h * (-0.5 * LOG2E))
    t = pl.reciprocal(1.0 + (0.3275911 / math.sqrt(2.0)) * jnp.abs(h), approx=False)
    poly = ((((0.5 * 1.061405429) * t - 0.5 * 1.453152027) * t + 0.5 * 1.421413741) * t - 0.5 * 0.284496736) * t + 0.5 * 0.254829592
    tail = poly * t * e
    phi = jnp.where(h >= 0, 1.0 - tail, tail)
    return h * phi, phi + h * e * (1.0 / math.sqrt(2.0 * math.pi))

def mean_of(v):
    return jnp.sum(v, axis=-1, keepdims=True) * (1.0 / v.shape[-1])

def dense_kernel(x_ref, y_ref, att_ref, gs_ref, gd_ref, wo_ref, up_ref, down_ref, g1_ref, b1_ref, g2_ref, b2_ref,
                 ns_ref, nd_ref, act_ref, dh_ref, gf_ref, fl_ref, gm_ref, gb_ref, do_ref, vec_ref, der_ref):
    @pl.when(pl.program_id(0) == 0)
    def _():
        vec_ref[...] = jnp.zeros_like(vec_ref)
    branch = nn(att_ref[...], wo_ref[...])
    mixed = x_ref[...].astype(F32) + branch
    c1 = mixed - mean_of(mixed)
    rstd1 = lax.rsqrt(mean_of(c1 * c1) + 1e-5)
    zhat1 = c1 * rstd1
    first = zhat1 * g1_ref[...] + b1_ref[...]
    low = first.astype(BF)
    fl_ref[...] = low
    ff = up_ref.shape[0]
    CH = 512
    for c in range(ff // CH):
        cs = slice(c * CH, (c + 1) * CH)
        val, der = gelu_parts(nt(low, up_ref[cs, :]))
        act_ref[:, cs] = val.astype(BF)
        der_ref[:, cs] = der
    ffn = nn(act_ref[...], down_ref[...])
    z2 = first + ffn
    c2 = z2 - mean_of(z2)
    rstd2 = lax.rsqrt(mean_of(c2 * c2) + 1e-5)
    zhat2 = c2 * rstd2
    ns_ref[...] = (zhat2 * g2_ref[...] + b2_ref[...]).astype(BF)
    nd_ref[...] = (y_ref[...].astype(F32) + branch + ffn).astype(BF)
    u = gs_ref[...].astype(F32)
    w = u * g2_ref[...]
    second = rstd2 * (w - mean_of(w) - zhat2 * mean_of(w * zhat2))
    gd = gd_ref[...].astype(F32)
    gf = (second + gd).astype(BF)
    gf_ref[...] = gf
    for c in range(ff // CH):
        cs = slice(c * CH, (c + 1) * CH)
        dh_ref[:, cs] = (nt(gf, down_ref[cs, :]) * der_ref[:, cs]).astype(BF)
    gfirst = second + nn(dh_ref[...], up_ref[...])
    w1 = gfirst * g1_ref[...]
    gm = rstd1 * (w1 - mean_of(w1) - zhat1 * mean_of(w1 * zhat1))
    gm_ref[...] = gm
    gb = (gm + gd).astype(BF)
    gb_ref[...] = gb
    do_ref[...] = nt(gb, wo_ref[...]).astype(BF)
    fold = lambda v: jnp.sum(v, axis=0, keepdims=True)
    vec_ref[...] += jnp.concatenate([fold(gfirst * zhat1), fold(gfirst), fold(u * zhat2), fold(u), jnp.zeros((4, u.shape[1]), F32)], axis=0)

def dense(x, y, att, gs, gd, wo, ffw, g1, b1, g2, b2, blk=256):
    seq, width = x.shape
    ff = ffw.shape[1]
    ffspec = lambda which: pl.BlockSpec((None, ff, width), lambda p: (which, 0, 0))
    row = lambda w: pl.BlockSpec((blk, w), lambda p: (p, 0))
    full = lambda shape: pl.BlockSpec(shape, lambda p: (0,) * len(shape))
    sd = lambda w, t: jax.ShapeDtypeStruct((seq, w), t)
    return pl.pallas_call(
        dense_kernel,
        grid=(seq // blk,),
        in_specs=[row(width)] * 5 + [full(wo.shape), ffspec(0), ffspec(1)] + [full((1, width))] * 4,
        out_specs=[row(width), row(width), row(ff), row(ff), row(width), row(width), row(width), row(width), row(width), full((8, width))],
        out_shape=[sd(width, BF), sd(width, BF), sd(ff, BF), sd(ff, BF), sd(width, BF), sd(width, BF), sd(width, F32), sd(width, BF), sd(width, BF), jax.ShapeDtypeStruct((8, width), F32)],
        scratch_shapes=[pltpu.VMEM((blk, ff), F32)],
        compiler_params=pltpu.CompilerParams(vmem_limit_bytes=56 * MIB),
        cost_estimate=pl.CostEstimate(flops=2 * 10**10, bytes_accessed=2 * 10**7, transcendentals=0),
        name="dense",
    )(x, y, att, gs, gd, wo, ffw, ffw, g1, b1, g2, b2)

def wgrad_kernel(a_ref, g_ref, dh_ref, fl_ref, out_ref):
    out_ref[0] = tn(dh_ref[...], fl_ref[...]).astype(BF)
    out_ref[1] = tn(a_ref[...], g_ref[...]).astype(BF)

def wgrad(act, gf, dh, fl, part, steps=2):
    seq, ff = act.shape
    width = gf.shape[1]
    b = ff // 2 // steps
    full = lambda shape: pl.BlockSpec(shape, lambda p: (0,) * len(shape))
    cols = pl.BlockSpec((seq, b), lambda p: (0, p + part * steps))
    return pl.pallas_call(
        wgrad_kernel,
        grid=(steps,),
        in_specs=[cols, full((seq, width)), cols, full((seq, width))],
        out_specs=pl.BlockSpec((2, b, width), lambda p: (0, p, 0)),
        out_shape=jax.ShapeDtypeStruct((2, ff // 2, width), BF),
        compiler_params=pltpu.CompilerParams(vmem_limit_bytes=56 * MIB),
        cost_estimate=pl.CostEstimate(flops=5 * 10**9, bytes_accessed=10**7, transcendentals=0),
        name="wgrad",
    )(act, gf, dh, fl)

def ograd_kernel(a_ref, g_ref, out_ref):
    out_ref[...] = tn(a_ref[...], g_ref[...]).astype(BF)

def ograd(att, gb):
    return pl.pallas_call(
        ograd_kernel,
        out_shape=jax.ShapeDtypeStruct((att.shape[1], gb.shape[1]), BF),
        compiler_params=pltpu.CompilerParams(vmem_limit_bytes=56 * MIB),
        cost_estimate=pl.CostEstimate(flops=10**9, bytes_accessed=2 * 10**6, transcendentals=0),
        name="ograd",
    )(att, gb)


def body(
    dp_size,
    head_size,
    stream_x,
    stream_y,
    segments,
    keep_mask,
    query_weight,
    key_weight,
    value_weight,
    output_weight,
    first_gain,
    first_shift,
    up_weight,
    down_weight,
    second_gain,
    second_shift,
    grad_stream,
    grad_dual,
):
    seq, width = stream_x.shape
    cols = query_weight.shape[1]
    scale = 1.0 / math.sqrt(width // HEADS)
    axes = ("dp", "head")
    total = dp_size * head_size
    core_step = head_size
    head_steps = [1 << b for b in range(head_size.bit_length() - 1)]
    chip_steps = [core_step << b for b in range(1, dp_size.bit_length() - 1)]

    def swap(value, even_step, odd_step=None):
        odd_step = even_step if odd_step is None else odd_step
        pairs = [
            (i, i ^ (odd_step if i // core_step % 2 else even_step)) for i in range(total)
        ]
        return lax.ppermute(value, axes, pairs)

    head_index = lax.axis_index("head")
    core = lax.axis_index("dp") % 2
    seg = lax.dynamic_slice_in_dim(segments, head_index * seq, seq).reshape(1, seq)
    keep = lax.dynamic_slice_in_dim(keep_mask, head_index * seq, seq).reshape(1, seq)

    proj = jnp.stack([query_weight, key_weight, value_weight])
    outw = output_weight
    for step in head_steps:
        proj = jnp.concatenate([proj, swap(proj, step)], axis=2)
        outw = jnp.concatenate([outw, swap(outw, step)], axis=0)

    even = [chip_steps[-1]] + chip_steps[:-1] + head_steps
    odd = [chip_steps[-1]] + chip_steps[1:-1] + head_steps + chip_steps[:1]
    ffw = jnp.stack([up_weight, down_weight])
    for a, b in zip(even, odd):
        ffw = jnp.concatenate([ffw, swap(ffw, a, b)], axis=1)
    ffw = jnp.concatenate([ffw, swap(ffw, core_step)], axis=1)

    q, k, v, att, lse = attn_fwd(stream_x, proj, seg, keep, scale)
    row = lambda vec: vec.reshape(1, width)
    ns, nd, act, dh, gf, low, gm, gb, do, vec = dense(
        stream_x, stream_y, att, grad_stream, grad_dual, outw, ffw,
        row(first_gain), row(first_shift), row(second_gain), row(second_shift),
    )
    half = ffw.shape[1] // 2
    upper = wgrad(act, gf, dh, low, 1)
    sent = swap(upper, core_step)
    lower = wgrad(act, gf, dh, low, 0)
    out_part = ograd(att, gb)
    part = lower + sent
    for a, b in zip(even[::-1], odd[::-1]):
        half = part.shape[1] // 2
        recv = swap(part[:, half:], a, b)
        if half == up_weight.shape[0]:
            part = part[:, :half].astype(F32) + recv.astype(F32)
        else:
            part = part[:, :half] + recv
    up_grad, down_grad = part[0], part[1]

    sg, dw = attn_bwd(stream_x, proj, q, k, v, att, do, lse, seg, keep, gm, scale)

    pairs = dw.shape[0]
    dw = dw.reshape(pairs, width, 3, 128).transpose(2, 1, 0, 3).reshape(3, width, width)
    for step in head_steps[::-1]:
        n = dw.shape[2] // 2
        dw = dw[:, :, :n] + swap(dw[:, :, n:], step)
        out_part = out_part[:n] + swap(out_part[n:], step)
        vec = vec + swap(vec, step)
    for step in [core_step] + chip_steps:
        dw = dw + swap(dw, step)
        out_part = out_part + swap(out_part, step)
        vec = vec + swap(vec, step)
    dw = dw.astype(F32)
    return (
        ns, nd, sg, dw[0], dw[1], dw[2], out_part.astype(F32),
        vec[0], vec[1], up_grad, down_grad, vec[2], vec[3],
    )


def solution(mesh):
    both = ("dp", "head")
    rows, cols, whole = P(both, None), P(None, "head"), P()
    in_specs = (
        rows, rows, P("dp"), P("dp"), cols, cols, cols, P("head", None),
        whole, whole, rows, rows, whole, whole, rows, rows,
    )
    out_specs = (
        rows, rows, rows, cols, cols, cols, P("head", None),
        whole, whole, rows, rows, whole, whole,
    )
    inner = functools.partial(body, mesh.shape["dp"], mesh.shape["head"])
    return jax.shard_map(inner, mesh=mesh, in_specs=in_specs, out_specs=out_specs, check_vma=False)
```

```python
import functools
import math

import jax
import jax.numpy as jnp
from jax import lax
from jax.experimental import pallas as pl
from jax.experimental.pallas import tpu as pltpu
from jax.sharding import PartitionSpec as P

HEADS = 8
BF = jnp.bfloat16
F32 = jnp.float32
LOG2E = 1.4426950408889634
NEG = -1e30
BLK = 256
MIB = 1 << 20
PAIR = 128
EXTRA = 32


def dot(a, b, left, right):
    return lax.dot_general(a, b, (((left,), (right,)), ((), ())), preferred_element_type=F32)


def nn(a, b):
    return dot(a, b, 1, 0)


def nt(a, b):
    return dot(a, b, 1, 1)


def tn(a, b):
    return dot(a, b, 0, 0)


def params(mib):
    return pltpu.CompilerParams(vmem_limit_bytes=mib * MIB)


def cost(us):
    return pl.CostEstimate(flops=int(us * 1e9), bytes_accessed=1 << 20, transcendentals=0)


def fill_mask(seg_ref, keep_ref, mask_ref):
    seq = mask_ref.shape[0]
    seg = seg_ref[...]
    code = jnp.where(keep_ref[...] == 1, seg, -1)
    code_col = jnp.broadcast_to(code.astype(F32), (128, seq)).T
    seg_row = seg.astype(F32)
    for kb in range(seq // BLK):
        rows = slice(kb * BLK, (kb + 1) * BLK)
        width = seq - kb * BLK
        same = jnp.concatenate([code_col[rows]] * (width // 128), axis=1) == seg_row[:, kb * BLK:]
        key = lax.broadcasted_iota(jnp.int32, (BLK, width), 0)
        query = lax.broadcasted_iota(jnp.int32, (BLK, width), 1)
        ok = (same & (key <= query)) | (key == query)
        mask_ref[rows, kb * BLK:] = jnp.where(ok, 0.0, NEG)


def lane_half(arr, h):
    lane = lax.broadcasted_iota(jnp.int32, arr.shape, 1)
    return jnp.where((lane < 64) if h == 0 else (lane >= 64), arr, jnp.zeros_like(arr))


def attn_fwd_kernel(scale, x_ref, w_ref, seg_ref, keep_ref, q_ref, k_ref, v_ref, att_ref, lse_ref, mask_ref):
    seq = x_ref.shape[0]
    fill_mask(seg_ref, keep_ref, mask_ref)
    x = x_ref[...]
    q_ref[...] = nn(x, w_ref[0]).astype(BF)
    k_ref[...] = nn(x, w_ref[1]).astype(BF)
    v = nn(x, w_ref[2]).astype(BF)
    v_ref[...] = v
    v_t = v.T
    for qb in range(seq // BLK):
        cols = slice(qb * BLK, (qb + 1) * BLK)
        length = (qb + 1) * BLK
        outs = []
        for h in range(2):
            qm = lane_half(q_ref[cols, :], h)
            s = nt(k_ref[:length, :], qm) * (scale * LOG2E) + mask_ref[:length, cols]
            m = jnp.max(s, axis=0, keepdims=True)
            p = jnp.exp2(s - m)
            l = jnp.sum(p, axis=0, keepdims=True)
            o = nn(v_t[64 * h:64 * h + 64, :length], p.astype(BF))
            outs.append(o / l)
            lse_ref[h:h + 1, cols] = m + jnp.log2(l)
        att_ref[cols, :] = jnp.concatenate(outs, axis=0).T.astype(BF)


def attn_fwd(x, w, seg, keep, scale):
    seq = x.shape[0]
    o = jax.ShapeDtypeStruct((seq, PAIR), BF)
    return pl.pallas_call(
        functools.partial(attn_fwd_kernel, scale),
        out_shape=[o, o, o, o, jax.ShapeDtypeStruct((2, seq), F32)],
        scratch_shapes=[pltpu.VMEM((seq, seq), F32)],
        compiler_params=params(32),
        cost_estimate=cost(6),
        name="attn_fwd",
    )(x, w, seg, keep)


def attn_bwd_kernel(scale, x_ref, q_ref, k_ref, v_ref, att_ref, do_ref, gb_ref, lse_ref, seg_ref, keep_ref,
                    g_ref, pay_ref, mask_ref, dqt_ref, dkv_ref):
    seq, width = x_ref.shape
    fill_mask(seg_ref, keep_ref, mask_ref)
    prod = (do_ref[...].astype(F32) * att_ref[...].astype(F32)).T
    k_t = k_ref[...].T
    for h in range(2):
        delta = jnp.sum(prod[64 * h:64 * h + 64], axis=0, keepdims=True)
        lse = lse_ref[h:h + 1, :]
        for kb in range(seq // BLK):
            rows = slice(kb * BLK, (kb + 1) * BLK)
            lo = kb * BLK
            qm = lane_half(q_ref[lo:, :], h)
            dom = lane_half(do_ref[lo:, :], h)
            s = nt(k_ref[rows, :], qm) * (scale * LOG2E) + mask_ref[rows, lo:]
            p = jnp.exp2(s - lse[:, lo:])
            dp = nt(v_ref[rows, :], dom)
            ds = (p * (dp - delta[:, lo:])).astype(BF)
            dv = nn(p.astype(BF), dom)
            dk = nn(ds, qm) * scale
            dq = nn(k_t[64 * h:64 * h + 64, rows], ds)
            if h == 0:
                dkv_ref[rows, 0:128] = dk
                dkv_ref[rows, 128:256] = dv
            else:
                dkv_ref[rows, 0:128] += dk
                dkv_ref[rows, 128:256] += dv
            if kb == 0:
                dqt_ref[64 * h:64 * h + 64, :] = dq
            else:
                dqt_ref[64 * h:64 * h + 64, lo:] += dq
    g_ref[:, 0:128] = (dqt_ref[...] * scale).T.astype(BF)
    g_ref[:, 128:384] = dkv_ref[...].astype(BF)
    pay_ref[0:width, 0:384] = tn(x_ref[...], g_ref[...]).astype(BF)
    pay_ref[0:width, 384:512] = tn(gb_ref[...], att_ref[...]).astype(BF)
    pay_ref[width:, :] = jnp.zeros((EXTRA, 512), BF)


def attn_bwd(x, q, k, v, att, do, gb, lse, seg, keep, scale):
    seq, width = x.shape
    return pl.pallas_call(
        functools.partial(attn_bwd_kernel, scale),
        out_shape=[jax.ShapeDtypeStruct((seq, 3 * PAIR), BF), jax.ShapeDtypeStruct((width + EXTRA, 4 * PAIR), BF)],
        scratch_shapes=[pltpu.VMEM((seq, seq), F32), pltpu.VMEM((PAIR, seq), F32), pltpu.VMEM((seq, 2 * PAIR), F32)],
        compiler_params=params(32),
        cost_estimate=cost(7),
        name="attn_bwd",
    )(x, q, k, v, att, do, gb, lse, seg, keep)


def gelu_parts(h):
    e = jnp.exp2(h * h * (-0.5 * LOG2E))
    t = pl.reciprocal(1.0 + (0.3275911 / math.sqrt(2.0)) * jnp.abs(h), approx=False)
    poly = ((((0.5 * 1.061405429) * t - 0.5 * 1.453152027) * t + 0.5 * 1.421413741) * t - 0.5 * 0.284496736) * t + 0.5 * 0.254829592
    tail = poly * t * e
    phi = jnp.where(h >= 0, 1.0 - tail, tail)
    return h * phi, phi + h * e * (1.0 / math.sqrt(2.0 * math.pi))


def mean_of(v):
    return jnp.sum(v, axis=-1, keepdims=True) * (1.0 / v.shape[-1])


def normed(z):
    c = z - mean_of(z)
    rstd = lax.rsqrt(mean_of(c * c) + 1e-5)
    return c * rstd, rstd


def norm_back(w, zhat, rstd):
    return rstd * (w - mean_of(w) - zhat * mean_of(w * zhat))


def row_specs(blk):
    row = lambda w: pl.BlockSpec((blk, w), lambda p: (p, 0))
    full = lambda shape: pl.BlockSpec(shape, lambda p: (0,) * len(shape))
    return row, full


def first_kernel(pairs, pieces, x_ref, *refs):
    att, refs = refs[:pairs], refs[pairs:]
    wo, refs = refs[:pairs], refs[pairs:]
    ffw, refs = refs[:pieces], refs[pieces:]
    g1_ref, b1_ref, mixed_ref, low_ref, act_ref, der_ref, ffn_ref = refs
    branch = nn(jnp.concatenate([a[...] for a in att], axis=1), jnp.concatenate([w[...] for w in wo], axis=0))
    mixed = x_ref[...].astype(F32) + branch
    mixed_ref[...] = mixed
    zhat, _ = normed(mixed)
    low = (zhat * g1_ref[...] + b1_ref[...]).astype(BF)
    low_ref[...] = low
    at = 0
    for w in ffw:
        n = w.shape[1]
        val, der = gelu_parts(nt(low, w[0]))
        act_ref[:, at:at + n] = val.astype(BF)
        der_ref[:, at:at + n] = der.astype(BF)
        at += n
    ffn_ref[...] = nn(act_ref[...], jnp.concatenate([w[1] for w in ffw], axis=0))


def first_part(x, att, wo, ffw, g1, b1, blk=256):
    seq, width = x.shape
    ff = sum(w.shape[1] for w in ffw)
    row, full = row_specs(blk)
    sd = lambda w, t: jax.ShapeDtypeStruct((seq, w), t)
    return pl.pallas_call(
        functools.partial(first_kernel, len(att), len(ffw)),
        grid=(seq // blk,),
        in_specs=[row(width)] + [row(a.shape[1]) for a in att] + [full(w.shape) for w in wo] + [full(w.shape) for w in ffw] + [full((1, width))] * 2,
        out_specs=[row(width), row(width), row(ff), row(ff), row(width)],
        out_shape=[sd(width, F32), sd(width, BF), sd(ff, BF), sd(ff, BF), sd(width, F32)],
        compiler_params=params(40),
        cost_estimate=cost(8),
        name="first_part",
    )(x, *att, *wo, *ffw, g1, b1)


def second_kernel(pairs, pa, pb, x_ref, y_ref, gs_ref, gd_ref, mixed_ref, low_ref, ffn_ref, der_a_ref, *refs):
    wo, refs = refs[:pairs], refs[pairs:]
    ffa, refs = refs[:pa], refs[pa:]
    ffb, refs = refs[:pb], refs[pb:]
    (g1_ref, b1_ref, g2_ref, b2_ref, ns_ref, nd_ref, act_ref, dh_ref, gf_ref, gm_ref, gb_ref, *rest) = refs
    do, (vec_ref, der_ref) = rest[:pairs], rest[pairs:]
    @pl.when(pl.program_id(0) == 0)
    def _():
        vec_ref[...] = jnp.zeros_like(vec_ref)
    mixed = mixed_ref[...]
    zhat1, rstd1 = normed(mixed)
    first = zhat1 * g1_ref[...] + b1_ref[...]
    low = low_ref[...]
    at = 0
    for w in ffb:
        n = w.shape[1]
        val, der = gelu_parts(nt(low, w[0]))
        act_ref[:, at:at + n] = val.astype(BF)
        der_ref[:, at:at + n] = der.astype(BF)
        at += n
    ffn = ffn_ref[...] + nn(act_ref[...], jnp.concatenate([w[1] for w in ffb], axis=0))
    zhat2, rstd2 = normed(first + ffn)
    ns_ref[...] = (zhat2 * g2_ref[...] + b2_ref[...]).astype(BF)
    nd_ref[...] = (y_ref[...].astype(F32) + (mixed - x_ref[...].astype(F32)) + ffn).astype(BF)
    u = gs_ref[...].astype(F32)
    second = norm_back(u * g2_ref[...], zhat2, rstd2)
    gd = gd_ref[...].astype(F32)
    gf = (second + gd).astype(BF)
    gf_ref[...] = gf
    at = 0
    for side, der, base in ((ffa, der_a_ref, 0), (ffb, der_ref, der_a_ref.shape[1])):
        for w in side:
            n = w.shape[1]
            dh_ref[:, at:at + n] = (nt(gf, w[1]) * der[:, at - base:at - base + n].astype(F32)).astype(BF)
            at += n
    gfirst = second + nn(dh_ref[...], jnp.concatenate([w[0] for w in ffa + ffb], axis=0))
    gm = norm_back(gfirst * g1_ref[...], zhat1, rstd1)
    gm_ref[...] = gm
    gb = (gm + gd).astype(BF)
    gb_ref[...] = gb
    dout = nt(gb, jnp.concatenate([w[...] for w in wo], axis=0)).astype(BF)
    for i, ref in enumerate(do):
        ref[...] = dout[:, i * PAIR:(i + 1) * PAIR]
    fold = lambda v: jnp.sum(v, axis=0, keepdims=True)
    vec_ref[...] += jnp.concatenate([fold(gfirst * zhat1), fold(gfirst), fold(u * zhat2), fold(u), jnp.zeros((4, u.shape[1]), F32)], axis=0)


def second_part(x, y, gs, gd, mixed, low, ffn, der, wo, ffa, ffb, g1, b1, g2, b2, blk=256):
    seq, width = x.shape
    fa, fb = sum(w.shape[1] for w in ffa), sum(w.shape[1] for w in ffb)
    row, full = row_specs(blk)
    sd = lambda w, t: jax.ShapeDtypeStruct((seq, w), t)
    return pl.pallas_call(
        functools.partial(second_kernel, len(wo), len(ffa), len(ffb)),
        grid=(seq // blk,),
        in_specs=[row(width)] * 7 + [row(fa)] + [full(w.shape) for w in (*wo, *ffa, *ffb)] + [full((1, width))] * 4,
        out_specs=[row(width), row(width), row(fb), row(fa + fb), row(width), row(width), row(width)] + [row(PAIR)] * len(wo) + [full((8, width))],
        out_shape=[sd(width, BF), sd(width, BF), sd(fb, BF), sd(fa + fb, BF), sd(width, BF), sd(width, F32), sd(width, BF)] + [sd(PAIR, BF)] * len(wo) + [jax.ShapeDtypeStruct((8, width), F32)],
        scratch_shapes=[pltpu.VMEM((blk, fb), BF)],
        compiler_params=params(48),
        cost_estimate=cost(18),
        name="second_part",
    )(x, y, gs, gd, mixed, low, ffn, der, *wo, *ffa, *ffb, g1, b1, g2, b2)


def wgrad_kernel(act_a_ref, act_b_ref, dh_ref, gf_ref, low_ref, out_ref):
    out_ref[0] = tn(dh_ref[...], low_ref[...]).astype(BF)
    @pl.when(pl.program_id(0) == 0)
    def _():
        out_ref[1] = tn(act_a_ref[...], gf_ref[...]).astype(BF)
    @pl.when(pl.program_id(0) == 1)
    def _():
        out_ref[1] = tn(act_b_ref[...], gf_ref[...]).astype(BF)


def wgrad(act_a, act_b, dh, gf, low, which):
    seq, width = gf.shape
    b = act_a.shape[1] // 2
    full = lambda shape: pl.BlockSpec(shape, lambda p: (0,) * len(shape))
    half = pl.BlockSpec((seq, b), lambda p: (0, which))
    return pl.pallas_call(
        wgrad_kernel,
        grid=(2,),
        in_specs=[half, half, pl.BlockSpec((seq, b), lambda p: (0, 2 * p + which)), full((seq, width)), full((seq, width))],
        out_specs=pl.BlockSpec((None, 2, b, width), lambda p: (p, 0, 0, 0)),
        out_shape=jax.ShapeDtypeStruct((2, 2, b, width), BF),
        compiler_params=params(32),
        cost_estimate=cost(6),
        name="wgrad",
    )(act_a, act_b, dh, gf, low)


def sgrad_kernel(pairs, gm_ref, *refs):
    g, refs = refs[:pairs], refs[pairs:]
    w, (out_ref,) = refs[:pairs], refs[pairs:]
    left = jnp.concatenate([a[...] for a in g], axis=1)
    right = jnp.concatenate([a[i] for a in w for i in range(3)], axis=1)
    out_ref[...] = gm_ref[...] + nt(left, right)


def sgrad(gm, g, w, blk=256):
    seq, width = gm.shape
    row, full = row_specs(blk)
    return pl.pallas_call(
        functools.partial(sgrad_kernel, len(g)),
        grid=(seq // blk,),
        in_specs=[row(width)] + [row(3 * PAIR)] * len(g) + [full(a.shape) for a in w],
        out_specs=row(width),
        out_shape=jax.ShapeDtypeStruct((seq, width), F32),
        compiler_params=params(32),
        cost_estimate=cost(4),
        name="sgrad",
    )(gm, *g, *w)


def after(value, *earlier):
    return lax.optimization_barrier((value, earlier))[0]


def body(
    dp_size,
    head_size,
    stream_x,
    stream_y,
    segments,
    keep_mask,
    query_weight,
    key_weight,
    value_weight,
    output_weight,
    first_gain,
    first_shift,
    up_weight,
    down_weight,
    second_gain,
    second_shift,
    grad_stream,
    grad_dual,
):
    seq, width = stream_x.shape
    cols = query_weight.shape[1]
    scale = 1.0 / math.sqrt(width // HEADS)
    total = dp_size * head_size
    core_step = head_size
    head_steps = [1 << b for b in range(head_size.bit_length() - 1)]
    chip_steps = [core_step << b for b in range(1, dp_size.bit_length() - 1)]
    fast = cols == 2 * PAIR and head_size == 2

    def swap(value, even_step, odd_step=None):
        odd_step = even_step if odd_step is None else odd_step
        pairs = [
            (i, i ^ (odd_step if i // core_step % 2 else even_step)) for i in range(total)
        ]
        return lax.ppermute(value, ("dp", "head"), pairs)

    def pick(bit, first, second):
        return jnp.where(bit == 0, first, second)

    index = lax.axis_index("dp") * head_size + lax.axis_index("head")
    core = index // core_step % 2
    row = lambda vec: vec.reshape(1, width)
    g1, b1, g2, b2 = row(first_gain), row(first_shift), row(second_gain), row(second_shift)

    even = [chip_steps[-1]] + chip_steps[:-1] + head_steps
    odd = [chip_steps[-1]] + chip_steps[1:-1] + head_steps + chip_steps[:1]
    steps = list(zip(even, odd))

    seg = lax.dynamic_slice_in_dim(segments, lax.axis_index("head") * seq, seq).reshape(1, seq)
    keep = lax.dynamic_slice_in_dim(keep_mask, lax.axis_index("head") * seq, seq).reshape(1, seq)
    stacked = jnp.stack([query_weight, key_weight, value_weight])
    ffw = jnp.stack([up_weight, down_weight])
    fwd = lambda w: attn_fwd(stream_x, w, seg, keep, scale)

    if fast:
        mine = lax.dynamic_slice_in_dim(stacked, core * PAIR, PAIR, 2)
        other = lax.dynamic_slice_in_dim(stacked, (1 - core) * PAIR, PAIR, 2)
        wo_mine = lax.dynamic_slice_in_dim(output_weight, core * PAIR, PAIR, 0)
        wo_other = lax.dynamic_slice_in_dim(output_weight, (1 - core) * PAIR, PAIR, 0)
        far_mine = swap(mine, head_steps[0])
        far_wo = swap(wo_mine, head_steps[0])
        weights, outs = [mine, other], [wo_mine, wo_other]
        runs = [None] * 4
        got = swap(ffw, *steps[0])
        runs[0] = fwd(mine)
        ffw = jnp.concatenate([ffw, after(got, runs[0])], axis=1)
        got = swap(ffw, *steps[1])
        far_mine, far_wo = after((far_mine, far_wo), runs[0])
        far_other, far_wo_other = swap(far_mine, core_step), swap(far_wo, core_step)
        runs[1] = fwd(after(other, ffw))
        ffw = jnp.concatenate([ffw, after(got, runs[1])], axis=1)
        got = swap(ffw, *steps[2])
        runs[2] = fwd(after(far_mine, ffw))
        ffw = jnp.concatenate([ffw, after(got, runs[2])], axis=1)
        got = swap(ffw, *steps[3])
        part = swap(ffw, core_step)
        runs[3] = fwd(after(far_other, ffw))
        weights += [far_mine, far_other]
        outs += [far_wo, far_wo_other]
        side_a = [ffw, part]
    else:
        for step in head_steps:
            stacked = jnp.concatenate([stacked, swap(stacked, step)], axis=2)
            output_weight = jnp.concatenate([output_weight, swap(output_weight, step)], axis=0)
        weights = [stacked[:, :, i:i + PAIR] for i in range(0, width, PAIR)]
        outs = [output_weight[i:i + PAIR] for i in range(0, width, PAIR)]
        runs = [fwd(w) for w in weights]
        for a, b in steps[:-1]:
            ffw = jnp.concatenate([ffw, swap(ffw, a, b)], axis=1)
        got = swap(ffw, *steps[-1])
        side_a = [ffw, swap(ffw, core_step)]

    mixed, low, act_a, der_a, ffn_a = first_part(stream_x, [r[3] for r in runs], outs, side_a, g1, b1)
    got = after(got, mixed)
    side_b = [got, swap(got, core_step)]
    ns, nd, act_b, dh, gf, gm, gb, *do, vec = second_part(
        stream_x, stream_y, grad_stream, grad_dual, mixed, low, ffn_a, der_a, outs, side_a, side_b, g1, b1, g2, b2
    )

    theirs = wgrad(act_a, act_b, dh, gf, low, 1)
    crossed = swap(theirs, core_step)
    ours = wgrad(act_a, act_b, after(dh, theirs), gf, low, 0)
    crossed, ours = after((crossed, ours))
    sum_b = ours[1] + crossed[1]
    recv = swap(sum_b, *steps[-1])
    sum_a = ours[0] + crossed[0]

    def bwd(i, *earlier):
        q, k, v, att, lse = runs[i]
        return attn_bwd(stream_x, q, k, v, att, after(do[i], *earlier), gb, lse, seg, keep, scale)

    def halve(total, received, step, last=False):
        n = total.shape[1] // 2
        total = total + after(received, total)
        return total[:, :n], total[:, n:]

    low_vec = jnp.concatenate([vec.astype(BF), jnp.zeros((EXTRA - 8, width), BF)], axis=0)
    if fast:
        grads = [None] * 4
        grads[3], pay_far_other = bwd(3, sum_b)
        pay_far_other = pay_far_other.at[width:].set(low_vec)
        from_core = swap(pay_far_other, core_step)
        part = sum_a + after(recv, grads[3])
        n = part.shape[1] // 2
        recv = swap(part[:, n:], *steps[2])
        part = part[:, :n]
        grads[2], pay_far = bwd(2, part, pay_far_other)
        pay_far = pay_far.at[width:].set(low_vec) + from_core
        from_head = swap(pay_far, head_steps[0])
        part = part + after(recv, grads[2])
        n = part.shape[1] // 2
        recv = swap(part[:, n:], *steps[1])
        part = part[:, :n]
        grads[1], pay_other = bwd(1, part, pay_far)
        from_core = swap(pay_other, core_step)
        part = part + after(recv, grads[1])
        n = part.shape[1] // 2
        recv = swap(part[:, n:], *steps[0])
        part = part[:, :n]
        grads[0], pay_mine = bwd(0, part, pay_other)
        part = part.astype(F32) + after(recv, grads[0]).astype(F32)
        tail = jnp.zeros((width + EXTRA, 1), BF)
        whole = pay_mine + from_core + from_head
        whole = jnp.concatenate([whole[:width], pay_far[width:] + from_head[width:]], axis=0)
        chip = index // (2 * core_step)
        s0, s1, s2 = chip_steps
        bit0, bit1 = chip % 2, chip // 2 % 2
        first_bit, second_bit = pick(core, bit0, bit1), pick(core, bit1, bit0)
        n = whole.shape[0] // 2
        sent, kept = pick(first_bit, whole[n:], whole[:n]), pick(first_bit, whole[:n], whole[n:])
        whole = kept + swap(sent, s0, s1)
        n = n // 2
        sent, kept = pick(second_bit, whole[n:], whole[:n]), pick(second_bit, whole[:n], whole[n:])
        whole = kept + swap(sent, s1, s0)
        whole = whole + swap(whole, s2)
        got = swap(whole, s1, s0)
        whole = pick(second_bit, jnp.concatenate([whole, got]), jnp.concatenate([got, whole]))
        got = swap(whole, s0, s1)
        whole = pick(first_bit, jnp.concatenate([whole, got]), jnp.concatenate([got, whole]))
        got = swap(whole, core_step)
        left, right = pick(core, whole, got).astype(F32), pick(core, got, whole).astype(F32)
        both = jnp.stack([left, right], axis=1)[:width].reshape(width, 2, 4, PAIR)
        dw = [both[:, :, j].reshape(width, cols) for j in range(3)]
        out_grad = both[:, :, 3].reshape(width, cols).T
        vec = left[width:width + 4]
    else:
        res = [bwd(i) for i in range(len(runs))]
        grads = [r[0] for r in res]
        pays = jnp.stack([r[1][:width] for r in res])
        pays = pays.reshape(len(runs), width, 4, PAIR).transpose(2, 1, 0, 3).reshape(4, width, width)
        part = sum_a + recv
        for a, b in steps[-2::-1]:
            n = part.shape[1] // 2
            recv = swap(part[:, n:], a, b)
            part = part[:, :n].astype(F32) + recv.astype(F32)
            part = part.astype(BF) if n > up_weight.shape[0] else part
        for step in head_steps[::-1]:
            n = pays.shape[2] // 2
            pays = pays[:, :, :n] + swap(pays[:, :, n:], step)
            low_vec = low_vec + swap(low_vec, step)
        for step in [core_step] + chip_steps:
            pays = pays + swap(pays, step)
            low_vec = low_vec + swap(low_vec, step)
        pays = pays.astype(F32)
        dw, out_grad = [pays[0], pays[1], pays[2]], pays[3].T
        vec = low_vec[:4].astype(F32)

    sg = sgrad(gm, grads, weights)
    return (
        ns, nd, sg, dw[0], dw[1], dw[2], out_grad,
        vec[0], vec[1], part[0], part[1], vec[2], vec[3],
    )


def solution(mesh):
    both = ("dp", "head")
    rows, cols, whole = P(both, None), P(None, "head"), P()
    in_specs = (
        rows, rows, P("dp"), P("dp"), cols, cols, cols, P("head", None),
        whole, whole, rows, rows, whole, whole, rows, rows,
    )
    out_specs = (
        rows, rows, rows, cols, cols, cols, P("head", None),
        whole, whole, rows, rows, whole, whole,
    )
    inner = functools.partial(body, mesh.shape["dp"], mesh.shape["head"])
    return jax.shard_map(inner, mesh=mesh, in_specs=in_specs, out_specs=out_specs, check_vma=False)
```

```python
import functools
import math

import jax
import jax.numpy as jnp
from jax import lax
from jax.experimental import pallas as pl
from jax.experimental.pallas import tpu as pltpu
from jax.sharding import PartitionSpec as P

HEADS = 8
BF = jnp.bfloat16
F32 = jnp.float32
LOG2E = 1.4426950408889634
NEG = -1e30
BLK = 256
MIB = 1 << 20
PAIR = 128
EXTRA = 32
VMEM = 58


def dot(a, b, left, right):
    return lax.dot_general(a, b, (((left,), (right,)), ((), ())), preferred_element_type=F32)


def nn(a, b):
    return dot(a, b, 1, 0)


def nt(a, b):
    return dot(a, b, 1, 1)


def tn(a, b):
    return dot(a, b, 0, 0)


def params(mib):
    return pltpu.CompilerParams(vmem_limit_bytes=mib * MIB)


def cost(us):
    return pl.CostEstimate(flops=int(us * 1e9), bytes_accessed=1 << 20, transcendentals=0)


def fill_mask(seg_ref, keep_ref, mask_ref):
    seq = mask_ref.shape[0]
    seg = seg_ref[...]
    code = jnp.where(keep_ref[...] == 1, seg, -1)
    code_col = jnp.broadcast_to(code.astype(F32), (128, seq)).T
    seg_row = seg.astype(F32)
    for kb in range(seq // BLK):
        rows = slice(kb * BLK, (kb + 1) * BLK)
        width = seq - kb * BLK
        same = jnp.concatenate([code_col[rows]] * (width // 128), axis=1) == seg_row[:, kb * BLK:]
        key = lax.broadcasted_iota(jnp.int32, (BLK, width), 0)
        query = lax.broadcasted_iota(jnp.int32, (BLK, width), 1)
        ok = (same & (key <= query)) | (key == query)
        mask_ref[rows, kb * BLK:] = jnp.where(ok, 0.0, NEG)


def lane_half(arr, h):
    lane = lax.broadcasted_iota(jnp.int32, arr.shape, 1)
    return jnp.where(lane // 64 == h, arr, jnp.zeros_like(arr))


def attn_fwd_kernel(scale, x_ref, w_ref, seg_ref, keep_ref, q_ref, k_ref, v_ref, att_ref, lse_ref, mask_ref, vt_ref, ot_ref):
    seq = x_ref.shape[0]
    fill_mask(seg_ref, keep_ref, mask_ref)
    x = x_ref[...]
    q_ref[...] = nn(x, w_ref[0]).astype(BF)
    k_ref[...] = nn(x, w_ref[1]).astype(BF)
    v = nn(x, w_ref[2]).astype(BF)
    v_ref[...] = v
    vt_ref[...] = v.T

    def one_head(h, carry):
        head = pl.ds(pl.multiple_of(64 * h, 64), 64)
        for qb in range(seq // BLK):
            cols = slice(qb * BLK, (qb + 1) * BLK)
            length = (qb + 1) * BLK
            qm = lane_half(q_ref[cols, :], h)
            s = nt(k_ref[:length, :], qm) * (scale * LOG2E) + mask_ref[:length, cols]
            m = jnp.max(s, axis=0, keepdims=True)
            p = jnp.exp2(s - m)
            l = jnp.sum(p, axis=0, keepdims=True)
            o = nn(vt_ref[head, :length], p.astype(BF))
            ot_ref[head, cols] = o / l
            lse_ref[pl.ds(h, 1), cols] = m + jnp.log2(l)
        return carry

    lax.fori_loop(0, 2, one_head, 0)
    att_ref[...] = ot_ref[...].T.astype(BF)


def attn_fwd(x, w, seg, keep, scale):
    seq = x.shape[0]
    o = jax.ShapeDtypeStruct((seq, PAIR), BF)
    return pl.pallas_call(
        functools.partial(attn_fwd_kernel, scale),
        out_shape=[o, o, o, o, jax.ShapeDtypeStruct((2, seq), F32)],
        scratch_shapes=[pltpu.VMEM((seq, seq), F32), pltpu.VMEM((PAIR, seq), BF), pltpu.VMEM((PAIR, seq), F32)],
        compiler_params=params(16),
        cost_estimate=cost(6),
        name="attn_fwd",
    )(x, w, seg, keep)


def attn_bwd_kernel(scale, x_ref, q_ref, k_ref, v_ref, att_ref, do_ref, gb_ref, lse_ref, seg_ref, keep_ref,
                    g_ref, pay_ref, mask_ref, dqt_ref, dkv_ref, prod_ref, kt_ref):
    seq, width = x_ref.shape
    fill_mask(seg_ref, keep_ref, mask_ref)
    prod_ref[...] = (do_ref[...].astype(F32) * att_ref[...].astype(F32)).T
    kt_ref[...] = k_ref[...].T
    dqt_ref[...] = jnp.zeros_like(dqt_ref)
    dkv_ref[...] = jnp.zeros_like(dkv_ref)

    def one_head(h, carry):
        head = pl.ds(pl.multiple_of(64 * h, 64), 64)
        delta = jnp.sum(prod_ref[head, :], axis=0, keepdims=True)
        lse = lse_ref[pl.ds(h, 1), :]
        for kb in range(seq // BLK):
            rows = slice(kb * BLK, (kb + 1) * BLK)
            lo = kb * BLK
            qm = lane_half(q_ref[lo:, :], h)
            dom = lane_half(do_ref[lo:, :], h)
            s = nt(k_ref[rows, :], qm) * (scale * LOG2E) + mask_ref[rows, lo:]
            p = jnp.exp2(s - lse[:, lo:])
            dp = nt(v_ref[rows, :], dom)
            ds = (p * (dp - delta[:, lo:])).astype(BF)
            dkv_ref[rows, 0:128] += nn(ds, qm) * scale
            dkv_ref[rows, 128:256] += nn(p.astype(BF), dom)
            dqt_ref[head, lo:] += nn(kt_ref[head, rows], ds)
        return carry

    lax.fori_loop(0, 2, one_head, 0)
    g_ref[:, 0:128] = (dqt_ref[...] * scale).T.astype(BF)
    g_ref[:, 128:384] = dkv_ref[...].astype(BF)
    pay_ref[0:width, 0:384] = tn(x_ref[...], g_ref[...]).astype(BF)
    pay_ref[0:width, 384:512] = tn(gb_ref[...], att_ref[...]).astype(BF)
    pay_ref[width:, :] = jnp.zeros((EXTRA, 512), BF)


def attn_bwd(x, q, k, v, att, do, gb, lse, seg, keep, scale):
    seq, width = x.shape
    return pl.pallas_call(
        functools.partial(attn_bwd_kernel, scale),
        out_shape=[jax.ShapeDtypeStruct((seq, 3 * PAIR), BF), jax.ShapeDtypeStruct((width + EXTRA, 4 * PAIR), BF)],
        scratch_shapes=[pltpu.VMEM((seq, seq), F32), pltpu.VMEM((PAIR, seq), F32), pltpu.VMEM((seq, 2 * PAIR), F32), pltpu.VMEM((PAIR, seq), F32), pltpu.VMEM((PAIR, seq), BF)],
        compiler_params=params(16),
        cost_estimate=cost(7),
        name="attn_bwd",
    )(x, q, k, v, att, do, gb, lse, seg, keep)


def gelu_parts(h):
    e = jnp.exp2(h * h * (-0.5 * LOG2E))
    t = pl.reciprocal(1.0 + (0.3275911 / math.sqrt(2.0)) * jnp.abs(h), approx=False)
    poly = ((((0.5 * 1.061405429) * t - 0.5 * 1.453152027) * t + 0.5 * 1.421413741) * t - 0.5 * 0.284496736) * t + 0.5 * 0.254829592
    tail = poly * t * e
    phi = jnp.where(h >= 0, 1.0 - tail, tail)
    return h * phi, phi + h * e * (1.0 / math.sqrt(2.0 * math.pi))


def mean_of(v):
    return jnp.sum(v, axis=-1, keepdims=True) * (1.0 / v.shape[-1])


def normed(z):
    c = z - mean_of(z)
    rstd = lax.rsqrt(mean_of(c * c) + 1e-5)
    return c * rstd, rstd


def norm_back(w, zhat, rstd):
    return rstd * (w - mean_of(w) - zhat * mean_of(w * zhat))


def row_specs(blk):
    row = lambda w: pl.BlockSpec((blk, w), lambda p: (p, 0))
    full = lambda shape: pl.BlockSpec(shape, lambda p: (0,) * len(shape))
    return row, full


def first_kernel(pairs, pieces, x_ref, *refs):
    att, refs = refs[:pairs], refs[pairs:]
    wo, refs = refs[:pairs], refs[pairs:]
    ffw, refs = refs[:pieces], refs[pieces:]
    g1_ref, b1_ref, mixed_ref, low_ref, act_ref, der_ref, ffn_ref = refs
    branch = nn(jnp.concatenate([a[...] for a in att], axis=1), jnp.concatenate([w[...] for w in wo], axis=0))
    mixed = x_ref[...].astype(F32) + branch
    mixed_ref[...] = mixed
    zhat, _ = normed(mixed)
    low = (zhat * g1_ref[...] + b1_ref[...]).astype(BF)
    low_ref[...] = low
    at = 0
    for w in ffw:
        n = w.shape[1]
        val, der = gelu_parts(nt(low, w[0]))
        act_ref[:, at:at + n] = val.astype(BF)
        der_ref[:, at:at + n] = der.astype(BF)
        at += n
    ffn_ref[...] = nn(act_ref[...], jnp.concatenate([w[1] for w in ffw], axis=0))


def first_part(x, att, wo, ffw, g1, b1, blk=256):
    seq, width = x.shape
    ff = sum(w.shape[1] for w in ffw)
    row, full = row_specs(blk)
    sd = lambda w, t: jax.ShapeDtypeStruct((seq, w), t)
    return pl.pallas_call(
        functools.partial(first_kernel, len(att), len(ffw)),
        grid=(seq // blk,),
        in_specs=[row(width)] + [row(a.shape[1]) for a in att] + [full(w.shape) for w in wo] + [full(w.shape) for w in ffw] + [full((1, width))] * 2,
        out_specs=[row(width), row(width), row(ff), row(ff), row(width)],
        out_shape=[sd(width, F32), sd(width, BF), sd(ff, BF), sd(ff, BF), sd(width, F32)],
        compiler_params=params(20),
        cost_estimate=cost(8),
        name="first_part",
    )(x, *att, *wo, *ffw, g1, b1)


def second_kernel(pairs, pa, pb, x_ref, y_ref, gs_ref, gd_ref, mixed_ref, low_ref, ffn_ref, der_a_ref, *refs):
    wo, refs = refs[:pairs], refs[pairs:]
    ffa, refs = refs[:pa], refs[pa:]
    ffb, refs = refs[:pb], refs[pb:]
    (g1_ref, b1_ref, g2_ref, b2_ref, ns_ref, nd_ref, act_ref, dh_ref, gf_ref, gm_ref, gb_ref, *rest) = refs
    do, (vec_ref, der_ref) = rest[:pairs], rest[pairs:]
    @pl.when(pl.program_id(0) == 0)
    def _():
        vec_ref[...] = jnp.zeros_like(vec_ref)
    mixed = mixed_ref[...]
    zhat1, rstd1 = normed(mixed)
    first = zhat1 * g1_ref[...] + b1_ref[...]
    low = low_ref[...]
    at = 0
    for w in ffb:
        n = w.shape[1]
        val, der = gelu_parts(nt(low, w[0]))
        act_ref[:, at:at + n] = val.astype(BF)
        der_ref[:, at:at + n] = der.astype(BF)
        at += n
    ffn = ffn_ref[...] + nn(act_ref[...], jnp.concatenate([w[1] for w in ffb], axis=0))
    zhat2, rstd2 = normed(first + ffn)
    ns_ref[...] = (zhat2 * g2_ref[...] + b2_ref[...]).astype(BF)
    nd_ref[...] = (y_ref[...].astype(F32) + (mixed - x_ref[...].astype(F32)) + ffn).astype(BF)
    u = gs_ref[...].astype(F32)
    second = norm_back(u * g2_ref[...], zhat2, rstd2)
    gd = gd_ref[...].astype(F32)
    gf = (second + gd).astype(BF)
    gf_ref[...] = gf
    at = 0
    for side, der, base in ((ffa, der_a_ref, 0), (ffb, der_ref, der_a_ref.shape[1])):
        for w in side:
            n = w.shape[1]
            dh_ref[:, at:at + n] = (nt(gf, w[1]) * der[:, at - base:at - base + n].astype(F32)).astype(BF)
            at += n
    gfirst = second + nn(dh_ref[...], jnp.concatenate([w[0] for w in ffa + ffb], axis=0))
    gm = norm_back(gfirst * g1_ref[...], zhat1, rstd1)
    gm_ref[...] = gm
    gb = (gm + gd).astype(BF)
    gb_ref[...] = gb
    dout = nt(gb, jnp.concatenate([w[...] for w in wo], axis=0)).astype(BF)
    for i, ref in enumerate(do):
        ref[...] = dout[:, i * PAIR:(i + 1) * PAIR]
    fold = lambda v: jnp.sum(v, axis=0, keepdims=True)
    vec_ref[...] += jnp.concatenate([fold(gfirst * zhat1), fold(gfirst), fold(u * zhat2), fold(u), jnp.zeros((4, u.shape[1]), F32)], axis=0)


def second_part(x, y, gs, gd, mixed, low, ffn, der, wo, ffa, ffb, g1, b1, g2, b2, blk=256):
    seq, width = x.shape
    fa, fb = sum(w.shape[1] for w in ffa), sum(w.shape[1] for w in ffb)
    row, full = row_specs(blk)
    sd = lambda w, t: jax.ShapeDtypeStruct((seq, w), t)
    return pl.pallas_call(
        functools.partial(second_kernel, len(wo), len(ffa), len(ffb)),
        grid=(seq // blk,),
        in_specs=[row(width)] * 7 + [row(fa)] + [full(w.shape) for w in (*wo, *ffa, *ffb)] + [full((1, width))] * 4,
        out_specs=[row(width), row(width), row(fb), row(fa + fb), row(width), row(width), row(width)] + [row(PAIR)] * len(wo) + [full((8, width))],
        out_shape=[sd(width, BF), sd(width, BF), sd(fb, BF), sd(fa + fb, BF), sd(width, BF), sd(width, F32), sd(width, BF)] + [sd(PAIR, BF)] * len(wo) + [jax.ShapeDtypeStruct((8, width), F32)],
        scratch_shapes=[pltpu.VMEM((blk, fb), BF)],
        compiler_params=params(32),
        cost_estimate=cost(18),
        name="second_part",
    )(x, y, gs, gd, mixed, low, ffn, der, *wo, *ffa, *ffb, g1, b1, g2, b2)


def wgrad_kernel(act_a_ref, act_b_ref, dh_ref, gf_ref, low_ref, out_ref):
    out_ref[0] = tn(dh_ref[...], low_ref[...]).astype(BF)
    @pl.when(pl.program_id(0) == 0)
    def _():
        out_ref[1] = tn(act_a_ref[...], gf_ref[...]).astype(BF)
    @pl.when(pl.program_id(0) == 1)
    def _():
        out_ref[1] = tn(act_b_ref[...], gf_ref[...]).astype(BF)


def wgrad(act_a, act_b, dh, gf, low, which):
    seq, width = gf.shape
    b = act_a.shape[1] // 2
    full = lambda shape: pl.BlockSpec(shape, lambda p: (0,) * len(shape))
    half = pl.BlockSpec((seq, b), lambda p: (0, which))
    return pl.pallas_call(
        wgrad_kernel,
        grid=(2,),
        in_specs=[half, half, pl.BlockSpec((seq, b), lambda p: (0, 2 * p + which)), full((seq, width)), full((seq, width))],
        out_specs=pl.BlockSpec((None, 2, b, width), lambda p: (p, 0, 0, 0)),
        out_shape=jax.ShapeDtypeStruct((2, 2, b, width), BF),
        compiler_params=params(20),
        cost_estimate=cost(6),
        name="wgrad",
    )(act_a, act_b, dh, gf, low)


def sgrad_kernel(pairs, gm_ref, *refs):
    g, refs = refs[:pairs], refs[pairs:]
    w, (out_ref,) = refs[:pairs], refs[pairs:]
    left = jnp.concatenate([a[...] for a in g], axis=1)
    right = jnp.concatenate([a[i] for a in w for i in range(3)], axis=1)
    out_ref[...] = gm_ref[...] + nt(left, right)


def sgrad(gm, g, w, blk=256):
    seq, width = gm.shape
    row, full = row_specs(blk)
    return pl.pallas_call(
        functools.partial(sgrad_kernel, len(g)),
        grid=(seq // blk,),
        in_specs=[row(width)] + [row(3 * PAIR)] * len(g) + [full(a.shape) for a in w],
        out_specs=row(width),
        out_shape=jax.ShapeDtypeStruct((seq, width), F32),
        compiler_params=params(14),
        cost_estimate=cost(4),
        name="sgrad",
    )(gm, *g, *w)


def finish_kernel(core_ref, mine_ref, other_ref, dq_ref, dk_ref, dv_ref, og_ref, vec_ref):
    width = dq_ref.shape[0]
    own = core_ref[0] == 0
    mine, other = mine_ref[...].astype(F32), other_ref[...].astype(F32)
    left, right = jnp.where(own, mine, other), jnp.where(own, other, mine)
    for i, ref in enumerate((dq_ref, dk_ref, dv_ref)):
        cols = slice(i * PAIR, (i + 1) * PAIR)
        ref[:, :PAIR] = left[:width, cols]
        ref[:, PAIR:] = right[:width, cols]
    og_ref[:PAIR, :] = left[:width, 3 * PAIR:].T
    og_ref[PAIR:, :] = right[:width, 3 * PAIR:].T
    vec_ref[...] = mine[width:width + 8]


def finish(core, mine, other):
    width = mine.shape[1]
    sd = lambda *shape: jax.ShapeDtypeStruct(shape, F32)
    vmem = pl.BlockSpec(memory_space=pltpu.VMEM)
    return pl.pallas_call(
        finish_kernel,
        in_specs=[pl.BlockSpec(memory_space=pltpu.SMEM), vmem, vmem],
        out_shape=[sd(width, 2 * PAIR)] * 3 + [sd(2 * PAIR, width), sd(8, width)],
        compiler_params=params(14),
        cost_estimate=cost(3),
        name="finish",
    )(core.reshape(1), mine, other)


def after(value, *earlier):
    return lax.optimization_barrier((value, earlier))[0]


def body(
    dp_size,
    head_size,
    stream_x,
    stream_y,
    segments,
    keep_mask,
    query_weight,
    key_weight,
    value_weight,
    output_weight,
    first_gain,
    first_shift,
    up_weight,
    down_weight,
    second_gain,
    second_shift,
    grad_stream,
    grad_dual,
):
    seq, width = stream_x.shape
    cols = query_weight.shape[1]
    scale = 1.0 / math.sqrt(width // HEADS)
    total = dp_size * head_size
    core_step = head_size
    head_steps = [1 << b for b in range(head_size.bit_length() - 1)]
    chip_steps = [core_step << b for b in range(1, dp_size.bit_length() - 1)]
    fast = cols == 2 * PAIR and head_size == 2

    def swap(value, even_step, odd_step=None):
        odd_step = even_step if odd_step is None else odd_step
        pairs = [
            (i, i ^ (odd_step if i // core_step % 2 else even_step)) for i in range(total)
        ]
        return lax.ppermute(value, ("dp", "head"), pairs)

    def pick(bit, first, second):
        return jnp.where(bit == 0, first, second)

    index = lax.axis_index("dp") * head_size + lax.axis_index("head")
    core = index // core_step % 2
    row = lambda vec: vec.reshape(1, width)
    g1, b1, g2, b2 = row(first_gain), row(first_shift), row(second_gain), row(second_shift)

    even = [chip_steps[-1]] + chip_steps[:-1] + head_steps
    odd = [chip_steps[-1]] + chip_steps[1:-1] + head_steps + chip_steps[:1]
    steps = list(zip(even, odd))

    seg = lax.dynamic_slice_in_dim(segments, lax.axis_index("head") * seq, seq).reshape(1, seq)
    keep = lax.dynamic_slice_in_dim(keep_mask, lax.axis_index("head") * seq, seq).reshape(1, seq)
    stacked = jnp.stack([query_weight, key_weight, value_weight])
    ffw = jnp.stack([up_weight, down_weight])
    fwd = lambda w: attn_fwd(stream_x, w, seg, keep, scale)

    if fast:
        mine = lax.dynamic_slice_in_dim(stacked, core * PAIR, PAIR, 2)
        other = lax.dynamic_slice_in_dim(stacked, (1 - core) * PAIR, PAIR, 2)
        wo_mine = lax.dynamic_slice_in_dim(output_weight, core * PAIR, PAIR, 0)
        wo_other = lax.dynamic_slice_in_dim(output_weight, (1 - core) * PAIR, PAIR, 0)
        far_mine = swap(mine, head_steps[0])
        far_wo = swap(wo_mine, head_steps[0])
        weights, outs = [mine, other], [wo_mine, wo_other]
        runs = [None] * 4
        got = swap(ffw, *steps[0])
        runs[0] = fwd(mine)
        ffw = jnp.concatenate([ffw, after(got, runs[0])], axis=1)
        got = swap(ffw, *steps[1])
        far_mine, far_wo = after((far_mine, far_wo), runs[0])
        far_other, far_wo_other = swap(far_mine, core_step), swap(far_wo, core_step)
        runs[1] = fwd(after(other, ffw))
        ffw = jnp.concatenate([ffw, after(got, runs[1])], axis=1)
        got = swap(ffw, *steps[2])
        runs[2] = fwd(after(far_mine, ffw))
        ffw = jnp.concatenate([ffw, after(got, runs[2])], axis=1)
        got = swap(ffw, *steps[3])
        part = swap(ffw, core_step)
        runs[3] = fwd(after(far_other, ffw))
        weights += [far_mine, far_other]
        outs += [far_wo, far_wo_other]
        side_a = [ffw, part]
    else:
        for step in head_steps:
            stacked = jnp.concatenate([stacked, swap(stacked, step)], axis=2)
            output_weight = jnp.concatenate([output_weight, swap(output_weight, step)], axis=0)
        weights = [stacked[:, :, i:i + PAIR] for i in range(0, width, PAIR)]
        outs = [output_weight[i:i + PAIR] for i in range(0, width, PAIR)]
        runs = [fwd(w) for w in weights]
        for a, b in steps[:-1]:
            ffw = jnp.concatenate([ffw, swap(ffw, a, b)], axis=1)
        got = swap(ffw, *steps[-1])
        side_a = [ffw, swap(ffw, core_step)]

    mixed, low, act_a, der_a, ffn_a = first_part(stream_x, [r[3] for r in runs], outs, side_a, g1, b1)
    got = after(got, mixed)
    side_b = [got, swap(got, core_step)]
    ns, nd, act_b, dh, gf, gm, gb, *do, vec = second_part(
        stream_x, stream_y, grad_stream, grad_dual, mixed, low, ffn_a, der_a, outs, side_a, side_b, g1, b1, g2, b2
    )

    theirs = wgrad(act_a, act_b, dh, gf, low, 1)
    crossed = swap(theirs, core_step)
    ours = wgrad(act_a, act_b, after(dh, theirs), gf, low, 0)
    crossed, ours = after((crossed, ours))
    sum_b = ours[1] + crossed[1]
    recv = swap(sum_b, *steps[-1])
    sum_a = ours[0] + crossed[0]

    def bwd(i, *earlier):
        q, k, v, att, lse = runs[i]
        return attn_bwd(stream_x, q, k, v, att, after(do[i], *earlier), gb, lse, seg, keep, scale)

    def halves(own, received):
        n = own.shape[1] // 2
        return own[:, n:] + received[:, n:], own[:, :n] + received[:, :n]

    low_vec = jnp.concatenate([vec.astype(BF), jnp.zeros((EXTRA - 8, width), BF)], axis=0)
    if fast:
        grads = [None] * 4
        grads[3], pay_far_other = bwd(3, sum_b)
        pay_far_other = pay_far_other.at[width:].set(low_vec)
        from_core = swap(pay_far_other, core_step)
        sent, part = halves(sum_a, after(recv, grads[3]))
        recv = swap(sent, *steps[2])
        grads[2], pay_far = bwd(2, sent, part, pay_far_other)
        pay_far = pay_far.at[width:].set(low_vec) + from_core
        from_head = swap(pay_far, head_steps[0])
        sent, part = halves(part, after(recv, grads[2]))
        recv = swap(sent, *steps[1])
        grads[1], pay_other = bwd(1, sent, part, pay_far)
        from_core = swap(pay_other, core_step)
        sent, part = halves(part, after(recv, grads[1]))
        recv = swap(sent, *steps[0])
        grads[0], pay_mine = bwd(0, sent, part, pay_other)
        part = part.astype(F32) + after(recv, grads[0]).astype(F32)
        whole = pay_mine + from_core + from_head
        whole = jnp.concatenate([whole[:width], pay_far[width:] + from_head[width:]], axis=0)
        chip = index // (2 * core_step)
        s0, s1, s2 = chip_steps
        bit0, bit1 = chip % 2, chip // 2 % 2
        first_bit, second_bit = pick(core, bit0, bit1), pick(core, bit1, bit0)
        n = whole.shape[0] // 2
        sent, kept = pick(first_bit, whole[n:], whole[:n]), pick(first_bit, whole[:n], whole[n:])
        whole = kept + swap(sent, s0, s1)
        n = n // 2
        sent, kept = pick(second_bit, whole[n:], whole[:n]), pick(second_bit, whole[:n], whole[n:])
        whole = kept + swap(sent, s1, s0)
        got = swap(whole, s2)
        sg = sgrad(gm, [after(grads[0], whole), *grads[1:]], weights)
        whole = whole + after(got, sg)
        got = swap(whole, s1, s0)
        whole = pick(second_bit, jnp.concatenate([whole, got]), jnp.concatenate([got, whole]))
        got = swap(whole, s0, s1)
        whole = pick(first_bit, jnp.concatenate([whole, got]), jnp.concatenate([got, whole]))
        got = swap(whole, core_step)
        *dw, out_grad, vec = finish(core, whole, got)
    else:
        res = [bwd(i) for i in range(len(runs))]
        grads = [r[0] for r in res]
        pays = jnp.stack([r[1][:width] for r in res])
        pays = pays.reshape(len(runs), width, 4, PAIR).transpose(2, 1, 0, 3).reshape(4, width, width)
        part = sum_a + recv
        for a, b in steps[-2::-1]:
            n = part.shape[1] // 2
            recv = swap(part[:, n:], a, b)
            part = part[:, :n].astype(F32) + recv.astype(F32)
            part = part.astype(BF) if n > up_weight.shape[0] else part
        for step in head_steps[::-1]:
            n = pays.shape[2] // 2
            pays = pays[:, :, :n] + swap(pays[:, :, n:], step)
            low_vec = low_vec + swap(low_vec, step)
        for step in [core_step] + chip_steps:
            pays = pays + swap(pays, step)
            low_vec = low_vec + swap(low_vec, step)
        pays = pays.astype(F32)
        dw, out_grad = [pays[0], pays[1], pays[2]], pays[3].T
        vec = low_vec[:4].astype(F32)
        sg = sgrad(gm, grads, weights)

    return (
        ns, nd, sg, dw[0], dw[1], dw[2], out_grad,
        vec[0], vec[1], part[0], part[1], vec[2], vec[3],
    )


def solution(mesh):
    both = ("dp", "head")
    rows, cols, whole = P(both, None), P(None, "head"), P()
    in_specs = (
        rows, rows, P("dp"), P("dp"), cols, cols, cols, P("head", None),
        whole, whole, rows, rows, whole, whole, rows, rows,
    )
    out_specs = (
        rows, rows, rows, cols, cols, cols, P("head", None),
        whole, whole, rows, rows, whole, whole,
    )
    inner = functools.partial(body, mesh.shape["dp"], mesh.shape["head"])
    return jax.shard_map(inner, mesh=mesh, in_specs=in_specs, out_specs=out_specs, check_vma=False)
```

```python
import functools
import math

import jax
import jax.numpy as jnp
from jax import lax
from jax.experimental import pallas as pl
from jax.experimental.pallas import tpu as pltpu
from jax.sharding import PartitionSpec as P

HEADS = 8
BF = jnp.bfloat16
F32 = jnp.float32
LOG2E = 1.4426950408889634
NEG = -1e30
BLK = 256
MIB = 1 << 20
PAIR = 128
EXTRA = 32
VMEM = 58


def dot(a, b, left, right):
    return lax.dot_general(a, b, (((left,), (right,)), ((), ())), preferred_element_type=F32)


def nn(a, b):
    return dot(a, b, 1, 0)


def nt(a, b):
    return dot(a, b, 1, 1)


def tn(a, b):
    return dot(a, b, 0, 0)


def params(mib):
    return pltpu.CompilerParams(vmem_limit_bytes=mib * MIB)


def cost(us):
    return pl.CostEstimate(flops=int(us * 1e9), bytes_accessed=1 << 20, transcendentals=0)


def mask_kernel(x_ref, seg_ref, keep_ref, mask_ref, xt_ref):
    seq = x_ref.shape[0]
    seg = seg_ref[...]
    code = jnp.where(keep_ref[...] == 1, seg, -1).astype(F32)
    seg = seg.astype(F32)
    line = lambda v: jnp.concatenate([v[i:i + 1] for i in range(v.shape[0])], axis=1)
    seg_row = line(seg)
    code_col = jnp.broadcast_to(line(code), (128, seq)).T
    at = 0
    for kb in range(seq // BLK):
        rows = slice(kb * BLK, (kb + 1) * BLK)
        width = seq - kb * BLK
        same = jnp.concatenate([code_col[rows]] * (width // 128), axis=1) == seg_row[:, kb * BLK:]
        key = lax.broadcasted_iota(jnp.int32, (BLK, BLK), 0)
        query = lax.broadcasted_iota(jnp.int32, (BLK, BLK), 1)
        own = (same[:, :BLK] & (key <= query)) | (key == query)
        mask_ref[:, at:at + BLK] = jnp.where(own, 0.0, NEG)
        if width > BLK:
            mask_ref[:, at + BLK:at + width] = jnp.where(same[:, BLK:], 0.0, NEG)
        at += width
    xt_ref[...] = x_ref[...].T


def make_mask(x, seg, keep):
    seq, width = x.shape
    blocks = seq // BLK
    return pl.pallas_call(
        mask_kernel,
        out_shape=[jax.ShapeDtypeStruct((BLK, BLK * blocks * (blocks + 1) // 2), F32), jax.ShapeDtypeStruct((width, seq), BF)],
        compiler_params=params(10),
        cost_estimate=cost(2),
        name="make_mask",
    )(x, seg, keep)


def offset(kb, seq):
    return sum(seq - i * BLK for i in range(kb))


def attn_fwd_kernel(scale, xt_ref, w_ref, mask_ref, *refs):
    qkv_ref, att_ref, lse_ref = refs[-3:]
    seq = xt_ref.shape[1]
    qkv_ref[...] = nn(w_ref[:3 * PAIR], xt_ref[...]).astype(BF)
    for h in range(2):
        head = lambda i: slice(i * PAIR + 64 * h, i * PAIR + 64 * h + 64)
        keys = qkv_ref[head(1), :].T
        for qb in range(seq // BLK):
            cols = slice(qb * BLK, (qb + 1) * BLK)
            q = qkv_ref[head(0), cols]
            scores = []
            for kb in range(qb + 1):
                at = offset(kb, seq) + (qb - kb) * BLK
                scores.append(nn(keys[kb * BLK:(kb + 1) * BLK], q) * (scale * LOG2E) + mask_ref[:, at:at + BLK])
            m = functools.reduce(jnp.maximum, [jnp.max(s, axis=0, keepdims=True) for s in scores])
            out, l = 0.0, 0.0
            for kb, s in enumerate(scores):
                p = jnp.exp2(s - m)
                l = l + jnp.sum(p, axis=0, keepdims=True)
                out = out + nn(qkv_ref[head(2), kb * BLK:(kb + 1) * BLK], p.astype(BF))
            att_ref[head(0), cols] = (out / l).astype(BF)
            lse_ref[h:h + 1, cols] = m + jnp.log2(l)


def attn_fwd(xt, w, mask, scale, slot, held=()):
    width, seq = xt.shape
    full = lambda shape: pl.BlockSpec(shape, lambda p: (0,) * len(shape))
    own = lambda rows: pl.BlockSpec((None, rows, seq), lambda p: (slot, 0, 0))
    return pl.pallas_call(
        functools.partial(attn_fwd_kernel, scale),
        grid=(1,),
        in_specs=[full((width, seq)), full(w.shape), full(mask.shape)] + [pl.BlockSpec(memory_space=pl.ANY)] * len(held),
        out_specs=[own(3 * PAIR), own(PAIR), own(2)],
        out_shape=[pltpu.HBM((2, 3 * PAIR, seq), BF), jax.ShapeDtypeStruct((2, PAIR, seq), BF), jax.ShapeDtypeStruct((2, 2, seq), F32)],
        input_output_aliases={3 + i: i for i in range(len(held))},
        compiler_params=params(12),
        cost_estimate=cost(5),
        name="attn_fwd",
    )(xt, w, mask, *held)


def attn_bwd_kernel(scale, xt_ref, qkv_ref, att_ref, do_ref, gb_ref, lse_ref, vec_ref, mask_ref, g_ref, other_ref, mine_ref, pay_ref, dq_ref):
    width, seq = xt_ref.shape
    dq_ref[...] = jnp.zeros_like(dq_ref)

    for h in range(2):
        head = lambda i: slice(i * PAIR + 64 * h, i * PAIR + 64 * h + 64)
        own = head(0)
        keys, values = qkv_ref[head(1), :].T, qkv_ref[head(2), :].T
        delta = jnp.sum(do_ref[own, :].astype(F32) * att_ref[own, :].astype(F32), axis=0, keepdims=True)
        lse = lse_ref[h:h + 1, :]
        for kb in range(seq // BLK):
            rows = slice(kb * BLK, (kb + 1) * BLK)
            lo, at = kb * BLK, offset(kb, seq)
            q, dout = qkv_ref[own, lo:], do_ref[own, lo:]
            s = nn(keys[rows], q) * (scale * LOG2E) + mask_ref[:, at:at + seq - lo]
            p = jnp.exp2(s - lse[:, lo:])
            dp = nn(values[rows], dout)
            ds = (p * (dp - delta[:, lo:])).astype(BF)
            g_ref[head(2), rows] = nt(dout, p.astype(BF)).astype(BF)
            g_ref[head(1), rows] = (nt(q, ds) * scale).astype(BF)
            dq_ref[own, lo:] += nn(qkv_ref[head(1), rows], ds)
    g_ref[0:PAIR, :] = (dq_ref[...] * scale).astype(BF)
    pay_ref[0:width, 0:3 * PAIR] = nt(xt_ref[...], g_ref[...]).astype(BF)
    pay_ref[0:width, 3 * PAIR:] = nt(gb_ref[...], att_ref[...]).astype(BF)
    pay_ref[width:, :] = jnp.concatenate([vec_ref[...], jnp.zeros((EXTRA - 8, 4 * PAIR), F32)], axis=0).astype(BF)

    @pl.when(pl.program_id(0) == 0)
    def _():
        other_ref[...] = pay_ref[...]

    @pl.when(pl.program_id(0) == 1)
    def _():
        mine_ref[...] = pay_ref[...]


def attn_bwd(xt, qkv, att, do, gb, lse, vec, mask, scale):
    width, seq = xt.shape
    full = lambda shape: pl.BlockSpec(shape, lambda p: (0,) * len(shape))
    own = lambda rows: pl.BlockSpec((None, rows, seq), lambda p: (p, 0, 0))
    pay = (width + EXTRA, 4 * PAIR)
    return pl.pallas_call(
        functools.partial(attn_bwd_kernel, scale),
        grid=(2,),
        in_specs=[full((width, seq)), own(3 * PAIR), own(PAIR), own(PAIR), full((width, seq)), own(2), full(vec.shape), full(mask.shape)],
        out_specs=[own(3 * PAIR), full(pay), full(pay)],
        out_shape=[pltpu.HBM((2, 3 * PAIR, seq), BF), jax.ShapeDtypeStruct(pay, BF), jax.ShapeDtypeStruct(pay, BF)],
        scratch_shapes=[pltpu.VMEM(pay, BF), pltpu.VMEM((PAIR, seq), F32)],
        compiler_params=params(16),
        cost_estimate=cost(11),
        name="attn_bwd",
    )(xt, qkv, att, do, gb, lse, vec, mask)


def gelu_parts(h):
    phi = 0.5 * lax.erf(h * math.sqrt(0.5)) + 0.5
    slope = jnp.exp2(h * h * (-0.5 * LOG2E)) * (1.0 / math.sqrt(2.0 * math.pi))
    return h * phi, phi + h * slope


def mean_of(v):
    return jnp.sum(v, axis=-1, keepdims=True) * (1.0 / v.shape[-1])


def normed(z):
    c = z - mean_of(z)
    rstd = lax.rsqrt(mean_of(c * c) + 1e-5)
    return c * rstd, rstd


def norm_back(w, zhat, rstd):
    return rstd * (w - mean_of(w) - zhat * mean_of(w * zhat))


def row_specs(blk):
    row = lambda w: pl.BlockSpec((blk, w), lambda p: (p, 0))
    full = lambda shape: pl.BlockSpec(shape, lambda p: (0,) * len(shape))
    return row, full


def column(rows, blk):
    return pl.BlockSpec((2, rows, blk), lambda p: (0, 0, p))


def joined(refs):
    return jnp.concatenate([ref[i] for ref in refs for i in range(2)], axis=0)


def out_spec(width):
    return pl.BlockSpec((PAIR, width), lambda p: (3, 0))


def first_kernel(pairs, pieces, x_ref, *refs):
    att, refs = refs[:pairs // 2], refs[pairs // 2:]
    wo, refs = refs[:pairs], refs[pairs:]
    ffw, refs = refs[:pieces], refs[pieces:]
    g1_ref, b1_ref, mixed_ref, low_ref, act_ref, der_ref, ffn_ref = refs
    branch = nn(joined(att).T, jnp.concatenate([w[...] for w in wo], axis=0))
    mixed = x_ref[...].astype(F32) + branch
    mixed_ref[...] = mixed
    zhat, _ = normed(mixed)
    low = (zhat * g1_ref[...] + b1_ref[...]).astype(BF)
    low_ref[...] = low
    at = 0
    for w in ffw:
        n = w.shape[1]
        val, der = gelu_parts(nt(low, w[0]))
        act_ref[:, at:at + n] = val.astype(BF)
        der_ref[:, at:at + n] = der.astype(BF)
        at += n
    ffn_ref[...] = nn(act_ref[...], jnp.concatenate([w[1] for w in ffw], axis=0))


def first_part(x, att, wo, ffw, g1, b1, blk=256):
    seq, width = x.shape
    ff = sum(w.shape[1] for w in ffw)
    row, full = row_specs(blk)
    sd = lambda w, t: jax.ShapeDtypeStruct((seq, w), t)
    return pl.pallas_call(
        functools.partial(first_kernel, len(wo), len(ffw)),
        grid=(seq // blk,),
        in_specs=[row(width)] + [column(PAIR, blk)] * len(att) + [out_spec(width)] * len(wo) + [full(w.shape) for w in ffw] + [full((1, width))] * 2,
        out_specs=[row(width), row(width), row(ff), row(ff), row(width)],
        out_shape=[sd(width, F32), sd(width, BF), sd(ff, BF), sd(ff, BF), sd(width, F32)],
        compiler_params=params(10),
        cost_estimate=cost(8),
        name="first_part",
    )(x, *att, *wo, *ffw, g1, b1)


def second_kernel(pairs, pa, pb, x_ref, y_ref, gs_ref, gd_ref, mixed_ref, low_ref, ffn_ref, der_a_ref, *refs):
    wo, refs = refs[:pairs], refs[pairs:]
    ffa, refs = refs[:pa], refs[pa:]
    ffb, refs = refs[:pb], refs[pb:]
    (g1_ref, b1_ref, g2_ref, b2_ref, ns_ref, nd_ref, act_ref, dh_ref, gf_ref, gm_ref, gb_ref, *rest) = refs
    do, (vec_ref, der_ref) = rest[:pairs // 2], rest[pairs // 2:]
    @pl.when(pl.program_id(0) == 0)
    def _():
        vec_ref[...] = jnp.zeros_like(vec_ref)
    mixed = mixed_ref[...]
    zhat1, rstd1 = normed(mixed)
    first = zhat1 * g1_ref[...] + b1_ref[...]
    low = low_ref[...]
    at = 0
    for w in ffb:
        n = w.shape[1]
        val, der = gelu_parts(nt(low, w[0]))
        act_ref[:, at:at + n] = val.astype(BF)
        der_ref[:, at:at + n] = der.astype(BF)
        at += n
    ffn = ffn_ref[...] + nn(act_ref[...], jnp.concatenate([w[1] for w in ffb], axis=0))
    zhat2, rstd2 = normed(first + ffn)
    ns_ref[...] = (zhat2 * g2_ref[...] + b2_ref[...]).astype(BF)
    nd_ref[...] = (y_ref[...].astype(F32) + (mixed - x_ref[...].astype(F32)) + ffn).astype(BF)
    u = gs_ref[...].astype(F32)
    second = norm_back(u * g2_ref[...], zhat2, rstd2)
    gd = gd_ref[...].astype(F32)
    gf = (second + gd).astype(BF)
    gf_ref[...] = gf
    at = 0
    for side, der, base in ((ffa, der_a_ref, 0), (ffb, der_ref, der_a_ref.shape[1])):
        for w in side:
            n = w.shape[1]
            dh_ref[:, at:at + n] = (nt(gf, w[1]) * der[:, at - base:at - base + n].astype(F32)).astype(BF)
            at += n
    gfirst = second + nn(dh_ref[...], jnp.concatenate([w[0] for w in ffa + ffb], axis=0))
    gm = norm_back(gfirst * g1_ref[...], zhat1, rstd1)
    gm_ref[...] = gm
    gb = (gm + gd).astype(BF)
    gb_ref[...] = gb.T
    dout = nt(gb, jnp.concatenate([w[...] for w in wo], axis=0)).astype(BF).T
    for i in range(pairs):
        do[i // 2][i % 2] = dout[i * PAIR:(i + 1) * PAIR]
    fold = lambda v: jnp.sum(v, axis=0, keepdims=True)
    vec_ref[...] += jnp.concatenate([fold(gfirst * zhat1), fold(gfirst), fold(u * zhat2), fold(u), jnp.zeros((4, u.shape[1]), F32)], axis=0)


def second_part(x, y, gs, gd, mixed, low, ffn, der, wo, ffa, ffb, g1, b1, g2, b2, blk=256):
    seq, width = x.shape
    fa, fb = sum(w.shape[1] for w in ffa), sum(w.shape[1] for w in ffb)
    row, full = row_specs(blk)
    sd = lambda w, t: jax.ShapeDtypeStruct((seq, w), t)
    return pl.pallas_call(
        functools.partial(second_kernel, len(wo), len(ffa), len(ffb)),
        grid=(seq // blk,),
        in_specs=[row(width)] * 7 + [row(fa)] + [out_spec(width)] * len(wo) + [full(w.shape) for w in (*ffa, *ffb)] + [full((1, width))] * 4,
        out_specs=[row(width), row(width), row(fb), row(fa + fb), row(width), row(width), pl.BlockSpec((width, blk), lambda p: (0, p))] + [column(PAIR, blk)] * (len(wo) // 2) + [full((8, width))],
        out_shape=[sd(width, BF), sd(width, BF), sd(fb, BF), sd(fa + fb, BF), sd(width, BF), pltpu.HBM((seq, width), F32), jax.ShapeDtypeStruct((width, seq), BF)] + [jax.ShapeDtypeStruct((2, PAIR, seq), BF)] * (len(wo) // 2) + [jax.ShapeDtypeStruct((8, width), F32)],
        scratch_shapes=[pltpu.VMEM((blk, fb), BF)],
        compiler_params=params(14),
        cost_estimate=cost(18),
        name="second_part",
    )(x, y, gs, gd, mixed, low, ffn, der, *wo, *ffa, *ffb, g1, b1, g2, b2)


def wgrad_kernel(act_a_ref, act_b_ref, dh_ref, gf_ref, low_ref, out_ref):
    out_ref[0] = tn(dh_ref[...], low_ref[...]).astype(BF)
    @pl.when(pl.program_id(0) == 0)
    def _():
        out_ref[1] = tn(act_a_ref[...], gf_ref[...]).astype(BF)
    @pl.when(pl.program_id(0) == 1)
    def _():
        out_ref[1] = tn(act_b_ref[...], gf_ref[...]).astype(BF)


def wgrad(act_a, act_b, dh, gf, low, which):
    seq, width = gf.shape
    b = act_a.shape[1] // 2
    full = lambda shape: pl.BlockSpec(shape, lambda p: (0,) * len(shape))
    half = pl.BlockSpec((seq, b), lambda p: (0, which))
    return pl.pallas_call(
        wgrad_kernel,
        grid=(2,),
        in_specs=[half, half, pl.BlockSpec((seq, b), lambda p: (0, 2 * p + which)), full((seq, width)), full((seq, width))],
        out_specs=pl.BlockSpec((None, 2, b, width), lambda p: (p, 0, 0, 0)),
        out_shape=jax.ShapeDtypeStruct((2, 2, b, width), BF),
        compiler_params=params(10),
        cost_estimate=cost(6),
        name="wgrad",
    )(act_a, act_b, dh, gf, low)


def sgrad_kernel(pairs, gm_ref, *refs):
    g, refs = refs[:pairs // 2], refs[pairs // 2:]
    w, (out_ref,) = refs[:pairs], refs[pairs:]
    left = joined(g).T
    out_ref[...] = gm_ref[...] + nn(left, jnp.concatenate([a[...] for a in w], axis=0))


def sgrad(gm, g, w, blk=256):
    seq, width = gm.shape
    row, full = row_specs(blk)
    return pl.pallas_call(
        functools.partial(sgrad_kernel, len(w)),
        grid=(seq // blk,),
        in_specs=[row(width)] + [column(3 * PAIR, blk)] * len(g) + [full((3 * PAIR, width))] * len(w),
        out_specs=row(width),
        out_shape=jax.ShapeDtypeStruct((seq, width), F32),
        compiler_params=params(8),
        cost_estimate=cost(4),
        name="sgrad",
    )(gm, *g, *w)


def prep_kernel(place_ref, wq_ref, wk_ref, wv_ref, wo_ref, up_ref, down_ref, mine_ref, other_ref, ffw_ref):
    ffw_ref[0] = up_ref[...]
    ffw_ref[1] = down_ref[...]
    for out_ref, which in ((mine_ref, place_ref[0]), (other_ref, 1 - place_ref[0])):
        part = pl.ds(pl.multiple_of(which * PAIR, PAIR), PAIR)
        for i, ref in enumerate((wq_ref, wk_ref, wv_ref)):
            out_ref[i * PAIR:(i + 1) * PAIR, :] = ref[:, part].T
        out_ref[3 * PAIR:, :] = wo_ref[part, :]


def prep(core, wq, wk, wv, wo, up, down):
    width = wq.shape[0]
    sd = lambda *shape: jax.ShapeDtypeStruct(shape, BF)
    here = lambda v: pltpu.with_memory_space_constraint(v, pltpu.HBM)
    vmem = pl.BlockSpec()
    return pl.pallas_call(
        prep_kernel,
        in_specs=[pl.BlockSpec(memory_space=pltpu.SMEM)] + [vmem] * 6,
        out_shape=[sd(4 * PAIR, width), sd(4 * PAIR, width), sd(2, *up.shape)],
        compiler_params=params(8),
        cost_estimate=cost(2),
        name="prep",
    )(core.reshape(1), *map(here, (wq, wk, wv, wo, up, down)))


def finish_kernel(core_ref, mine_ref, other_ref, dq_ref, dk_ref, dv_ref, og_ref, vec_ref):
    width = dq_ref.shape[0]
    own = core_ref[0] == 0
    mine, other = mine_ref[...].astype(F32), other_ref[...].astype(F32)
    left, right = jnp.where(own, mine, other), jnp.where(own, other, mine)
    for i, ref in enumerate((dq_ref, dk_ref, dv_ref)):
        cols = slice(i * PAIR, (i + 1) * PAIR)
        ref[:, :PAIR] = left[:width, cols]
        ref[:, PAIR:] = right[:width, cols]
    og_ref[:PAIR, :] = left[:width, 3 * PAIR:].T
    og_ref[PAIR:, :] = right[:width, 3 * PAIR:].T
    vec_ref[...] = mine[width:width + 8]


def finish(core, mine, other):
    width = mine.shape[1]
    sd = lambda *shape: jax.ShapeDtypeStruct(shape, F32)
    vmem = pl.BlockSpec(memory_space=pltpu.VMEM)
    return pl.pallas_call(
        finish_kernel,
        in_specs=[pl.BlockSpec(memory_space=pltpu.SMEM), vmem, vmem],
        out_shape=[sd(width, 2 * PAIR)] * 3 + [sd(2 * PAIR, width), sd(8, width)],
        compiler_params=params(8),
        cost_estimate=cost(3),
        name="finish",
    )(core.reshape(1), mine, other)


def after(value, *earlier):
    return lax.optimization_barrier((value, earlier))[0]


def body(
    dp_size,
    head_size,
    stream_x,
    stream_y,
    segments,
    keep_mask,
    query_weight,
    key_weight,
    value_weight,
    output_weight,
    first_gain,
    first_shift,
    up_weight,
    down_weight,
    second_gain,
    second_shift,
    grad_stream,
    grad_dual,
):
    seq, width = stream_x.shape
    cols = query_weight.shape[1]
    scale = 1.0 / math.sqrt(width // HEADS)
    total = dp_size * head_size
    core_step = head_size
    head_steps = [1 << b for b in range(head_size.bit_length() - 1)]
    chip_steps = [core_step << b for b in range(1, dp_size.bit_length() - 1)]
    fast = cols == 2 * PAIR and head_size == 2

    def swap(value, even_step, odd_step=None):
        odd_step = even_step if odd_step is None else odd_step
        pairs = [
            (i, i ^ (odd_step if i // core_step % 2 else even_step)) for i in range(total)
        ]
        return lax.ppermute(value, ("dp", "head"), pairs)

    def pick(low, first, second):
        return jnp.where(low, first, second)

    index = lax.axis_index("dp") * head_size + lax.axis_index("head")
    bit_of = lambda step: (index >> (step.bit_length() - 1)) & 1
    core = bit_of(core_step)
    row = lambda vec: vec.reshape(1, width)
    g1, b1, g2, b2 = row(first_gain), row(first_shift), row(second_gain), row(second_shift)

    even = [chip_steps[-1]] + chip_steps[:-1] + head_steps
    odd = [chip_steps[-1]] + chip_steps[1:-1] + head_steps + chip_steps[:1]
    steps = list(zip(even, odd))

    tokens = lambda v: lax.dynamic_slice_in_dim(v.reshape(-1, 128), lax.axis_index("head") * (seq // 128), seq // 128)
    mask, xt = make_mask(stream_x, tokens(segments), tokens(keep_mask))
    fwd = functools.partial(attn_fwd, xt, mask=mask, scale=scale)

    if fast:
        s0, s1, s2 = chip_steps
        bit0, bit1 = bit_of(s0), bit_of(s1)
        core, first_low, second_low = lax.optimization_barrier((core, pick(core == 0, bit0, bit1) == 0, pick(core == 0, bit1, bit0) == 0))
        mine, other, ffw = prep(core, query_weight, key_weight, value_weight, output_weight, up_weight, down_weight)
        far_mine = swap(mine, head_steps[0])
        got = swap(ffw, *steps[0])
        near = fwd(mine, slot=1)
        ffw = jnp.concatenate([ffw, after(got, near[1])], axis=1)
        got = swap(ffw, *steps[1])
        near = fwd(after(other, ffw), slot=0, held=near)
        ffw = jnp.concatenate([ffw, after(got, near[1])], axis=1)
        got = swap(ffw, *steps[2])
        far_mine = after(far_mine, near[1])
        far_other = swap(far_mine, core_step)
        far = fwd(after(far_mine, ffw), slot=1)
        ffw = jnp.concatenate([ffw, after(got, far[1])], axis=1)
        got = swap(ffw, *steps[3])
        part = swap(ffw, core_step)
        far = fwd(after(far_other, ffw), slot=0, held=far)
        weights = [other, mine, far_other, far_mine]
        side_a = [ffw, part]
    else:
        ffw = jnp.stack([up_weight, down_weight])
        stacked = jnp.stack([query_weight.T, key_weight.T, value_weight.T, output_weight])
        for step in head_steps:
            stacked = jnp.concatenate([stacked, swap(stacked, step)], axis=1)
        weights = [stacked[:, i:i + PAIR].reshape(4 * PAIR, width) for i in range(0, width, PAIR)]
        near = fwd(weights[1], slot=1, held=fwd(weights[0], slot=0))
        far = fwd(weights[3], slot=1, held=fwd(weights[2], slot=0))
        for a, b in steps[:-1]:
            ffw = jnp.concatenate([ffw, swap(ffw, a, b)], axis=1)
        got = swap(ffw, *steps[-1])
        side_a = [ffw, swap(ffw, core_step)]

    mixed, low, act_a, der_a, ffn_a = first_part(stream_x, [near[1], far[1]], weights, side_a, g1, b1)
    got = after(got, mixed)
    side_b = [got, swap(got, core_step)]
    ns, nd, act_b, dh, gf, gm, gb, do_near, do_far, vec = second_part(
        stream_x, stream_y, grad_stream, grad_dual, mixed, low, ffn_a, der_a, weights, side_a, side_b, g1, b1, g2, b2
    )

    ffgrad = lambda which, *earlier: wgrad(act_a, act_b, after(dh, *earlier), gf, low, which)

    def bwd(group, do, *earlier):
        qkv, att, lse = group
        return attn_bwd(xt, qkv, att, after(do, *earlier), gb, lse, vec, mask, scale)

    def halves(own, received):
        n = own.shape[1] // 2
        return own[:, n:] + received[:, n:], own[:, :n] + received[:, :n]

    g_far, pay_far_other, pay_far = bwd(far, do_far)
    if fast:
        crossed_pay = swap(pay_far_other, core_step)
        theirs = ffgrad(1, pay_far)
        crossed = swap(theirs, core_step)
        pay_far = pay_far + after(crossed_pay, theirs)
        from_head = swap(pay_far, head_steps[0])
        g_near, pay_other, pay_mine = bwd(near, do_near, pay_far)
        crossed_pay = swap(pay_other, core_step)
        ours = ffgrad(0, pay_mine)
        whole = pay_mine + after(crossed_pay, ours) + from_head
        whole = jnp.concatenate([whole[:width], pay_far[width:] + from_head[width:]], axis=0)

        def split(low, value):
            n = value.shape[0] // 2
            return pick(low, value[n:], value[:n]), pick(low, value[:n], value[n:])

        def merge(low, own, received):
            return pick(low, jnp.concatenate([own, received]), jnp.concatenate([received, own]))

        sent, kept = split(first_low, whole)
        got = swap(sent, s0, s1)
        crossed, ours = after((crossed, ours), sent)
        part_b = ours[1] + crossed[1]
        recv = swap(part_b, *steps[3])
        part = ours[0] + crossed[0]
        sg = sgrad(gm, [g_near, after(g_far, part_b)], weights)
        sent, kept = split(second_low, kept + after(got, part, sg))
        got = swap(sent, s1, s0)
        whole = kept + got
        got = swap(whole, s2)
        sent, part = halves(part, after(recv, whole))
        recv = swap(sent, *steps[2])
        whole = whole + after(got, sent)
        got = swap(whole, s1, s0)
        sent, part = halves(part, after(recv, whole))
        recv = swap(sent, *steps[1])
        whole = merge(second_low, whole, after(got, sent))
        got = swap(whole, s0, s1)
        sent, part = halves(part, after(recv, whole))
        recv = swap(sent, *steps[0])
        whole = merge(first_low, whole, after(got, sent))
        got = swap(whole, core_step)
        part = part.astype(F32) + recv.astype(F32)
        *dw, out_grad, vec = finish(core, whole, got)
    else:
        g_near, pay_near_other, pay_near = bwd(near, do_near)
        crossed = swap(ffgrad(1), core_step)
        ours = ffgrad(0)
        part = ours[0] + crossed[0] + swap(ours[1] + crossed[1], *steps[-1])
        for a, b in steps[-2::-1]:
            n = part.shape[1] // 2
            recv = swap(part[:, n:], a, b)
            part = part[:, :n].astype(F32) + recv.astype(F32)
            part = part.astype(BF) if n > up_weight.shape[0] else part
        pays = [pay_near_other, pay_near, pay_far_other, pay_far]
        low_vec = pay_near[width:]
        pays = jnp.stack([pay[:width] for pay in pays]).reshape(len(pays), width, 4, PAIR)
        pays = pays.transpose(2, 1, 0, 3).reshape(4, width, width)
        for step in head_steps[::-1]:
            n = pays.shape[2] // 2
            pays = pays[:, :, :n] + swap(pays[:, :, n:], step)
            low_vec = low_vec + swap(low_vec, step)
        for step in [core_step] + chip_steps:
            pays = pays + swap(pays, step)
            low_vec = low_vec + swap(low_vec, step)
        pays = pays.astype(F32)
        dw, out_grad = [pays[0], pays[1], pays[2]], pays[3].T
        vec = low_vec[:4].astype(F32)
        sg = sgrad(gm, [g_near, g_far], weights)

    return (
        ns, nd, sg, dw[0], dw[1], dw[2], out_grad,
        vec[0], vec[1], part[0], part[1], vec[2], vec[3],
    )


def solution(mesh):
    both = ("dp", "head")
    rows, cols, whole = P(both, None), P(None, "head"), P()
    in_specs = (
        rows, rows, P("dp"), P("dp"), cols, cols, cols, P("head", None),
        whole, whole, rows, rows, whole, whole, rows, rows,
    )
    out_specs = (
        rows, rows, rows, cols, cols, cols, P("head", None),
        whole, whole, rows, rows, whole, whole,
    )
    inner = functools.partial(body, mesh.shape["dp"], mesh.shape["head"])
    return jax.shard_map(inner, mesh=mesh, in_specs=in_specs, out_specs=out_specs, check_vma=False)
```

```python
import functools
import math

import jax
import jax.numpy as jnp
from jax import lax
from jax.experimental import pallas as pl
from jax.experimental.pallas import tpu as pltpu
from jax.sharding import PartitionSpec as P

HEADS = 8
BF = jnp.bfloat16
F32 = jnp.float32
LOG2E = 1.4426950408889634
NEG = -1e30
BLK = 256
MIB = 1 << 20
PAIR = 128
EXTRA = 32
VMEM = 58


def dot(a, b, left, right):
    return lax.dot_general(a, b, (((left,), (right,)), ((), ())), preferred_element_type=F32)


def nn(a, b):
    return dot(a, b, 1, 0)


def nt(a, b):
    return dot(a, b, 1, 1)


def tn(a, b):
    return dot(a, b, 0, 0)


def params(mib):
    return pltpu.CompilerParams(vmem_limit_bytes=mib * MIB)


def cost(us):
    return pl.CostEstimate(flops=int(us * 1e9), bytes_accessed=1 << 20, transcendentals=0)


def mask_kernel(x_ref, seg_ref, keep_ref, mask_ref, xt_ref):
    seq = x_ref.shape[0]
    seg = seg_ref[...]
    code = jnp.where(keep_ref[...] == 1, seg, -1).astype(F32)
    seg = seg.astype(F32)
    line = lambda v: jnp.concatenate([v[i:i + 1] for i in range(v.shape[0])], axis=1)
    seg_row = line(seg)
    code_col = jnp.broadcast_to(line(code), (128, seq)).T
    at = 0
    for kb in range(seq // BLK):
        rows = slice(kb * BLK, (kb + 1) * BLK)
        width = seq - kb * BLK
        same = jnp.concatenate([code_col[rows]] * (width // 128), axis=1) == seg_row[:, kb * BLK:]
        key = lax.broadcasted_iota(jnp.int32, (BLK, BLK), 0)
        query = lax.broadcasted_iota(jnp.int32, (BLK, BLK), 1)
        own = (same[:, :BLK] & (key <= query)) | (key == query)
        mask_ref[:, at:at + BLK] = jnp.where(own, 0.0, NEG)
        if width > BLK:
            mask_ref[:, at + BLK:at + width] = jnp.where(same[:, BLK:], 0.0, NEG)
        at += width
    xt_ref[...] = x_ref[...].T


def make_mask(x, seg, keep):
    seq, width = x.shape
    blocks = seq // BLK
    return pl.pallas_call(
        mask_kernel,
        out_shape=[jax.ShapeDtypeStruct((BLK, BLK * blocks * (blocks + 1) // 2), F32), jax.ShapeDtypeStruct((width, seq), BF)],
        compiler_params=params(10),
        cost_estimate=cost(2),
        name="make_mask",
    )(x, seg, keep)


def offset(kb, seq):
    return sum(seq - i * BLK for i in range(kb))


def block_at(kb, qb):
    at = qb * (qb + 1) // 2 + kb
    return slice(at * BLK, (at + 1) * BLK)


def attn_fwd_kernel(scale, slot, xt_ref, w_ref, mask_ref, *refs):
    qkv_ref, att_ref, inv_ref, prob_hbm, prob_ref, sems = refs[-6:]
    seq = xt_ref.shape[1]
    copies = []
    qkv_ref[...] = nn(w_ref[:3 * PAIR], xt_ref[...]).astype(BF)
    for h in range(2):
        head = lambda i: slice(i * PAIR + 64 * h, i * PAIR + 64 * h + 64)
        keys = qkv_ref[head(1), :].T
        for qb in reversed(range(seq // BLK)):
            cols = slice(qb * BLK, (qb + 1) * BLK)
            q = qkv_ref[head(0), cols]
            scores = []
            for kb in range(qb + 1):
                at = offset(kb, seq) + (qb - kb) * BLK
                scores.append(nn(keys[kb * BLK:(kb + 1) * BLK], q) * (scale * LOG2E) + mask_ref[:, at:at + BLK])
            m = functools.reduce(jnp.maximum, [jnp.max(s, axis=0, keepdims=True) for s in scores])
            out, l = 0.0, 0.0
            for kb, s in enumerate(scores):
                p = jnp.exp2(s - m)
                l = l + jnp.sum(p, axis=0, keepdims=True)
                p = p.astype(BF)
                prob_ref[h, :, block_at(kb, qb)] = p
                out = out + nn(qkv_ref[head(2), kb * BLK:(kb + 1) * BLK], p)
            inv = 1.0 / l
            att_ref[head(0), cols] = (out * inv).astype(BF)
            inv_ref[h:h + 1, cols] = inv
            span = slice(block_at(0, qb).start, block_at(qb, qb).stop)
            copies.append(pltpu.make_async_copy(prob_ref.at[h, :, span], prob_hbm.at[slot, h, :, span], sems.at[len(copies)]))
            copies[-1].start()
    for copy in copies:
        copy.wait()


def attn_fwd(xt, w, mask, scale, slot, held=()):
    width, seq = xt.shape
    full = lambda shape: pl.BlockSpec(shape, lambda p: (0,) * len(shape))
    own = lambda rows: pl.BlockSpec((None, rows, seq), lambda p: (slot, 0, 0))
    return pl.pallas_call(
        functools.partial(attn_fwd_kernel, scale, slot),
        grid=(1,),
        in_specs=[full((width, seq)), full(w.shape), full(mask.shape)] + [pl.BlockSpec(memory_space=pl.ANY)] * len(held),
        out_specs=[own(3 * PAIR), own(PAIR), own(2), pl.BlockSpec(memory_space=pl.ANY)],
        out_shape=[jax.ShapeDtypeStruct((2, 3 * PAIR, seq), BF), jax.ShapeDtypeStruct((2, PAIR, seq), BF), jax.ShapeDtypeStruct((2, 2, seq), F32), pltpu.HBM((2, 2, *mask.shape), BF)],
        scratch_shapes=[pltpu.VMEM((2, *mask.shape), BF), pltpu.SemaphoreType.DMA((2 * (seq // BLK),))],
        input_output_aliases={3 + i: i for i in range(len(held))},
        compiler_params=params(16),
        cost_estimate=cost(5),
        name="attn_fwd",
    )(xt, w, mask, *held)


def attn_bwd_kernel(scale, xt_ref, qkv_ref, att_ref, do_ref, gb_ref, inv_ref, vec_ref, prob_ref, g_ref, other_ref, mine_ref, pay_ref, dq_ref):
    width, seq = xt_ref.shape
    dq_ref[...] = jnp.zeros_like(dq_ref)
    for h in range(2):
        head = lambda i: slice(i * PAIR + 64 * h, i * PAIR + 64 * h + 64)
        own = head(0)
        values = qkv_ref[head(2), :].T
        scaled = do_ref[own, :].astype(F32) * inv_ref[h:h + 1, :]
        delta = jnp.sum(scaled * att_ref[own, :].astype(F32), axis=0, keepdims=True)
        scaled = scaled.astype(BF)
        for kb in range(seq // BLK):
            rows = slice(kb * BLK, (kb + 1) * BLK)
            lo = kb * BLK
            q, dout = qkv_ref[own, lo:], scaled[:, lo:]
            p = jnp.concatenate([prob_ref[h, :, block_at(kb, qb)] for qb in range(kb, seq // BLK)], axis=1)
            ds = (p.astype(F32) * (nn(values[rows], dout) - delta[:, lo:])).astype(BF)
            g_ref[head(2), rows] = nt(dout, p).astype(BF)
            g_ref[head(1), rows] = (nt(q, ds) * scale).astype(BF)
            dq_ref[own, lo:] += nn(qkv_ref[head(1), rows], ds)
    g_ref[0:PAIR, :] = (dq_ref[...] * scale).astype(BF)
    pay_ref[0:width, 0:3 * PAIR] = nt(xt_ref[...], g_ref[...]).astype(BF)
    pay_ref[0:width, 3 * PAIR:] = nt(gb_ref[...], att_ref[...]).astype(BF)
    pay_ref[width:, :] = jnp.concatenate([vec_ref[...], jnp.zeros((EXTRA - 8, 4 * PAIR), F32)], axis=0).astype(BF)

    @pl.when(pl.program_id(0) == 0)
    def _():
        other_ref[...] = pay_ref[...]

    @pl.when(pl.program_id(0) == 1)
    def _():
        mine_ref[...] = pay_ref[...]


def attn_bwd(xt, qkv, att, do, gb, inv, vec, prob, scale):
    width, seq = xt.shape
    full = lambda shape: pl.BlockSpec(shape, lambda p: (0,) * len(shape))
    own = lambda rows: pl.BlockSpec((None, rows, seq), lambda p: (p, 0, 0))
    pay = (width + EXTRA, 4 * PAIR)
    return pl.pallas_call(
        functools.partial(attn_bwd_kernel, scale),
        grid=(2,),
        in_specs=[full((width, seq)), own(3 * PAIR), own(PAIR), own(PAIR), full((width, seq)), own(2), full(vec.shape), pl.BlockSpec((None, *prob.shape[1:]), lambda p: (p, 0, 0, 0))],
        out_specs=[own(3 * PAIR), full(pay), full(pay)],
        out_shape=[pltpu.HBM((2, 3 * PAIR, seq), BF), jax.ShapeDtypeStruct(pay, BF), jax.ShapeDtypeStruct(pay, BF)],
        scratch_shapes=[pltpu.VMEM(pay, BF), pltpu.VMEM((PAIR, seq), F32)],
        compiler_params=params(16),
        cost_estimate=cost(11),
        name="attn_bwd",
    )(xt, qkv, att, do, gb, inv, vec, prob)


def gelu_parts(h):
    phi = 0.5 * lax.erf(h * math.sqrt(0.5)) + 0.5
    slope = jnp.exp2(h * h * (-0.5 * LOG2E)) * (1.0 / math.sqrt(2.0 * math.pi))
    return h * phi, phi + h * slope


def mean_of(v):
    return jnp.sum(v, axis=-1, keepdims=True) * (1.0 / v.shape[-1])


def normed(z):
    c = z - mean_of(z)
    rstd = lax.rsqrt(mean_of(c * c) + 1e-5)
    return c * rstd, rstd


def norm_back(w, zhat, rstd):
    return rstd * (w - mean_of(w) - zhat * mean_of(w * zhat))


def row_specs(blk):
    row = lambda w: pl.BlockSpec((blk, w), lambda p: (p, 0))
    full = lambda shape: pl.BlockSpec(shape, lambda p: (0,) * len(shape))
    return row, full


def column(rows, blk):
    return pl.BlockSpec((2, rows, blk), lambda p: (0, 0, p))


def joined(refs):
    return jnp.concatenate([ref[i] for ref in refs for i in range(2)], axis=0)


def out_spec(width):
    return pl.BlockSpec((PAIR, width), lambda p: (3, 0))


def first_kernel(pairs, pieces, x_ref, *refs):
    att, refs = refs[:pairs // 2], refs[pairs // 2:]
    wo, refs = refs[:pairs], refs[pairs:]
    ffw, refs = refs[:pieces], refs[pieces:]
    g1_ref, b1_ref, mixed_ref, low_ref, act_ref, der_ref, ffn_ref = refs
    branch = nn(joined(att).T, jnp.concatenate([w[...] for w in wo], axis=0))
    mixed = x_ref[...].astype(F32) + branch
    mixed_ref[...] = mixed
    zhat, _ = normed(mixed)
    low = (zhat * g1_ref[...] + b1_ref[...]).astype(BF)
    low_ref[...] = low
    at = 0
    for w in ffw:
        n = w.shape[1]
        val, der = gelu_parts(nt(low, w[0]))
        act_ref[:, at:at + n] = val.astype(BF)
        der_ref[:, at:at + n] = der.astype(BF)
        at += n
    ffn_ref[...] = nn(act_ref[...], jnp.concatenate([w[1] for w in ffw], axis=0))


def first_part(x, att, wo, ffw, g1, b1, blk=512):
    seq, width = x.shape
    ff = sum(w.shape[1] for w in ffw)
    row, full = row_specs(blk)
    sd = lambda w, t: jax.ShapeDtypeStruct((seq, w), t)
    return pl.pallas_call(
        functools.partial(first_kernel, len(wo), len(ffw)),
        grid=(seq // blk,),
        in_specs=[row(width)] + [column(PAIR, blk)] * len(att) + [out_spec(width)] * len(wo) + [full(w.shape) for w in ffw] + [full((1, width))] * 2,
        out_specs=[row(width), row(width), row(ff), row(ff), row(width)],
        out_shape=[sd(width, F32), sd(width, BF), sd(ff, BF), sd(ff, BF), sd(width, F32)],
        compiler_params=params(10),
        cost_estimate=cost(8),
        name="first_part",
    )(x, *att, *wo, *ffw, g1, b1)


def second_kernel(pairs, pa, pb, x_ref, y_ref, gs_ref, gd_ref, mixed_ref, low_ref, ffn_ref, der_a_ref, *refs):
    wo, refs = refs[:pairs], refs[pairs:]
    ffa, refs = refs[:pa], refs[pa:]
    ffb, refs = refs[:pb], refs[pb:]
    (g1_ref, b1_ref, g2_ref, b2_ref, ns_ref, nd_ref, act_ref, dh_ref, gf_ref, gm_ref, gb_ref, *rest) = refs
    do, (vec_ref, der_ref) = rest[:pairs // 2], rest[pairs // 2:]
    @pl.when(pl.program_id(0) == 0)
    def _():
        vec_ref[...] = jnp.zeros_like(vec_ref)
    mixed = mixed_ref[...]
    zhat1, rstd1 = normed(mixed)
    first = zhat1 * g1_ref[...] + b1_ref[...]
    low = low_ref[...]
    at = 0
    for w in ffb:
        n = w.shape[1]
        val, der = gelu_parts(nt(low, w[0]))
        act_ref[:, at:at + n] = val.astype(BF)
        der_ref[:, at:at + n] = der.astype(BF)
        at += n
    ffn = ffn_ref[...] + nn(act_ref[...], jnp.concatenate([w[1] for w in ffb], axis=0))
    zhat2, rstd2 = normed(first + ffn)
    ns_ref[...] = (zhat2 * g2_ref[...] + b2_ref[...]).astype(BF)
    nd_ref[...] = (y_ref[...].astype(F32) + (mixed - x_ref[...].astype(F32)) + ffn).astype(BF)
    u = gs_ref[...].astype(F32)
    second = norm_back(u * g2_ref[...], zhat2, rstd2)
    gd = gd_ref[...].astype(F32)
    gf = (second + gd).astype(BF)
    gf_ref[...] = gf
    at = 0
    for side, der, base in ((ffa, der_a_ref, 0), (ffb, der_ref, der_a_ref.shape[1])):
        for w in side:
            n = w.shape[1]
            dh_ref[:, at:at + n] = (nt(gf, w[1]) * der[:, at - base:at - base + n].astype(F32)).astype(BF)
            at += n
    gfirst = second + nn(dh_ref[...], jnp.concatenate([w[0] for w in ffa + ffb], axis=0))
    gm = norm_back(gfirst * g1_ref[...], zhat1, rstd1)
    gm_ref[...] = gm
    gb = (gm + gd).astype(BF)
    gb_ref[...] = gb.T
    dout = nt(gb, jnp.concatenate([w[...] for w in wo], axis=0)).astype(BF).T
    for i in range(pairs):
        do[i // 2][i % 2] = dout[i * PAIR:(i + 1) * PAIR]
    fold = lambda v: jnp.sum(v, axis=0, keepdims=True)
    vec_ref[...] += jnp.concatenate([fold(gfirst * zhat1), fold(gfirst), fold(u * zhat2), fold(u), jnp.zeros((4, u.shape[1]), F32)], axis=0)


def second_part(x, y, gs, gd, mixed, low, ffn, der, wo, ffa, ffb, g1, b1, g2, b2, blk=512):
    seq, width = x.shape
    fa, fb = sum(w.shape[1] for w in ffa), sum(w.shape[1] for w in ffb)
    row, full = row_specs(blk)
    sd = lambda w, t: jax.ShapeDtypeStruct((seq, w), t)
    return pl.pallas_call(
        functools.partial(second_kernel, len(wo), len(ffa), len(ffb)),
        grid=(seq // blk,),
        in_specs=[row(width)] * 7 + [row(fa)] + [out_spec(width)] * len(wo) + [full(w.shape) for w in (*ffa, *ffb)] + [full((1, width))] * 4,
        out_specs=[row(width), row(width), row(fb), row(fa + fb), row(width), row(width), pl.BlockSpec((width, blk), lambda p: (0, p))] + [column(PAIR, blk)] * (len(wo) // 2) + [full((8, width))],
        out_shape=[sd(width, BF), sd(width, BF), sd(fb, BF), sd(fa + fb, BF), sd(width, BF), pltpu.HBM((seq, width), F32), jax.ShapeDtypeStruct((width, seq), BF)] + [jax.ShapeDtypeStruct((2, PAIR, seq), BF)] * (len(wo) // 2) + [jax.ShapeDtypeStruct((8, width), F32)],
        scratch_shapes=[pltpu.VMEM((blk, fb), BF)],
        compiler_params=params(14),
        cost_estimate=cost(18),
        name="second_part",
    )(x, y, gs, gd, mixed, low, ffn, der, *wo, *ffa, *ffb, g1, b1, g2, b2)


def wgrad_kernel(act_a_ref, act_b_ref, dh_ref, gf_ref, low_ref, out_ref):
    out_ref[0] = tn(dh_ref[...], low_ref[...]).astype(BF)
    @pl.when(pl.program_id(0) == 0)
    def _():
        out_ref[1] = tn(act_a_ref[...], gf_ref[...]).astype(BF)
    @pl.when(pl.program_id(0) == 1)
    def _():
        out_ref[1] = tn(act_b_ref[...], gf_ref[...]).astype(BF)


def wgrad(act_a, act_b, dh, gf, low, which):
    seq, width = gf.shape
    b = act_a.shape[1] // 2
    full = lambda shape: pl.BlockSpec(shape, lambda p: (0,) * len(shape))
    half = pl.BlockSpec((seq, b), lambda p: (0, which))
    return pl.pallas_call(
        wgrad_kernel,
        grid=(2,),
        in_specs=[half, half, pl.BlockSpec((seq, b), lambda p: (0, 2 * p + which)), full((seq, width)), full((seq, width))],
        out_specs=pl.BlockSpec((None, 2, b, width), lambda p: (p, 0, 0, 0)),
        out_shape=jax.ShapeDtypeStruct((2, 2, b, width), BF),
        compiler_params=params(10),
        cost_estimate=cost(6),
        name="wgrad",
    )(act_a, act_b, dh, gf, low)


def sgrad_kernel(pairs, gm_ref, *refs):
    g, refs = refs[:pairs // 2], refs[pairs // 2:]
    w, (out_ref,) = refs[:pairs], refs[pairs:]
    left = joined(g).T
    out_ref[...] = gm_ref[...] + nn(left, jnp.concatenate([a[...] for a in w], axis=0))


def sgrad(gm, g, w, blk=256):
    seq, width = gm.shape
    row, full = row_specs(blk)
    return pl.pallas_call(
        functools.partial(sgrad_kernel, len(w)),
        grid=(seq // blk,),
        in_specs=[row(width)] + [column(3 * PAIR, blk)] * len(g) + [full((3 * PAIR, width))] * len(w),
        out_specs=row(width),
        out_shape=jax.ShapeDtypeStruct((seq, width), F32),
        compiler_params=params(8),
        cost_estimate=cost(4),
        name="sgrad",
    )(gm, *g, *w)


def prep_kernel(place_ref, wq_ref, wk_ref, wv_ref, wo_ref, up_ref, down_ref, mine_ref, other_ref, ffw_ref):
    ffw_ref[0] = up_ref[...]
    ffw_ref[1] = down_ref[...]
    for out_ref, which in ((mine_ref, place_ref[0]), (other_ref, 1 - place_ref[0])):
        part = pl.ds(pl.multiple_of(which * PAIR, PAIR), PAIR)
        for i, ref in enumerate((wq_ref, wk_ref, wv_ref)):
            out_ref[i * PAIR:(i + 1) * PAIR, :] = ref[:, part].T
        out_ref[3 * PAIR:, :] = wo_ref[part, :]


def prep(core, wq, wk, wv, wo, up, down):
    width = wq.shape[0]
    sd = lambda *shape: jax.ShapeDtypeStruct(shape, BF)
    here = lambda v: pltpu.with_memory_space_constraint(v, pltpu.HBM)
    vmem = pl.BlockSpec()
    return pl.pallas_call(
        prep_kernel,
        in_specs=[pl.BlockSpec(memory_space=pltpu.SMEM)] + [vmem] * 6,
        out_shape=[sd(4 * PAIR, width), sd(4 * PAIR, width), sd(2, *up.shape)],
        compiler_params=params(8),
        cost_estimate=cost(2),
        name="prep",
    )(core.reshape(1), *map(here, (wq, wk, wv, wo, up, down)))


def finish_kernel(core_ref, mine_ref, other_ref, dq_ref, dk_ref, dv_ref, og_ref, *refs):
    width = dq_ref.shape[0]
    own = core_ref[0] == 0
    mine, other = mine_ref[...].astype(F32), other_ref[...].astype(F32)
    left, right = jnp.where(own, mine, other), jnp.where(own, other, mine)
    for i, ref in enumerate((dq_ref, dk_ref, dv_ref)):
        cols = slice(i * PAIR, (i + 1) * PAIR)
        ref[:, :PAIR] = left[:width, cols]
        ref[:, PAIR:] = right[:width, cols]
    og_ref[:PAIR, :] = left[:width, 3 * PAIR:].T
    og_ref[PAIR:, :] = right[:width, 3 * PAIR:].T
    for i in range(4):
        refs[i][...] = mine[width + i:width + i + 1]


def finish(core, mine, other):
    width = mine.shape[1]
    sd = lambda *shape: jax.ShapeDtypeStruct(shape, F32)
    vmem = pl.BlockSpec(memory_space=pltpu.VMEM)
    *dw, og, v0, v1, v2, v3 = pl.pallas_call(
        finish_kernel,
        in_specs=[pl.BlockSpec(memory_space=pltpu.SMEM)] + [vmem] * 2,
        out_shape=[sd(width, 2 * PAIR)] * 3 + [sd(2 * PAIR, width)] + [sd(1, width)] * 4,
        compiler_params=params(8),
        cost_estimate=cost(3),
        name="finish",
    )(core.reshape(1), mine, other)
    return dw, og, [v.reshape(width) for v in (v0, v1, v2, v3)]


def after(value, *earlier):
    return lax.optimization_barrier((value, earlier))[0]


def body(
    dp_size,
    head_size,
    stream_x,
    stream_y,
    segments,
    keep_mask,
    query_weight,
    key_weight,
    value_weight,
    output_weight,
    first_gain,
    first_shift,
    up_weight,
    down_weight,
    second_gain,
    second_shift,
    grad_stream,
    grad_dual,
):
    seq, width = stream_x.shape
    cols = query_weight.shape[1]
    scale = 1.0 / math.sqrt(width // HEADS)
    total = dp_size * head_size
    core_step = head_size
    head_steps = [1 << b for b in range(head_size.bit_length() - 1)]
    chip_steps = [core_step << b for b in range(1, dp_size.bit_length() - 1)]
    fast = cols == 2 * PAIR and head_size == 2

    def swap(value, even_step, odd_step=None):
        odd_step = even_step if odd_step is None else odd_step
        pairs = [
            (i, i ^ (odd_step if i // core_step % 2 else even_step)) for i in range(total)
        ]
        return lax.ppermute(value, ("dp", "head"), pairs)

    def pick(low, first, second):
        return jnp.where(low, first, second)

    index = lax.axis_index("dp") * head_size + lax.axis_index("head")
    bit_of = lambda step: (index >> (step.bit_length() - 1)) & 1
    core = bit_of(core_step)
    row = lambda vec: vec.reshape(1, width)
    g1, b1, g2, b2 = row(first_gain), row(first_shift), row(second_gain), row(second_shift)

    even = [chip_steps[-1]] + chip_steps[:-1] + head_steps
    odd = [chip_steps[-1]] + chip_steps[1:-1] + head_steps + chip_steps[:1]
    steps = list(zip(even, odd))

    tokens = lambda v: lax.dynamic_slice_in_dim(v.reshape(-1, 128), lax.axis_index("head") * (seq // 128), seq // 128)
    mask, xt = make_mask(stream_x, tokens(segments), tokens(keep_mask))
    fwd = functools.partial(attn_fwd, xt, mask=mask, scale=scale)

    if fast:
        s0, s1, s2 = chip_steps
        bit0, bit1 = bit_of(s0), bit_of(s1)
        core, first_low, second_low = lax.optimization_barrier((core, pick(core == 0, bit0, bit1) == 0, pick(core == 0, bit1, bit0) == 0))
        mine, other, ffw = prep(core, query_weight, key_weight, value_weight, output_weight, up_weight, down_weight)
        far_mine = swap(mine, head_steps[0])
        got = swap(ffw, *steps[0])
        near = fwd(mine, slot=1)
        ffw = jnp.concatenate([ffw, after(got, near[1])], axis=1)
        got = swap(ffw, *steps[1])
        near = fwd(after(other, ffw), slot=0, held=near)
        ffw = jnp.concatenate([ffw, after(got, near[1])], axis=1)
        got = swap(ffw, *steps[2])
        far_mine = after(far_mine, near[1])
        far_other = swap(far_mine, core_step)
        far = fwd(after(far_mine, ffw), slot=1)
        ffw = jnp.concatenate([ffw, after(got, far[1])], axis=1)
        got = swap(ffw, *steps[3])
        part = swap(ffw, core_step)
        far = fwd(after(far_other, ffw), slot=0, held=far)
        weights = [other, mine, far_other, far_mine]
        side_a = [ffw, part]
    else:
        ffw = jnp.stack([up_weight, down_weight])
        stacked = jnp.stack([query_weight.T, key_weight.T, value_weight.T, output_weight])
        for step in head_steps:
            stacked = jnp.concatenate([stacked, swap(stacked, step)], axis=1)
        weights = [stacked[:, i:i + PAIR].reshape(4 * PAIR, width) for i in range(0, width, PAIR)]
        near = fwd(weights[1], slot=1, held=fwd(weights[0], slot=0))
        far = fwd(weights[3], slot=1, held=fwd(weights[2], slot=0))
        for a, b in steps[:-1]:
            ffw = jnp.concatenate([ffw, swap(ffw, a, b)], axis=1)
        got = swap(ffw, *steps[-1])
        side_a = [ffw, swap(ffw, core_step)]

    mixed, low, act_a, der_a, ffn_a = first_part(stream_x, [near[1], far[1]], weights, side_a, g1, b1)
    got = after(got, mixed)
    side_b = [got, swap(got, core_step)]
    ns, nd, act_b, dh, gf, gm, gb, do_near, do_far, vec = second_part(
        stream_x, stream_y, grad_stream, grad_dual, mixed, low, ffn_a, der_a, weights, side_a, side_b, g1, b1, g2, b2
    )

    ffgrad = lambda which, *earlier: wgrad(act_a, act_b, after(dh, *earlier), gf, low, which)

    def bwd(group, do, *earlier):
        qkv, att, inv, prob = group
        return attn_bwd(xt, qkv, att, after(do, *earlier), gb, inv, vec, prob, scale)

    def halves(own, received):
        n = own.shape[1] // 2
        return own[:, n:] + received[:, n:], own[:, :n] + received[:, :n]

    g_far, pay_far_other, pay_far = bwd(far, do_far)
    if fast:
        crossed_pay = swap(pay_far_other, core_step)
        theirs = ffgrad(1, pay_far)
        crossed = swap(theirs, core_step)
        pay_far = pay_far + after(crossed_pay, theirs)
        from_head = swap(pay_far, head_steps[0])
        g_near, pay_other, pay_mine = bwd(near, do_near, pay_far)
        crossed_pay = swap(pay_other, core_step)
        ours = ffgrad(0, pay_mine)
        whole = pay_mine + after(crossed_pay, ours) + from_head
        whole = jnp.concatenate([whole[:width], pay_far[width:] + from_head[width:]], axis=0)

        def split(low, value):
            n = value.shape[0] // 2
            return pick(low, value[n:], value[:n]), pick(low, value[:n], value[n:])

        def merge(low, own, received):
            return pick(low, jnp.concatenate([own, received]), jnp.concatenate([received, own]))

        sent, kept = split(first_low, whole)
        got = swap(sent, s0, s1)
        crossed, ours = after((crossed, ours), sent)
        part_b = ours[1] + crossed[1]
        recv = swap(part_b, *steps[3])
        part = ours[0] + crossed[0]
        sg = sgrad(gm, [g_near, after(g_far, part_b)], weights)
        sent, kept = split(second_low, kept + after(got, part, sg))
        got = swap(sent, s1, s0)
        whole = kept + got
        got = swap(whole, s2)
        sent, part = halves(part, after(recv, whole))
        recv = swap(sent, *steps[2])
        whole = whole + after(got, sent)
        got = swap(whole, s1, s0)
        sent, part = halves(part, after(recv, whole))
        recv = swap(sent, *steps[1])
        whole = merge(second_low, whole, after(got, sent))
        got = swap(whole, s0, s1)
        sent, part = halves(part, after(recv, whole))
        recv = swap(sent, *steps[0])
        whole = merge(first_low, whole, after(got, sent))
        got = swap(whole, core_step)
        part = part.astype(F32) + recv.astype(F32)
        dw, out_grad, vec = finish(core, whole, got)
    else:
        g_near, pay_near_other, pay_near = bwd(near, do_near)
        crossed = swap(ffgrad(1), core_step)
        ours = ffgrad(0)
        part = ours[0] + crossed[0] + swap(ours[1] + crossed[1], *steps[-1])
        for a, b in steps[-2::-1]:
            n = part.shape[1] // 2
            recv = swap(part[:, n:], a, b)
            part = part[:, :n].astype(F32) + recv.astype(F32)
            part = part.astype(BF) if n > up_weight.shape[0] else part
        pays = [pay_near_other, pay_near, pay_far_other, pay_far]
        low_vec = pay_near[width:]
        pays = jnp.stack([pay[:width] for pay in pays]).reshape(len(pays), width, 4, PAIR)
        pays = pays.transpose(2, 1, 0, 3).reshape(4, width, width)
        for step in head_steps[::-1]:
            n = pays.shape[2] // 2
            pays = pays[:, :, :n] + swap(pays[:, :, n:], step)
            low_vec = low_vec + swap(low_vec, step)
        for step in [core_step] + chip_steps:
            pays = pays + swap(pays, step)
            low_vec = low_vec + swap(low_vec, step)
        pays = pays.astype(F32)
        dw, out_grad = [pays[0], pays[1], pays[2]], pays[3].T
        vec = low_vec[:4].astype(F32)
        sg = sgrad(gm, [g_near, g_far], weights)

    return (
        ns, nd, sg, dw[0], dw[1], dw[2], out_grad,
        vec[0], vec[1], part[0], part[1], vec[2], vec[3],
    )


def solution(mesh):
    both = ("dp", "head")
    rows, cols, whole = P(both, None), P(None, "head"), P()
    in_specs = (
        rows, rows, P("dp"), P("dp"), cols, cols, cols, P("head", None),
        whole, whole, rows, rows, whole, whole, rows, rows,
    )
    out_specs = (
        rows, rows, rows, cols, cols, cols, P("head", None),
        whole, whole, rows, rows, whole, whole,
    )
    inner = functools.partial(body, mesh.shape["dp"], mesh.shape["head"])
    return jax.shard_map(inner, mesh=mesh, in_specs=in_specs, out_specs=out_specs, check_vma=False)
```

```python
import functools
import math

import jax
import jax.numpy as jnp
from jax import lax
from jax.experimental import pallas as pl
from jax.experimental.pallas import tpu as pltpu
from jax.sharding import PartitionSpec as P

HEADS = 8
BF = jnp.bfloat16
F32 = jnp.float32
LOG2E = 1.4426950408889634
NEG = -1e30
BLK = 256
MIB = 1 << 20
PAIR = 128
EXTRA = 32
STREAM = 512
LIM1 = 12
LIM2 = 16
VMEM = 58


def dot(a, b, left, right):
    return lax.dot_general(a, b, (((left,), (right,)), ((), ())), preferred_element_type=F32)


def nn(a, b):
    return dot(a, b, 1, 0)


def nt(a, b):
    return dot(a, b, 1, 1)


def tn(a, b):
    return dot(a, b, 0, 0)


def params(mib):
    return pltpu.CompilerParams(vmem_limit_bytes=mib * MIB)


def cost(us):
    return pl.CostEstimate(flops=int(us * 1e9), bytes_accessed=1 << 20, transcendentals=0)


def mask_kernel(x_ref, seg_ref, keep_ref, mask_ref, xt_ref):
    seq = x_ref.shape[0]
    seg = seg_ref[...]
    code = jnp.where(keep_ref[...] == 1, seg, -1).astype(F32)
    seg = seg.astype(F32)
    line = lambda v: jnp.concatenate([v[i:i + 1] for i in range(v.shape[0])], axis=1)
    seg_row = line(seg)
    code_col = jnp.broadcast_to(line(code), (128, seq)).T
    at = 0
    for kb in range(seq // BLK):
        rows = slice(kb * BLK, (kb + 1) * BLK)
        width = seq - kb * BLK
        same = jnp.concatenate([code_col[rows]] * (width // 128), axis=1) == seg_row[:, kb * BLK:]
        key = lax.broadcasted_iota(jnp.int32, (BLK, BLK), 0)
        query = lax.broadcasted_iota(jnp.int32, (BLK, BLK), 1)
        own = (same[:, :BLK] & (key <= query)) | (key == query)
        mask_ref[:, at:at + BLK] = jnp.where(own, 0.0, NEG)
        if width > BLK:
            mask_ref[:, at + BLK:at + width] = jnp.where(same[:, BLK:], 0.0, NEG)
        at += width
    xt_ref[...] = x_ref[...].T


def make_mask(x, seg, keep):
    seq, width = x.shape
    blocks = seq // BLK
    return pl.pallas_call(
        mask_kernel,
        out_shape=[jax.ShapeDtypeStruct((BLK, BLK * blocks * (blocks + 1) // 2), F32), jax.ShapeDtypeStruct((width, seq), BF)],
        compiler_params=params(10),
        cost_estimate=cost(2),
        name="make_mask",
    )(x, seg, keep)


def offset(kb, seq):
    return sum(seq - i * BLK for i in range(kb))


def block_at(kb, qb):
    at = qb * (qb + 1) // 2 + kb
    return slice(at * BLK, (at + 1) * BLK)


def attn_fwd_kernel(scale, slot, xt_ref, w_ref, mask_ref, *refs):
    qkv_ref, att_ref, inv_ref, prob_hbm, prob_ref, sems = refs[-6:]
    seq = xt_ref.shape[1]
    copies = []
    qkv_ref[...] = nn(w_ref[:3 * PAIR], xt_ref[...]).astype(BF)
    for h in range(2):
        head = lambda i: slice(i * PAIR + 64 * h, i * PAIR + 64 * h + 64)
        keys = qkv_ref[head(1), :].T
        for qb in reversed(range(seq // BLK)):
            cols = slice(qb * BLK, (qb + 1) * BLK)
            q = qkv_ref[head(0), cols]
            scores = []
            for kb in range(qb + 1):
                at = offset(kb, seq) + (qb - kb) * BLK
                scores.append(nn(keys[kb * BLK:(kb + 1) * BLK], q) * (scale * LOG2E) + mask_ref[:, at:at + BLK])
            m = functools.reduce(jnp.maximum, [jnp.max(s, axis=0, keepdims=True) for s in scores])
            out, l = 0.0, 0.0
            for kb, s in enumerate(scores):
                p = jnp.exp2(s - m)
                l = l + jnp.sum(p, axis=0, keepdims=True)
                p = p.astype(BF)
                prob_ref[h, :, block_at(kb, qb)] = p
                out = out + nn(qkv_ref[head(2), kb * BLK:(kb + 1) * BLK], p)
            inv = 1.0 / l
            att_ref[head(0), cols] = (out * inv).astype(BF)
            inv_ref[h:h + 1, cols] = inv
            span = slice(block_at(0, qb).start, block_at(qb, qb).stop)
            copies.append(pltpu.make_async_copy(prob_ref.at[h, :, span], prob_hbm.at[slot, h, :, span], sems.at[len(copies)]))
            copies[-1].start()
    for copy in copies:
        copy.wait()


def attn_fwd(xt, w, mask, scale, slot, held=()):
    width, seq = xt.shape
    full = lambda shape: pl.BlockSpec(shape, lambda p: (0,) * len(shape))
    own = lambda rows: pl.BlockSpec((None, rows, seq), lambda p: (slot, 0, 0))
    return pl.pallas_call(
        functools.partial(attn_fwd_kernel, scale, slot),
        grid=(1,),
        in_specs=[full((width, seq)), full(w.shape), full(mask.shape)] + [pl.BlockSpec(memory_space=pl.ANY)] * len(held),
        out_specs=[own(3 * PAIR), own(PAIR), own(2), pl.BlockSpec(memory_space=pl.ANY)],
        out_shape=[jax.ShapeDtypeStruct((2, 3 * PAIR, seq), BF), jax.ShapeDtypeStruct((2, PAIR, seq), BF), jax.ShapeDtypeStruct((2, 2, seq), F32), pltpu.HBM((2, 2, *mask.shape), BF)],
        scratch_shapes=[pltpu.VMEM((2, *mask.shape), BF), pltpu.SemaphoreType.DMA((2 * (seq // BLK),))],
        input_output_aliases={3 + i: i for i in range(len(held))},
        compiler_params=params(12),
        cost_estimate=cost(5),
        name="attn_fwd",
    )(xt, w, mask, *held)


def attn_bwd_kernel(scale, xt_ref, qkv_ref, att_ref, do_ref, gb_ref, inv_ref, vec_ref, prob_ref, g_ref, other_ref, mine_ref, pay_ref, dq_ref):
    width, seq = xt_ref.shape
    dq_ref[...] = jnp.zeros_like(dq_ref)
    for h in range(2):
        head = lambda i: slice(i * PAIR + 64 * h, i * PAIR + 64 * h + 64)
        own = head(0)
        values = qkv_ref[head(2), :].T
        scaled = do_ref[own, :].astype(F32) * inv_ref[h:h + 1, :]
        delta = jnp.sum(scaled * att_ref[own, :].astype(F32), axis=0, keepdims=True)
        scaled = scaled.astype(BF)
        for kb in range(seq // BLK):
            rows = slice(kb * BLK, (kb + 1) * BLK)
            lo = kb * BLK
            q, dout = qkv_ref[own, lo:], scaled[:, lo:]
            p = jnp.concatenate([prob_ref[h, :, block_at(kb, qb)] for qb in range(kb, seq // BLK)], axis=1)
            ds = (p.astype(F32) * (nn(values[rows], dout) - delta[:, lo:])).astype(BF)
            g_ref[head(2), rows] = nt(dout, p).astype(BF)
            g_ref[head(1), rows] = (nt(q, ds) * scale).astype(BF)
            dq_ref[own, lo:] += nn(qkv_ref[head(1), rows], ds)
    g_ref[0:PAIR, :] = (dq_ref[...] * scale).astype(BF)
    pay_ref[0:width, 0:3 * PAIR] = nt(xt_ref[...], g_ref[...]).astype(BF)
    pay_ref[0:width, 3 * PAIR:] = nt(gb_ref[...], att_ref[...]).astype(BF)
    pay_ref[width:, :] = jnp.concatenate([vec_ref[...], jnp.zeros((EXTRA - 8, 4 * PAIR), F32)], axis=0).astype(BF)

    @pl.when(pl.program_id(0) == 0)
    def _():
        other_ref[...] = pay_ref[...]

    @pl.when(pl.program_id(0) == 1)
    def _():
        mine_ref[...] = pay_ref[...]


def attn_bwd(xt, qkv, att, do, gb, inv, vec, prob, scale):
    width, seq = xt.shape
    full = lambda shape: pl.BlockSpec(shape, lambda p: (0,) * len(shape))
    own = lambda rows: pl.BlockSpec((None, rows, seq), lambda p: (p, 0, 0))
    pay = (width + EXTRA, 4 * PAIR)
    return pl.pallas_call(
        functools.partial(attn_bwd_kernel, scale),
        grid=(2,),
        in_specs=[full((width, seq)), own(3 * PAIR), own(PAIR), own(PAIR), full((width, seq)), own(2), full(vec.shape), pl.BlockSpec((None, *prob.shape[1:]), lambda p: (p, 0, 0, 0))],
        out_specs=[own(3 * PAIR), full(pay), full(pay)],
        out_shape=[pltpu.HBM((2, 3 * PAIR, seq), BF), jax.ShapeDtypeStruct(pay, BF), jax.ShapeDtypeStruct(pay, BF)],
        scratch_shapes=[pltpu.VMEM(pay, BF), pltpu.VMEM((PAIR, seq), F32)],
        compiler_params=params(12),
        cost_estimate=cost(11),
        name="attn_bwd",
    )(xt, qkv, att, do, gb, inv, vec, prob)


def gelu_parts(h):
    phi = 0.5 * lax.erf(h * math.sqrt(0.5)) + 0.5
    slope = jnp.exp2(h * h * (-0.5 * LOG2E)) * (1.0 / math.sqrt(2.0 * math.pi))
    return h * phi, phi + h * slope


def mean_of(v):
    return jnp.sum(v, axis=-1, keepdims=True) * (1.0 / v.shape[-1])


def normed(z):
    c = z - mean_of(z)
    rstd = lax.rsqrt(mean_of(c * c) + 1e-5)
    return c * rstd, rstd


def norm_back(w, zhat, rstd):
    return rstd * (w - mean_of(w) - zhat * mean_of(w * zhat))


def row_specs(blk):
    row = lambda w: pl.BlockSpec((blk, w), lambda p: (p, 0))
    full = lambda shape: pl.BlockSpec(shape, lambda p: (0,) * len(shape))
    return row, full


def column(rows, blk):
    return pl.BlockSpec((2, rows, blk), lambda p: (0, 0, p))


def joined(refs):
    return jnp.concatenate([ref[i] for ref in refs for i in range(2)], axis=0)


def out_spec(width):
    return pl.BlockSpec((PAIR, width), lambda p: (3, 0))


def first_kernel(pairs, pieces, x_ref, y_ref, *refs):
    att, refs = refs[:pairs // 2], refs[pairs // 2:]
    wo, refs = refs[:pairs], refs[pairs:]
    ffw, refs = refs[:pieces], refs[pieces:]
    g1_ref, b1_ref, low_ref, act_ref, der_ref, zhat_ref, rstd_ref, sum_ref, dual_ref = refs
    branch = nn(joined(att).T, jnp.concatenate([w[...] for w in wo], axis=0))
    zhat, rstd = normed(x_ref[...].astype(F32) + branch)
    zhat_ref[...] = zhat.astype(BF)
    rstd_ref[...] = jnp.broadcast_to(rstd, rstd_ref.shape)
    first = zhat * g1_ref[...] + b1_ref[...]
    low = first.astype(BF)
    low_ref[...] = low
    acts = []
    at = 0
    for w in ffw:
        n = w.shape[1]
        val, der = gelu_parts(nt(low, w[0]))
        acts.append(val.astype(BF))
        act_ref[:, at:at + n] = acts[-1]
        der_ref[:, at:at + n] = der.astype(BF)
        at += n
    ffn = nn(jnp.concatenate(acts, axis=1), jnp.concatenate([w[1] for w in ffw], axis=0))
    sum_ref[...] = first + ffn
    dual_ref[...] = y_ref[...].astype(F32) + branch + ffn


def first_part(x, y, att, wo, ffw, g1, b1, blk=512):
    seq, width = x.shape
    ff = sum(w.shape[1] for w in ffw)
    row, full = row_specs(blk)
    sd = lambda w, t: jax.ShapeDtypeStruct((seq, w), t)
    return pl.pallas_call(
        functools.partial(first_kernel, len(wo), len(ffw)),
        grid=(seq // blk,),
        in_specs=[row(width)] * 2 + [column(PAIR, blk)] * len(att) + [out_spec(width)] * len(wo) + [full(w.shape) for w in ffw] + [full((1, width))] * 2,
        out_specs=[row(width), row(ff), row(ff), row(width), row(PAIR), row(width), row(width)],
        out_shape=[sd(width, BF), sd(ff, BF), sd(ff, BF), sd(width, BF), sd(PAIR, F32), sd(width, F32), sd(width, F32)],
        compiler_params=params(12),
        cost_estimate=cost(8),
        name="first_part",
    )(x, y, *att, *wo, *ffw, g1, b1)


def second_rows(rows, wo, ffa, ffb, gs_ref, gd_ref, low_ref, der_a_ref, zhat_ref, rstd_ref, sum_ref, dual_ref,
                g1_ref, g2_ref, b2_ref, ns_ref, nd_ref, act_ref, dh_ref, gf_ref, gm_ref, gb_ref, *rest):
    do, vec_ref = rest[:-1], rest[-1]
    low = low_ref[rows, :]
    ders, acts = [], []
    at = 0
    for w in ffa:
        ders.append(der_a_ref[rows, at:at + w.shape[1]])
        at += w.shape[1]
    at = 0
    for w in ffb:
        n = w.shape[1]
        val, der = gelu_parts(nt(low, w[0]))
        acts.append(val.astype(BF))
        ders.append(der.astype(BF))
        act_ref[rows, at:at + n] = acts[-1]
        at += n
        yield True
    ffn = nn(jnp.concatenate(acts, axis=1), jnp.concatenate([w[1] for w in ffb], axis=0))
    yield True
    zhat2, rstd2 = normed(sum_ref[rows, :] + ffn)
    ns_ref[rows, :] = (zhat2 * g2_ref[...] + b2_ref[...]).astype(BF)
    nd_ref[rows, :] = (dual_ref[rows, :] + ffn).astype(BF)
    u = gs_ref[rows, :].astype(F32)
    second = norm_back(u * g2_ref[...], zhat2, rstd2)
    gd = gd_ref[rows, :].astype(F32)
    gf = (second + gd).astype(BF)
    gf_ref[rows, :] = gf
    fold = lambda v: jnp.sum(v, axis=0, keepdims=True)
    vec = [fold(u * zhat2), fold(u)]
    yield True
    dhs = []
    at = 0
    for w, der in zip(ffa + ffb, ders):
        n = w.shape[1]
        dhs.append((nt(gf, w[1]) * der.astype(F32)).astype(BF))
        dh_ref[rows, at:at + n] = dhs[-1]
        at += n
        yield True
    gfirst = second + nn(jnp.concatenate(dhs, axis=1), jnp.concatenate([w[0] for w in ffa + ffb], axis=0))
    yield True
    zhat1 = zhat_ref[rows, :].astype(F32)
    gm = norm_back(gfirst * g1_ref[...], zhat1, rstd_ref[rows, :1])
    gm_ref[rows, :] = gm
    gb = (gm + gd).astype(BF)
    gb_ref[:, rows] = gb.T
    vec_ref[...] += jnp.concatenate([fold(gfirst * zhat1), fold(gfirst), *vec, jnp.zeros((4, u.shape[1]), F32)], axis=0)
    yield True
    dout = nt(gb, wo).astype(BF).T
    for i in range(2 * len(do)):
        do[i // 2][i % 2, :, rows] = dout[i * PAIR:(i + 1) * PAIR]
    yield True


def interleave(streams):
    waiting, running = list(streams), []
    while waiting or running:
        if waiting:
            running.append(waiting.pop(0))
        for stream in running[:]:
            if next(stream, None) is None:
                running.remove(stream)


def second_kernel(pairs, pa, pb, *refs):
    data, refs = refs[:8], refs[8:]
    wo, refs = refs[:pairs], refs[pairs:]
    ffa, refs = refs[:pa], refs[pa:]
    ffb, refs = refs[:pb], refs[pb:]
    vec_ref = refs[-1]

    @pl.when(pl.program_id(0) == 0)
    def _():
        vec_ref[...] = jnp.zeros_like(vec_ref)

    wo = jnp.concatenate([w[...] for w in wo], axis=0)
    rows = data[0].shape[0]
    interleave(second_rows(slice(lo, lo + STREAM), wo, ffa, ffb, *data, *refs) for lo in range(0, rows, STREAM))


def second_part(gs, gd, low, der, zhat, rstd, total, dual, wo, ffa, ffb, g1, g2, b2, blk=512):
    seq, width = gs.shape
    fa, fb = sum(w.shape[1] for w in ffa), sum(w.shape[1] for w in ffb)
    row, full = row_specs(blk)
    sd = lambda w, t: jax.ShapeDtypeStruct((seq, w), t)
    return pl.pallas_call(
        functools.partial(second_kernel, len(wo), len(ffa), len(ffb)),
        grid=(seq // blk,),
        in_specs=[row(width)] * 3 + [row(fa), row(width), row(PAIR), row(width), row(width)] + [out_spec(width)] * len(wo) + [full(w.shape) for w in (*ffa, *ffb)] + [full((1, width))] * 3,
        out_specs=[row(width), row(width), row(fb), row(fa + fb), row(width), row(width), pl.BlockSpec((width, blk), lambda p: (0, p))] + [column(PAIR, blk)] * (len(wo) // 2) + [full((8, width))],
        out_shape=[sd(width, BF), sd(width, BF), sd(fb, BF), sd(fa + fb, BF), sd(width, BF), pltpu.HBM((seq, width), F32), jax.ShapeDtypeStruct((width, seq), BF)] + [jax.ShapeDtypeStruct((2, PAIR, seq), BF)] * (len(wo) // 2) + [jax.ShapeDtypeStruct((8, width), F32)],
        compiler_params=params(12),
        cost_estimate=cost(18),
        name="second_part",
    )(gs, gd, low, der, zhat, rstd, total, dual, *wo, *ffa, *ffb, g1, g2, b2)


def wgrad_kernel(which, act_a_ref, act_b_ref, dh_ref, gf_ref, low_ref, out_ref):
    piece = act_a_ref.shape[1] // 2
    for side, act_ref in enumerate((act_a_ref, act_b_ref)):
        at = (2 * side + which) * piece
        out_ref[side, 0] = tn(dh_ref[:, at:at + piece], low_ref[...]).astype(BF)
        out_ref[side, 1] = tn(act_ref[:, which * piece:(which + 1) * piece], gf_ref[...]).astype(BF)


def wgrad(act_a, act_b, dh, gf, low, which):
    width = gf.shape[1]
    return pl.pallas_call(
        functools.partial(wgrad_kernel, which),
        out_shape=jax.ShapeDtypeStruct((2, 2, act_a.shape[1] // 2, width), BF),
        compiler_params=params(12),
        cost_estimate=cost(6),
        name="wgrad",
    )(act_a, act_b, dh, gf, low)


def sgrad_kernel(pairs, gm_ref, *refs):
    g, refs = refs[:pairs // 2], refs[pairs // 2:]
    w, (out_ref,) = refs[:pairs], refs[pairs:]
    left = joined(g).T
    out_ref[...] = gm_ref[...] + nn(left, jnp.concatenate([a[...] for a in w], axis=0))


def sgrad(gm, g, w, blk=256):
    seq, width = gm.shape
    row, full = row_specs(blk)
    return pl.pallas_call(
        functools.partial(sgrad_kernel, len(w)),
        grid=(seq // blk,),
        in_specs=[row(width)] + [column(3 * PAIR, blk)] * len(g) + [full((3 * PAIR, width))] * len(w),
        out_specs=row(width),
        out_shape=jax.ShapeDtypeStruct((seq, width), F32),
        compiler_params=params(8),
        cost_estimate=cost(4),
        name="sgrad",
    )(gm, *g, *w)


def prep_kernel(place_ref, wq_ref, wk_ref, wv_ref, wo_ref, up_ref, down_ref, mine_ref, other_ref, ffw_ref):
    ffw_ref[0] = up_ref[...]
    ffw_ref[1] = down_ref[...]
    for out_ref, which in ((mine_ref, place_ref[0]), (other_ref, 1 - place_ref[0])):
        part = pl.ds(pl.multiple_of(which * PAIR, PAIR), PAIR)
        for i, ref in enumerate((wq_ref, wk_ref, wv_ref)):
            out_ref[i * PAIR:(i + 1) * PAIR, :] = ref[:, part].T
        out_ref[3 * PAIR:, :] = wo_ref[part, :]


def prep(core, wq, wk, wv, wo, up, down):
    width = wq.shape[0]
    sd = lambda *shape: jax.ShapeDtypeStruct(shape, BF)
    here = lambda v: pltpu.with_memory_space_constraint(v, pltpu.HBM)
    vmem = pl.BlockSpec()
    return pl.pallas_call(
        prep_kernel,
        in_specs=[pl.BlockSpec(memory_space=pltpu.SMEM)] + [vmem] * 6,
        out_shape=[sd(4 * PAIR, width), sd(4 * PAIR, width), sd(2, *up.shape)],
        compiler_params=params(8),
        cost_estimate=cost(2),
        name="prep",
    )(core.reshape(1), *map(here, (wq, wk, wv, wo, up, down)))


def finish_kernel(core_ref, mine_ref, other_ref, dq_ref, dk_ref, dv_ref, og_ref, *refs):
    width = dq_ref.shape[0]
    own = core_ref[0] == 0
    mine, other = mine_ref[...].astype(F32), other_ref[...].astype(F32)
    left, right = jnp.where(own, mine, other), jnp.where(own, other, mine)
    for i, ref in enumerate((dq_ref, dk_ref, dv_ref)):
        cols = slice(i * PAIR, (i + 1) * PAIR)
        ref[:, :PAIR] = left[:width, cols]
        ref[:, PAIR:] = right[:width, cols]
    og_ref[:PAIR, :] = left[:width, 3 * PAIR:].T
    og_ref[PAIR:, :] = right[:width, 3 * PAIR:].T
    for i in range(4):
        refs[i][...] = mine[width + i:width + i + 1]


def finish(core, mine, other):
    width = mine.shape[1]
    sd = lambda *shape: jax.ShapeDtypeStruct(shape, F32)
    vmem = pl.BlockSpec(memory_space=pltpu.VMEM)
    *dw, og, v0, v1, v2, v3 = pl.pallas_call(
        finish_kernel,
        in_specs=[pl.BlockSpec(memory_space=pltpu.SMEM)] + [vmem] * 2,
        out_shape=[sd(width, 2 * PAIR)] * 3 + [sd(2 * PAIR, width)] + [sd(1, width)] * 4,
        compiler_params=params(8),
        cost_estimate=cost(3),
        name="finish",
    )(core.reshape(1), mine, other)
    return dw, og, [v.reshape(width) for v in (v0, v1, v2, v3)]


def after(value, *earlier):
    return lax.optimization_barrier((value, earlier))[0]


def body(
    dp_size,
    head_size,
    stream_x,
    stream_y,
    segments,
    keep_mask,
    query_weight,
    key_weight,
    value_weight,
    output_weight,
    first_gain,
    first_shift,
    up_weight,
    down_weight,
    second_gain,
    second_shift,
    grad_stream,
    grad_dual,
):
    seq, width = stream_x.shape
    cols = query_weight.shape[1]
    scale = 1.0 / math.sqrt(width // HEADS)
    total = dp_size * head_size
    core_step = head_size
    head_steps = [1 << b for b in range(head_size.bit_length() - 1)]
    chip_steps = [core_step << b for b in range(1, dp_size.bit_length() - 1)]
    fast = cols == 2 * PAIR and head_size == 2

    def swap(value, even_step, odd_step=None):
        odd_step = even_step if odd_step is None else odd_step
        pairs = [
            (i, i ^ (odd_step if i // core_step % 2 else even_step)) for i in range(total)
        ]
        return lax.ppermute(value, ("dp", "head"), pairs)

    def pick(low, first, second):
        return jnp.where(low, first, second)

    index = lax.axis_index("dp") * head_size + lax.axis_index("head")
    bit_of = lambda step: (index >> (step.bit_length() - 1)) & 1
    core = bit_of(core_step)
    row = lambda vec: vec.reshape(1, width)
    g1, b1, g2, b2 = row(first_gain), row(first_shift), row(second_gain), row(second_shift)

    even = [chip_steps[-1]] + chip_steps[:-1] + head_steps
    odd = [chip_steps[-1]] + chip_steps[1:-1] + head_steps + chip_steps[:1]
    steps = list(zip(even, odd))

    tokens = lambda v: lax.dynamic_slice_in_dim(v.reshape(-1, 128), lax.axis_index("head") * (seq // 128), seq // 128)
    mask, xt = make_mask(stream_x, tokens(segments), tokens(keep_mask))
    fwd = functools.partial(attn_fwd, xt, mask=mask, scale=scale)

    if fast:
        s0, s1, s2 = chip_steps
        bit0, bit1 = bit_of(s0), bit_of(s1)
        core, first_low, second_low = lax.optimization_barrier((core, pick(core == 0, bit0, bit1) == 0, pick(core == 0, bit1, bit0) == 0))
        mine, other, ffw = prep(core, query_weight, key_weight, value_weight, output_weight, up_weight, down_weight)
        far_mine = swap(mine, head_steps[0])
        got = swap(ffw, *steps[0])
        near = fwd(mine, slot=1)
        ffw = jnp.concatenate([ffw, after(got, near[1])], axis=1)
        got = swap(ffw, *steps[1])
        near = fwd(after(other, ffw), slot=0, held=near)
        ffw = jnp.concatenate([ffw, after(got, near[1])], axis=1)
        got = swap(ffw, *steps[2])
        far_mine = after(far_mine, near[1])
        far_other = swap(far_mine, core_step)
        far = fwd(after(far_mine, ffw), slot=1)
        ffw = jnp.concatenate([ffw, after(got, far[1])], axis=1)
        got = swap(ffw, *steps[3])
        part = swap(ffw, core_step)
        far = fwd(after(far_other, ffw), slot=0, held=far)
        weights = [other, mine, far_other, far_mine]
        side_a = [ffw, part]
    else:
        ffw = jnp.stack([up_weight, down_weight])
        stacked = jnp.stack([query_weight.T, key_weight.T, value_weight.T, output_weight])
        for step in head_steps:
            stacked = jnp.concatenate([stacked, swap(stacked, step)], axis=1)
        weights = [stacked[:, i:i + PAIR].reshape(4 * PAIR, width) for i in range(0, width, PAIR)]
        near = fwd(weights[1], slot=1, held=fwd(weights[0], slot=0))
        far = fwd(weights[3], slot=1, held=fwd(weights[2], slot=0))
        for a, b in steps[:-1]:
            ffw = jnp.concatenate([ffw, swap(ffw, a, b)], axis=1)
        got = swap(ffw, *steps[-1])
        side_a = [ffw, swap(ffw, core_step)]

    low, act_a, der_a, *kept = first_part(stream_x, stream_y, [near[1], far[1]], weights, side_a, g1, b1)
    got = after(got, low)
    side_b = [got, swap(got, core_step)]
    ns, nd, act_b, dh, gf, gm, gb, do_near, do_far, vec = second_part(
        grad_stream, grad_dual, low, der_a, *kept, weights, side_a, side_b, g1, g2, b2
    )

    ffgrad = lambda which, *earlier: wgrad(act_a, act_b, after(dh, *earlier), gf, low, which)

    def bwd(group, do, *earlier):
        qkv, att, inv, prob = group
        return attn_bwd(xt, qkv, att, after(do, *earlier), gb, inv, vec, prob, scale)

    def halves(own, received):
        n = own.shape[1] // 2
        return own[:, n:] + received[:, n:], own[:, :n] + received[:, :n]

    g_far, pay_far_other, pay_far = bwd(far, do_far)
    if fast:
        crossed_pay = swap(pay_far_other, core_step)
        theirs = ffgrad(1, pay_far)
        crossed = swap(theirs, core_step)
        pay_far = pay_far + after(crossed_pay, theirs)
        from_head = swap(pay_far, head_steps[0])
        g_near, pay_other, pay_mine = bwd(near, do_near, pay_far)
        crossed_pay = swap(pay_other, core_step)
        ours = ffgrad(0, pay_mine)
        whole = pay_mine + after(crossed_pay, ours) + from_head
        whole = jnp.concatenate([whole[:width], pay_far[width:] + from_head[width:]], axis=0)

        def split(low, value):
            n = value.shape[0] // 2
            return pick(low, value[n:], value[:n]), pick(low, value[:n], value[n:])

        def merge(low, own, received):
            return pick(low, jnp.concatenate([own, received]), jnp.concatenate([received, own]))

        sent, kept = split(first_low, whole)
        got = swap(sent, s0, s1)
        crossed, ours = after((crossed, ours), sent)
        part_b = ours[1] + crossed[1]
        recv = swap(part_b, *steps[3])
        part = ours[0] + crossed[0]
        sg = sgrad(gm, [g_near, after(g_far, part_b)], weights)
        sent, kept = split(second_low, kept + after(got, part, sg))
        got = swap(sent, s1, s0)
        whole = kept + got
        got = swap(whole, s2)
        sent, part = halves(part, after(recv, whole))
        recv = swap(sent, *steps[2])
        whole = whole + after(got, sent)
        got = swap(whole, s1, s0)
        sent, part = halves(part, after(recv, whole))
        recv = swap(sent, *steps[1])
        whole = merge(second_low, whole, after(got, sent))
        got = swap(whole, s0, s1)
        sent, part = halves(part, after(recv, whole))
        recv = swap(sent, *steps[0])
        whole = merge(first_low, whole, after(got, sent))
        got = swap(whole, core_step)
        part = part.astype(F32) + recv.astype(F32)
        dw, out_grad, vec = finish(core, whole, got)
    else:
        g_near, pay_near_other, pay_near = bwd(near, do_near)
        crossed = swap(ffgrad(1), core_step)
        ours = ffgrad(0)
        part = ours[0] + crossed[0] + swap(ours[1] + crossed[1], *steps[-1])
        for a, b in steps[-2::-1]:
            n = part.shape[1] // 2
            recv = swap(part[:, n:], a, b)
            part = part[:, :n].astype(F32) + recv.astype(F32)
            part = part.astype(BF) if n > up_weight.shape[0] else part
        pays = [pay_near_other, pay_near, pay_far_other, pay_far]
        low_vec = pay_near[width:]
        pays = jnp.stack([pay[:width] for pay in pays]).reshape(len(pays), width, 4, PAIR)
        pays = pays.transpose(2, 1, 0, 3).reshape(4, width, width)
        for step in head_steps[::-1]:
            n = pays.shape[2] // 2
            pays = pays[:, :, :n] + swap(pays[:, :, n:], step)
            low_vec = low_vec + swap(low_vec, step)
        for step in [core_step] + chip_steps:
            pays = pays + swap(pays, step)
            low_vec = low_vec + swap(low_vec, step)
        pays = pays.astype(F32)
        dw, out_grad = [pays[0], pays[1], pays[2]], pays[3].T
        vec = low_vec[:4].astype(F32)
        sg = sgrad(gm, [g_near, g_far], weights)

    return (
        ns, nd, sg, dw[0], dw[1], dw[2], out_grad,
        vec[0], vec[1], part[0], part[1], vec[2], vec[3],
    )


def solution(mesh):
    both = ("dp", "head")
    rows, cols, whole = P(both, None), P(None, "head"), P()
    in_specs = (
        rows, rows, P("dp"), P("dp"), cols, cols, cols, P("head", None),
        whole, whole, rows, rows, whole, whole, rows, rows,
    )
    out_specs = (
        rows, rows, rows, cols, cols, cols, P("head", None),
        whole, whole, rows, rows, whole, whole,
    )
    inner = functools.partial(body, mesh.shape["dp"], mesh.shape["head"])
    return jax.shard_map(inner, mesh=mesh, in_specs=in_specs, out_specs=out_specs, check_vma=False)
```

```python
import functools
import math

import jax
import jax.numpy as jnp
from jax import lax
from jax.experimental import pallas as pl
from jax.experimental.pallas import tpu as pltpu
from jax.sharding import PartitionSpec as P

HEADS = 8
BF = jnp.bfloat16
F32 = jnp.float32
LOG2E = 1.4426950408889634
NEG = -1e30
BLK = 256
MIB = 1 << 20
PAIR = 128
EXTRA = 32
STREAM = 512
LIM1 = 12
LIM2 = 16
VMEM = 58


def dot(a, b, left, right):
    return lax.dot_general(a, b, (((left,), (right,)), ((), ())), preferred_element_type=F32)


def nn(a, b):
    return dot(a, b, 1, 0)


def nt(a, b):
    return dot(a, b, 1, 1)


def tn(a, b):
    return dot(a, b, 0, 0)


def params(mib):
    return pltpu.CompilerParams(vmem_limit_bytes=mib * MIB)


def cost(us):
    return pl.CostEstimate(flops=int(us * 1e9), bytes_accessed=1 << 20, transcendentals=0)


def mask_kernel(x_ref, seg_ref, keep_ref, mask_ref, xt_ref):
    seq = x_ref.shape[0]
    seg = seg_ref[...]
    code = jnp.where(keep_ref[...] == 1, seg, -1).astype(F32)
    seg = seg.astype(F32)
    line = lambda v: jnp.concatenate([v[i:i + 1] for i in range(v.shape[0])], axis=1)
    seg_row = line(seg)
    code_col = jnp.broadcast_to(line(code), (128, seq)).T
    at = 0
    for kb in range(seq // BLK):
        rows = slice(kb * BLK, (kb + 1) * BLK)
        width = seq - kb * BLK
        same = jnp.concatenate([code_col[rows]] * (width // 128), axis=1) == seg_row[:, kb * BLK:]
        key = lax.broadcasted_iota(jnp.int32, (BLK, BLK), 0)
        query = lax.broadcasted_iota(jnp.int32, (BLK, BLK), 1)
        own = (same[:, :BLK] & (key <= query)) | (key == query)
        mask_ref[:, at:at + BLK] = jnp.where(own, 0.0, NEG)
        if width > BLK:
            mask_ref[:, at + BLK:at + width] = jnp.where(same[:, BLK:], 0.0, NEG)
        at += width
    xt_ref[...] = x_ref[...].T


def make_mask(x, seg, keep):
    seq, width = x.shape
    blocks = seq // BLK
    return pl.pallas_call(
        mask_kernel,
        out_shape=[jax.ShapeDtypeStruct((BLK, BLK * blocks * (blocks + 1) // 2), F32), jax.ShapeDtypeStruct((width, seq), BF)],
        compiler_params=params(10),
        cost_estimate=cost(2),
        name="make_mask",
    )(x, seg, keep)


def offset(kb, seq):
    return sum(seq - i * BLK for i in range(kb))


def block_at(kb, qb):
    at = qb * (qb + 1) // 2 + kb
    return slice(at * BLK, (at + 1) * BLK)


def attn_fwd_kernel(scale, slot, xt_ref, w_ref, mask_ref, *refs):
    qkv_ref, att_ref, inv_ref, prob_hbm, prob_ref, sems = refs[-6:]
    seq = xt_ref.shape[1]
    copies = []
    qkv_ref[...] = nn(w_ref[:3 * PAIR], xt_ref[...]).astype(BF)
    for h in range(2):
        head = lambda i: slice(i * PAIR + 64 * h, i * PAIR + 64 * h + 64)
        keys = qkv_ref[head(1), :].T
        for qb in reversed(range(seq // BLK)):
            cols = slice(qb * BLK, (qb + 1) * BLK)
            q = qkv_ref[head(0), cols]
            scores = []
            for kb in range(qb + 1):
                at = offset(kb, seq) + (qb - kb) * BLK
                scores.append(nn(keys[kb * BLK:(kb + 1) * BLK], q) * (scale * LOG2E) + mask_ref[:, at:at + BLK])
            m = functools.reduce(jnp.maximum, [jnp.max(s, axis=0, keepdims=True) for s in scores])
            out, l = 0.0, 0.0
            for kb, s in enumerate(scores):
                p = jnp.exp2(s - m)
                l = l + jnp.sum(p, axis=0, keepdims=True)
                p = p.astype(BF)
                prob_ref[h, :, block_at(kb, qb)] = p
                out = out + nn(qkv_ref[head(2), kb * BLK:(kb + 1) * BLK], p)
            inv = 1.0 / l
            att_ref[head(0), cols] = (out * inv).astype(BF)
            inv_ref[h:h + 1, cols] = inv
            span = slice(block_at(0, qb).start, block_at(qb, qb).stop)
            copies.append(pltpu.make_async_copy(prob_ref.at[h, :, span], prob_hbm.at[slot, h, :, span], sems.at[len(copies)]))
            copies[-1].start()
    for copy in copies:
        copy.wait()


def attn_fwd(xt, w, mask, scale, slot, held=()):
    width, seq = xt.shape
    full = lambda shape: pl.BlockSpec(shape, lambda p: (0,) * len(shape))
    own = lambda rows: pl.BlockSpec((None, rows, seq), lambda p: (slot, 0, 0))
    return pl.pallas_call(
        functools.partial(attn_fwd_kernel, scale, slot),
        grid=(1,),
        in_specs=[full((width, seq)), full(w.shape), full(mask.shape)] + [pl.BlockSpec(memory_space=pl.ANY)] * len(held),
        out_specs=[own(3 * PAIR), own(PAIR), own(2), pl.BlockSpec(memory_space=pl.ANY)],
        out_shape=[jax.ShapeDtypeStruct((2, 3 * PAIR, seq), BF), jax.ShapeDtypeStruct((2, PAIR, seq), BF), jax.ShapeDtypeStruct((2, 2, seq), F32), pltpu.HBM((2, 2, *mask.shape), BF)],
        scratch_shapes=[pltpu.VMEM((2, *mask.shape), BF), pltpu.SemaphoreType.DMA((2 * (seq // BLK),))],
        input_output_aliases={3 + i: i for i in range(len(held))},
        compiler_params=params(12),
        cost_estimate=cost(5),
        name="attn_fwd",
    )(xt, w, mask, *held)


def attn_bwd_kernel(scale, xt_ref, qkv_ref, att_ref, do_ref, gb_ref, inv_ref, vec_ref, prob_ref, g_ref, other_ref, mine_ref, pay_ref, dq_ref):
    width, seq = xt_ref.shape
    dq_ref[...] = jnp.zeros_like(dq_ref)
    for h in range(2):
        head = lambda i: slice(i * PAIR + 64 * h, i * PAIR + 64 * h + 64)
        own = head(0)
        values = qkv_ref[head(2), :].T
        scaled = do_ref[own, :].astype(F32) * inv_ref[h:h + 1, :]
        delta = jnp.sum(scaled * att_ref[own, :].astype(F32), axis=0, keepdims=True)
        scaled = scaled.astype(BF)
        for kb in range(seq // BLK):
            rows = slice(kb * BLK, (kb + 1) * BLK)
            lo = kb * BLK
            q, dout = qkv_ref[own, lo:], scaled[:, lo:]
            p = jnp.concatenate([prob_ref[h, :, block_at(kb, qb)] for qb in range(kb, seq // BLK)], axis=1)
            ds = (p.astype(F32) * (nn(values[rows], dout) - delta[:, lo:])).astype(BF)
            g_ref[head(2), rows] = nt(dout, p).astype(BF)
            g_ref[head(1), rows] = (nt(q, ds) * scale).astype(BF)
            dq_ref[own, lo:] += nn(qkv_ref[head(1), rows], ds)
    g_ref[0:PAIR, :] = (dq_ref[...] * scale).astype(BF)
    pay_ref[0:width, 0:3 * PAIR] = nt(xt_ref[...], g_ref[...]).astype(BF)
    pay_ref[0:width, 3 * PAIR:] = nt(gb_ref[...], att_ref[...]).astype(BF)
    pay_ref[width:, :] = jnp.concatenate([vec_ref[...], jnp.zeros((EXTRA - 8, 4 * PAIR), F32)], axis=0).astype(BF)

    @pl.when(pl.program_id(0) == 0)
    def _():
        other_ref[...] = pay_ref[...]

    @pl.when(pl.program_id(0) == 1)
    def _():
        mine_ref[...] = pay_ref[...]


def attn_bwd(xt, qkv, att, do, gb, inv, vec, prob, scale):
    width, seq = xt.shape
    full = lambda shape: pl.BlockSpec(shape, lambda p: (0,) * len(shape))
    own = lambda rows: pl.BlockSpec((None, rows, seq), lambda p: (p, 0, 0))
    pay = (width + EXTRA, 4 * PAIR)
    return pl.pallas_call(
        functools.partial(attn_bwd_kernel, scale),
        grid=(2,),
        in_specs=[full((width, seq)), own(3 * PAIR), own(PAIR), own(PAIR), full((width, seq)), own(2), full(vec.shape), pl.BlockSpec((None, *prob.shape[1:]), lambda p: (p, 0, 0, 0))],
        out_specs=[own(3 * PAIR), full(pay), full(pay)],
        out_shape=[pltpu.HBM((2, 3 * PAIR, seq), BF), jax.ShapeDtypeStruct(pay, BF), jax.ShapeDtypeStruct(pay, BF)],
        scratch_shapes=[pltpu.VMEM(pay, BF), pltpu.VMEM((PAIR, seq), F32)],
        compiler_params=params(12),
        cost_estimate=cost(11),
        name="attn_bwd",
    )(xt, qkv, att, do, gb, inv, vec, prob)


def gelu_parts(h):
    phi = 0.5 * lax.erf(h * math.sqrt(0.5)) + 0.5
    slope = jnp.exp2(h * h * (-0.5 * LOG2E)) * (1.0 / math.sqrt(2.0 * math.pi))
    return h * phi, phi + h * slope


def mean_of(v):
    return jnp.sum(v, axis=-1, keepdims=True) * (1.0 / v.shape[-1])


def normed(z):
    c = z - mean_of(z)
    rstd = lax.rsqrt(mean_of(c * c) + 1e-5)
    return c * rstd, rstd


def norm_back(w, zhat, rstd):
    return rstd * (w - mean_of(w) - zhat * mean_of(w * zhat))


def row_specs(blk):
    row = lambda w: pl.BlockSpec((blk, w), lambda p: (p, 0))
    full = lambda shape: pl.BlockSpec(shape, lambda p: (0,) * len(shape))
    return row, full


def column(rows, blk):
    return pl.BlockSpec((2, rows, blk), lambda p: (0, 0, p))


def joined(refs):
    return jnp.concatenate([ref[i] for ref in refs for i in range(2)], axis=0)


def out_spec(width):
    return pl.BlockSpec((PAIR, width), lambda p: (3, 0))


def first_kernel(pairs, pieces, x_ref, y_ref, *refs):
    att, refs = refs[:pairs // 2], refs[pairs // 2:]
    wo, refs = refs[:pairs], refs[pairs:]
    ffw, refs = refs[:pieces], refs[pieces:]
    g1_ref, b1_ref, low_ref, act_ref, der_ref, zhat_ref, rstd_ref, sum_ref, dual_ref = refs
    branch = nn(joined(att).T, jnp.concatenate([w[...] for w in wo], axis=0))
    zhat, rstd = normed(x_ref[...].astype(F32) + branch)
    zhat_ref[...] = zhat.astype(BF)
    rstd_ref[...] = jnp.broadcast_to(rstd, rstd_ref.shape)
    first = zhat * g1_ref[...] + b1_ref[...]
    low = first.astype(BF)
    low_ref[...] = low
    acts = []
    at = 0
    for w in ffw:
        n = w.shape[1]
        val, der = gelu_parts(nt(low, w[0]))
        acts.append(val.astype(BF))
        act_ref[:, at:at + n] = acts[-1]
        der_ref[:, at:at + n] = der.astype(BF)
        at += n
    ffn = nn(jnp.concatenate(acts, axis=1), jnp.concatenate([w[1] for w in ffw], axis=0))
    sum_ref[...] = first + ffn
    dual_ref[...] = y_ref[...].astype(F32) + branch + ffn


def first_part(x, y, att, wo, ffw, g1, b1, blk=512):
    seq, width = x.shape
    ff = sum(w.shape[1] for w in ffw)
    row, full = row_specs(blk)
    sd = lambda w, t: jax.ShapeDtypeStruct((seq, w), t)
    return pl.pallas_call(
        functools.partial(first_kernel, len(wo), len(ffw)),
        grid=(seq // blk,),
        in_specs=[row(width)] * 2 + [column(PAIR, blk)] * len(att) + [out_spec(width)] * len(wo) + [full(w.shape) for w in ffw] + [full((1, width))] * 2,
        out_specs=[row(width), row(ff), row(ff), row(width), row(PAIR), row(width), row(width)],
        out_shape=[sd(width, BF), sd(ff, BF), sd(ff, BF), sd(width, BF), sd(PAIR, F32), sd(width, F32), sd(width, F32)],
        compiler_params=params(12),
        cost_estimate=cost(8),
        name="first_part",
    )(x, y, *att, *wo, *ffw, g1, b1)


def second_rows(rows, wo, ffa, ffb, gs_ref, gd_ref, low_ref, der_a_ref, zhat_ref, rstd_ref, sum_ref, dual_ref,
                g1_ref, g2_ref, b2_ref, ns_ref, nd_ref, act_ref, dh_ref, gf_ref, gm_ref, gb_ref, *rest):
    do, vec_ref = rest[:-1], rest[-1]
    low = low_ref[rows, :]
    ders, acts = [], []
    at = 0
    for w in ffa:
        ders.append(der_a_ref[rows, at:at + w.shape[1]])
        at += w.shape[1]
    at = 0
    for w in ffb:
        n = w.shape[1]
        val, der = gelu_parts(nt(low, w[0]))
        acts.append(val.astype(BF))
        ders.append(der.astype(BF))
        act_ref[rows, at:at + n] = acts[-1]
        at += n
        yield True
    ffn = nn(jnp.concatenate(acts, axis=1), jnp.concatenate([w[1] for w in ffb], axis=0))
    yield True
    zhat2, rstd2 = normed(sum_ref[rows, :] + ffn)
    ns_ref[rows, :] = (zhat2 * g2_ref[...] + b2_ref[...]).astype(BF)
    nd_ref[rows, :] = (dual_ref[rows, :] + ffn).astype(BF)
    u = gs_ref[rows, :].astype(F32)
    second = norm_back(u * g2_ref[...], zhat2, rstd2)
    gd = gd_ref[rows, :].astype(F32)
    gf = (second + gd).astype(BF)
    gf_ref[rows, :] = gf
    fold = lambda v: jnp.sum(v, axis=0, keepdims=True)
    vec = [fold(u * zhat2), fold(u)]
    yield True
    dhs = []
    at = 0
    for w, der in zip(ffa + ffb, ders):
        n = w.shape[1]
        dhs.append((nt(gf, w[1]) * der.astype(F32)).astype(BF))
        dh_ref[rows, at:at + n] = dhs[-1]
        at += n
        yield True
    gfirst = second + nn(jnp.concatenate(dhs, axis=1), jnp.concatenate([w[0] for w in ffa + ffb], axis=0))
    yield True
    zhat1 = zhat_ref[rows, :].astype(F32)
    gm = norm_back(gfirst * g1_ref[...], zhat1, rstd_ref[rows, :1])
    gm_ref[rows, :] = gm
    gb = (gm + gd).astype(BF)
    gb_ref[:, rows] = gb.T
    vec_ref[...] += jnp.concatenate([fold(gfirst * zhat1), fold(gfirst), *vec, jnp.zeros((4, u.shape[1]), F32)], axis=0)
    yield True
    dout = nt(gb, wo).astype(BF).T
    for i in range(2 * len(do)):
        do[i // 2][i % 2, :, rows] = dout[i * PAIR:(i + 1) * PAIR]
    yield True


def interleave(streams):
    waiting, running = list(streams), []
    while waiting or running:
        if waiting:
            running.append(waiting.pop(0))
        for stream in running[:]:
            if next(stream, None) is None:
                running.remove(stream)


def second_kernel(pairs, pa, pb, *refs):
    data, refs = refs[:8], refs[8:]
    wo, refs = refs[:pairs], refs[pairs:]
    ffa, refs = refs[:pa], refs[pa:]
    ffb, refs = refs[:pb], refs[pb:]
    vec_ref = refs[-1]

    @pl.when(pl.program_id(0) == 0)
    def _():
        vec_ref[...] = jnp.zeros_like(vec_ref)

    wo = jnp.concatenate([w[...] for w in wo], axis=0)
    rows = data[0].shape[0]
    interleave(second_rows(slice(lo, lo + STREAM), wo, ffa, ffb, *data, *refs) for lo in range(0, rows, STREAM))


def second_part(gs, gd, low, der, zhat, rstd, total, dual, wo, ffa, ffb, g1, g2, b2, blk=512):
    seq, width = gs.shape
    fa, fb = sum(w.shape[1] for w in ffa), sum(w.shape[1] for w in ffb)
    row, full = row_specs(blk)
    sd = lambda w, t: jax.ShapeDtypeStruct((seq, w), t)
    return pl.pallas_call(
        functools.partial(second_kernel, len(wo), len(ffa), len(ffb)),
        grid=(seq // blk,),
        in_specs=[row(width)] * 3 + [row(fa), row(width), row(PAIR), row(width), row(width)] + [out_spec(width)] * len(wo) + [full(w.shape) for w in (*ffa, *ffb)] + [full((1, width))] * 3,
        out_specs=[row(width), row(width), row(fb), row(fa + fb), row(width), row(width), pl.BlockSpec((width, blk), lambda p: (0, p))] + [column(PAIR, blk)] * (len(wo) // 2) + [full((8, width))],
        out_shape=[sd(width, BF), sd(width, BF), sd(fb, BF), sd(fa + fb, BF), sd(width, BF), pltpu.HBM((seq, width), F32), jax.ShapeDtypeStruct((width, seq), BF)] + [jax.ShapeDtypeStruct((2, PAIR, seq), BF)] * (len(wo) // 2) + [jax.ShapeDtypeStruct((8, width), F32)],
        compiler_params=params(12),
        cost_estimate=cost(18),
        name="second_part",
    )(gs, gd, low, der, zhat, rstd, total, dual, *wo, *ffa, *ffb, g1, g2, b2)


def wgrad_kernel(which, act_a_ref, act_b_ref, dh_ref, gf_ref, low_ref, out_ref):
    piece = act_a_ref.shape[1] // 2
    for side, act_ref in enumerate((act_a_ref, act_b_ref)):
        at = (2 * side + which) * piece
        out_ref[side, 0] = tn(dh_ref[:, at:at + piece], low_ref[...]).astype(BF)
        out_ref[side, 1] = tn(act_ref[:, which * piece:(which + 1) * piece], gf_ref[...]).astype(BF)


def wgrad(act_a, act_b, dh, gf, low, which):
    width = gf.shape[1]
    return pl.pallas_call(
        functools.partial(wgrad_kernel, which),
        out_shape=jax.ShapeDtypeStruct((2, 2, act_a.shape[1] // 2, width), BF),
        compiler_params=params(12),
        cost_estimate=cost(6),
        name="wgrad",
    )(act_a, act_b, dh, gf, low)


def sgrad_kernel(pairs, gm_ref, *refs):
    g, refs = refs[:pairs // 2], refs[pairs // 2:]
    w, (out_ref,) = refs[:pairs], refs[pairs:]
    left = joined(g).T
    out_ref[...] = gm_ref[...] + nn(left, jnp.concatenate([a[...] for a in w], axis=0))


def sgrad(gm, g, w, blk=256):
    seq, width = gm.shape
    row, full = row_specs(blk)
    return pl.pallas_call(
        functools.partial(sgrad_kernel, len(w)),
        grid=(seq // blk,),
        in_specs=[row(width)] + [column(3 * PAIR, blk)] * len(g) + [full((3 * PAIR, width))] * len(w),
        out_specs=row(width),
        out_shape=jax.ShapeDtypeStruct((seq, width), F32),
        compiler_params=params(8),
        cost_estimate=cost(4),
        name="sgrad",
    )(gm, *g, *w)


def prep_kernel(place_ref, wq_ref, wk_ref, wv_ref, wo_ref, up_ref, down_ref, mine_ref, other_ref, ffw_ref):
    ffw_ref[0] = up_ref[...]
    ffw_ref[1] = down_ref[...]
    for out_ref, which in ((mine_ref, place_ref[0]), (other_ref, 1 - place_ref[0])):
        part = pl.ds(pl.multiple_of(which * PAIR, PAIR), PAIR)
        for i, ref in enumerate((wq_ref, wk_ref, wv_ref)):
            out_ref[i * PAIR:(i + 1) * PAIR, :] = ref[:, part].T
        out_ref[3 * PAIR:, :] = wo_ref[part, :]


def prep(core, wq, wk, wv, wo, up, down):
    width = wq.shape[0]
    sd = lambda *shape: jax.ShapeDtypeStruct(shape, BF)
    here = lambda v: pltpu.with_memory_space_constraint(v, pltpu.HBM)
    vmem = pl.BlockSpec()
    return pl.pallas_call(
        prep_kernel,
        in_specs=[pl.BlockSpec(memory_space=pltpu.SMEM)] + [vmem] * 6,
        out_shape=[sd(4 * PAIR, width), sd(4 * PAIR, width), sd(2, *up.shape)],
        compiler_params=params(8),
        cost_estimate=cost(2),
        name="prep",
    )(core.reshape(1), *map(here, (wq, wk, wv, wo, up, down)))


def finish_kernel(core_ref, mine_ref, other_ref, dq_ref, dk_ref, dv_ref, og_ref, *refs):
    width = dq_ref.shape[0]
    own = core_ref[0] == 0
    mine, other = mine_ref[...].astype(F32), other_ref[...].astype(F32)
    left, right = jnp.where(own, mine, other), jnp.where(own, other, mine)
    for i, ref in enumerate((dq_ref, dk_ref, dv_ref)):
        cols = slice(i * PAIR, (i + 1) * PAIR)
        ref[:, :PAIR] = left[:width, cols]
        ref[:, PAIR:] = right[:width, cols]
    og_ref[:PAIR, :] = left[:width, 3 * PAIR:].T
    og_ref[PAIR:, :] = right[:width, 3 * PAIR:].T
    for i in range(4):
        refs[i][...] = mine[width + i:width + i + 1]


def finish(core, mine, other):
    width = mine.shape[1]
    sd = lambda *shape: jax.ShapeDtypeStruct(shape, F32)
    vmem = pl.BlockSpec(memory_space=pltpu.VMEM)
    *dw, og, v0, v1, v2, v3 = pl.pallas_call(
        finish_kernel,
        in_specs=[pl.BlockSpec(memory_space=pltpu.SMEM)] + [vmem] * 2,
        out_shape=[sd(width, 2 * PAIR)] * 3 + [sd(2 * PAIR, width)] + [sd(1, width)] * 4,
        compiler_params=params(8),
        cost_estimate=cost(3),
        name="finish",
    )(core.reshape(1), mine, other)
    return dw, og, [v.reshape(width) for v in (v0, v1, v2, v3)]


def after(value, *earlier):
    return lax.optimization_barrier((value, earlier))[0]


def body(
    dp_size,
    head_size,
    stream_x,
    stream_y,
    segments,
    keep_mask,
    query_weight,
    key_weight,
    value_weight,
    output_weight,
    first_gain,
    first_shift,
    up_weight,
    down_weight,
    second_gain,
    second_shift,
    grad_stream,
    grad_dual,
):
    seq, width = stream_x.shape
    cols = query_weight.shape[1]
    scale = 1.0 / math.sqrt(width // HEADS)
    total = dp_size * head_size
    core_step = head_size
    head_steps = [1 << b for b in range(head_size.bit_length() - 1)]
    chip_steps = [core_step << b for b in range(1, dp_size.bit_length() - 1)]
    fast = cols == 2 * PAIR and head_size == 2

    def swap(value, even_step, odd_step=None):
        odd_step = even_step if odd_step is None else odd_step
        pairs = [
            (i, i ^ (odd_step if i // core_step % 2 else even_step)) for i in range(total)
        ]
        return lax.ppermute(value, ("dp", "head"), pairs)

    def pick(low, first, second):
        return jnp.where(low, first, second)

    index = lax.axis_index("dp") * head_size + lax.axis_index("head")
    bit_of = lambda step: (index >> (step.bit_length() - 1)) & 1
    core = bit_of(core_step)
    row = lambda vec: vec.reshape(1, width)
    g1, b1, g2, b2 = row(first_gain), row(first_shift), row(second_gain), row(second_shift)

    even = [chip_steps[-1]] + chip_steps[:-1] + head_steps
    odd = [chip_steps[-1]] + chip_steps[1:-1] + head_steps + chip_steps[:1]
    steps = list(zip(even, odd))

    tokens = lambda v: lax.dynamic_slice_in_dim(v.reshape(-1, 128), lax.axis_index("head") * (seq // 128), seq // 128)
    mask, xt = make_mask(stream_x, tokens(segments), tokens(keep_mask))
    fwd = functools.partial(attn_fwd, xt, mask=mask, scale=scale)

    if fast:
        s0, s1, s2 = chip_steps
        bit0, bit1 = bit_of(s0), bit_of(s1)
        core, first_low, second_low = lax.optimization_barrier((core, pick(core == 0, bit0, bit1) == 0, pick(core == 0, bit1, bit0) == 0))
        mine, other, ffw = prep(core, query_weight, key_weight, value_weight, output_weight, up_weight, down_weight)
        far_mine = swap(mine, head_steps[0])
        got = swap(ffw, *steps[0])
        near = fwd(mine, slot=1)
        ffw = jnp.concatenate([ffw, after(got, near[1])], axis=1)
        got = swap(ffw, *steps[1])
        near = fwd(after(other, ffw), slot=0, held=near)
        ffw = jnp.concatenate([ffw, after(got, near[1])], axis=1)
        got = swap(ffw, *steps[2])
        far_mine = after(far_mine, near[1])
        far_other = swap(far_mine, core_step)
        far = fwd(after(far_mine, ffw), slot=1)
        ffw = jnp.concatenate([ffw, after(got, far[1])], axis=1)
        got = swap(ffw, *steps[3])
        part = swap(ffw, core_step)
        far = fwd(after(far_other, ffw), slot=0, held=far)
        weights = [other, mine, far_other, far_mine]
        side_a = [ffw, part]
    else:
        ffw = jnp.stack([up_weight, down_weight])
        stacked = jnp.stack([query_weight.T, key_weight.T, value_weight.T, output_weight])
        for step in head_steps:
            stacked = jnp.concatenate([stacked, swap(stacked, step)], axis=1)
        weights = [stacked[:, i:i + PAIR].reshape(4 * PAIR, width) for i in range(0, width, PAIR)]
        near = fwd(weights[1], slot=1, held=fwd(weights[0], slot=0))
        far = fwd(weights[3], slot=1, held=fwd(weights[2], slot=0))
        for a, b in steps[:-1]:
            ffw = jnp.concatenate([ffw, swap(ffw, a, b)], axis=1)
        got = swap(ffw, *steps[-1])
        side_a = [ffw, swap(ffw, core_step)]

    low, act_a, der_a, *kept = first_part(stream_x, stream_y, [near[1], far[1]], weights, side_a, g1, b1)
    got = after(got, low)
    side_b = [got, swap(got, core_step)]
    ns, nd, act_b, dh, gf, gm, gb, do_near, do_far, vec = second_part(
        grad_stream, grad_dual, low, der_a, *kept, weights, side_a, side_b, g1, g2, b2
    )

    ffgrad = lambda which, *earlier: wgrad(act_a, act_b, after(dh, *earlier), gf, low, which)

    def bwd(group, do, *earlier):
        qkv, att, inv, prob = group
        return attn_bwd(xt, qkv, att, after(do, *earlier), gb, inv, vec, prob, scale)

    def halves(own, received, groups=1):
        pairs, rows, _ = own.shape
        cut = lambda v: v.reshape(pairs, groups, 2, -1, width)
        own, received = cut(own), cut(received)
        both = [(own[:, :, i] + received[:, :, i]).reshape(pairs, rows // 2, width) for i in range(2)]
        return both[1], both[0]

    g_far, pay_far_other, pay_far = bwd(far, do_far)
    if fast:
        crossed_pay = swap(pay_far_other, core_step)
        theirs = ffgrad(1, pay_far)
        crossed = swap(theirs, core_step)
        pay_far = pay_far + after(crossed_pay, theirs)
        from_head = swap(pay_far, head_steps[0])
        g_near, pay_other, pay_mine = bwd(near, do_near, pay_far)
        crossed_pay = swap(pay_other, core_step)
        ours = ffgrad(0, pay_mine)
        part_b = ours[1] + crossed[1]
        recv = swap(part_b, *steps[3])
        part = ours[0] + crossed[0]
        crossed_pay, from_head = after((crossed_pay, from_head), part_b)
        whole = pay_mine + crossed_pay + from_head
        whole = jnp.concatenate([whole[:width], pay_far[width:] + from_head[width:]], axis=0)

        def split(low, value):
            n = value.shape[0] // 2
            return pick(low, value[n:], value[:n]), pick(low, value[:n], value[n:])

        def merge(low, own, received):
            return pick(low, jnp.concatenate([own, received]), jnp.concatenate([received, own]))

        sent, kept = split(first_low, whole)
        got = swap(sent, s0, s1)
        sg = sgrad(gm, [g_near, after(g_far, sent)], weights)
        sent, kept = split(second_low, kept + after(got, part, sg))
        got = swap(sent, s1, s0)
        sent, part = halves(part, after(recv, sent), 2)
        recv = swap(sent, *steps[1])
        whole = kept + after(got, sent)
        got = swap(whole, s2)
        sent, part = halves(part, after(recv, sent))
        recv = swap(sent, *steps[2])
        whole = whole + after(got, sent)
        got = swap(whole, s1, s0)
        whole = merge(second_low, whole, got)
        got = swap(whole, s0, s1)
        sent, part = halves(part, after(recv, whole))
        recv = swap(sent, *steps[0])
        whole = merge(first_low, whole, after(got, sent))
        got = swap(whole, core_step)
        part = part.astype(F32) + recv.astype(F32)
        dw, out_grad, vec = finish(core, whole, got)
    else:
        g_near, pay_near_other, pay_near = bwd(near, do_near)
        crossed = swap(ffgrad(1), core_step)
        ours = ffgrad(0)
        part = ours[0] + crossed[0] + swap(ours[1] + crossed[1], *steps[-1])
        for a, b in steps[-2::-1]:
            n = part.shape[1] // 2
            recv = swap(part[:, n:], a, b)
            part = part[:, :n].astype(F32) + recv.astype(F32)
            part = part.astype(BF) if n > up_weight.shape[0] else part
        pays = [pay_near_other, pay_near, pay_far_other, pay_far]
        low_vec = pay_near[width:]
        pays = jnp.stack([pay[:width] for pay in pays]).reshape(len(pays), width, 4, PAIR)
        pays = pays.transpose(2, 1, 0, 3).reshape(4, width, width)
        for step in head_steps[::-1]:
            n = pays.shape[2] // 2
            pays = pays[:, :, :n] + swap(pays[:, :, n:], step)
            low_vec = low_vec + swap(low_vec, step)
        for step in [core_step] + chip_steps:
            pays = pays + swap(pays, step)
            low_vec = low_vec + swap(low_vec, step)
        pays = pays.astype(F32)
        dw, out_grad = [pays[0], pays[1], pays[2]], pays[3].T
        vec = low_vec[:4].astype(F32)
        sg = sgrad(gm, [g_near, g_far], weights)

    return (
        ns, nd, sg, dw[0], dw[1], dw[2], out_grad,
        vec[0], vec[1], part[0], part[1], vec[2], vec[3],
    )


def solution(mesh):
    both = ("dp", "head")
    rows, cols, whole = P(both, None), P(None, "head"), P()
    in_specs = (
        rows, rows, P("dp"), P("dp"), cols, cols, cols, P("head", None),
        whole, whole, rows, rows, whole, whole, rows, rows,
    )
    out_specs = (
        rows, rows, rows, cols, cols, cols, P("head", None),
        whole, whole, rows, rows, whole, whole,
    )
    inner = functools.partial(body, mesh.shape["dp"], mesh.shape["head"])
    return jax.shard_map(inner, mesh=mesh, in_specs=in_specs, out_specs=out_specs, check_vma=False)
```

```python
import functools
import math

import jax
import jax.numpy as jnp
from jax import lax
from jax.experimental import pallas as pl
from jax.experimental.pallas import tpu as pltpu
from jax.sharding import PartitionSpec as P

HEADS = 8
BF = jnp.bfloat16
F32 = jnp.float32
LOG2E = 1.4426950408889634
NEG = -1e30
BLK = 256
MIB = 1 << 20
PAIR = 128
EXTRA = 32
STREAM = 512
LIM1 = 12
LIM2 = 16
VMEM = 58


def dot(a, b, left, right):
    return lax.dot_general(a, b, (((left,), (right,)), ((), ())), preferred_element_type=F32)


def nn(a, b):
    return dot(a, b, 1, 0)


def nt(a, b):
    return dot(a, b, 1, 1)


def tn(a, b):
    return dot(a, b, 0, 0)


def params(mib):
    return pltpu.CompilerParams(vmem_limit_bytes=mib * MIB)


def cost(us):
    return pl.CostEstimate(flops=int(us * 1e9), bytes_accessed=1 << 20, transcendentals=0)


def mask_kernel(x_ref, seg_ref, keep_ref, mask_ref, xt_ref):
    seq = x_ref.shape[0]
    seg = seg_ref[...]
    code = jnp.where(keep_ref[...] == 1, seg, -1).astype(F32)
    seg = seg.astype(F32)
    line = lambda v: jnp.concatenate([v[i:i + 1] for i in range(v.shape[0])], axis=1)
    seg_row = line(seg)
    code_col = jnp.broadcast_to(line(code), (128, seq)).T
    at = 0
    for kb in range(seq // BLK):
        rows = slice(kb * BLK, (kb + 1) * BLK)
        width = seq - kb * BLK
        same = jnp.concatenate([code_col[rows]] * (width // 128), axis=1) == seg_row[:, kb * BLK:]
        key = lax.broadcasted_iota(jnp.int32, (BLK, BLK), 0)
        query = lax.broadcasted_iota(jnp.int32, (BLK, BLK), 1)
        own = (same[:, :BLK] & (key <= query)) | (key == query)
        mask_ref[:, at:at + BLK] = jnp.where(own, 0.0, NEG)
        if width > BLK:
            mask_ref[:, at + BLK:at + width] = jnp.where(same[:, BLK:], 0.0, NEG)
        at += width
    xt_ref[...] = x_ref[...].T


def make_mask(x, seg, keep):
    seq, width = x.shape
    blocks = seq // BLK
    return pl.pallas_call(
        mask_kernel,
        out_shape=[jax.ShapeDtypeStruct((BLK, BLK * blocks * (blocks + 1) // 2), F32), jax.ShapeDtypeStruct((width, seq), BF)],
        compiler_params=params(10),
        cost_estimate=cost(2),
        name="make_mask",
    )(x, seg, keep)


def offset(kb, seq):
    return sum(seq - i * BLK for i in range(kb))


def block_at(kb, qb):
    at = qb * (qb + 1) // 2 + kb
    return slice(at * BLK, (at + 1) * BLK)


def attn_fwd_kernel(scale, slot, xt_ref, w_ref, mask_ref, *refs):
    qkv_ref, att_ref, inv_ref, prob_hbm, prob_ref, sems = refs[-6:]
    seq = xt_ref.shape[1]
    copies = []
    qkv_ref[...] = nn(w_ref[:3 * PAIR], xt_ref[...]).astype(BF)
    for h in range(2):
        head = lambda i: slice(i * PAIR + 64 * h, i * PAIR + 64 * h + 64)
        keys = qkv_ref[head(1), :].T
        for qb in reversed(range(seq // BLK)):
            cols = slice(qb * BLK, (qb + 1) * BLK)
            q = qkv_ref[head(0), cols]
            scores = []
            for kb in range(qb + 1):
                at = offset(kb, seq) + (qb - kb) * BLK
                scores.append(nn(keys[kb * BLK:(kb + 1) * BLK], q) * (scale * LOG2E) + mask_ref[:, at:at + BLK])
            m = functools.reduce(jnp.maximum, [jnp.max(s, axis=0, keepdims=True) for s in scores])
            out, l = 0.0, 0.0
            for kb, s in enumerate(scores):
                p = jnp.exp2(s - m)
                l = l + jnp.sum(p, axis=0, keepdims=True)
                p = p.astype(BF)
                prob_ref[h, :, block_at(kb, qb)] = p
                out = out + nn(qkv_ref[head(2), kb * BLK:(kb + 1) * BLK], p)
            inv = 1.0 / l
            att_ref[head(0), cols] = (out * inv).astype(BF)
            inv_ref[h:h + 1, cols] = inv
            span = slice(block_at(0, qb).start, block_at(qb, qb).stop)
            copies.append(pltpu.make_async_copy(prob_ref.at[h, :, span], prob_hbm.at[slot, h, :, span], sems.at[len(copies)]))
            copies[-1].start()
    for copy in copies:
        copy.wait()


def attn_fwd(xt, w, mask, scale, slot, held=()):
    width, seq = xt.shape
    full = lambda shape: pl.BlockSpec(shape, lambda p: (0,) * len(shape))
    own = lambda rows: pl.BlockSpec((None, rows, seq), lambda p: (slot, 0, 0))
    return pl.pallas_call(
        functools.partial(attn_fwd_kernel, scale, slot),
        grid=(1,),
        in_specs=[full((width, seq)), full(w.shape), full(mask.shape)] + [pl.BlockSpec(memory_space=pl.ANY)] * len(held),
        out_specs=[own(3 * PAIR), own(PAIR), own(2), pl.BlockSpec(memory_space=pl.ANY)],
        out_shape=[jax.ShapeDtypeStruct((2, 3 * PAIR, seq), BF), jax.ShapeDtypeStruct((2, PAIR, seq), BF), jax.ShapeDtypeStruct((2, 2, seq), F32), pltpu.HBM((2, 2, *mask.shape), BF)],
        scratch_shapes=[pltpu.VMEM((2, *mask.shape), BF), pltpu.SemaphoreType.DMA((2 * (seq // BLK),))],
        input_output_aliases={3 + i: i for i in range(len(held))},
        compiler_params=params(12),
        cost_estimate=cost(5),
        name="attn_fwd",
    )(xt, w, mask, *held)


def attn_bwd_kernel(scale, xt_ref, qkv_ref, att_ref, do_ref, gb_ref, inv_ref, vec_ref, prob_ref, g_ref, other_ref, mine_ref, pay_ref, dq_ref):
    width, seq = xt_ref.shape
    dq_ref[...] = jnp.zeros_like(dq_ref)
    for h in range(2):
        head = lambda i: slice(i * PAIR + 64 * h, i * PAIR + 64 * h + 64)
        own = head(0)
        values = qkv_ref[head(2), :].T
        scaled = do_ref[own, :].astype(F32) * inv_ref[h:h + 1, :]
        delta = jnp.sum(scaled * att_ref[own, :].astype(F32), axis=0, keepdims=True)
        scaled = scaled.astype(BF)
        for kb in range(seq // BLK):
            rows = slice(kb * BLK, (kb + 1) * BLK)
            lo = kb * BLK
            q, dout = qkv_ref[own, lo:], scaled[:, lo:]
            p = jnp.concatenate([prob_ref[h, :, block_at(kb, qb)] for qb in range(kb, seq // BLK)], axis=1)
            ds = (p.astype(F32) * (nn(values[rows], dout) - delta[:, lo:])).astype(BF)
            g_ref[head(2), rows] = nt(dout, p).astype(BF)
            g_ref[head(1), rows] = (nt(q, ds) * scale).astype(BF)
            dq_ref[own, lo:] += nn(qkv_ref[head(1), rows], ds)
    g_ref[0:PAIR, :] = (dq_ref[...] * scale).astype(BF)
    pay_ref[0:width, 0:3 * PAIR] = nt(xt_ref[...], g_ref[...]).astype(BF)
    pay_ref[0:width, 3 * PAIR:] = nt(gb_ref[...], att_ref[...]).astype(BF)
    pay_ref[width:, :] = jnp.concatenate([vec_ref[...], jnp.zeros((EXTRA - 8, 4 * PAIR), F32)], axis=0).astype(BF)

    @pl.when(pl.program_id(0) == 0)
    def _():
        other_ref[...] = pay_ref[...]

    @pl.when(pl.program_id(0) == 1)
    def _():
        mine_ref[...] = pay_ref[...]


def attn_bwd(xt, qkv, att, do, gb, inv, vec, prob, scale):
    width, seq = xt.shape
    full = lambda shape: pl.BlockSpec(shape, lambda p: (0,) * len(shape))
    own = lambda rows: pl.BlockSpec((None, rows, seq), lambda p: (p, 0, 0))
    pay = (width + EXTRA, 4 * PAIR)
    return pl.pallas_call(
        functools.partial(attn_bwd_kernel, scale),
        grid=(2,),
        in_specs=[full((width, seq)), own(3 * PAIR), own(PAIR), own(PAIR), full((width, seq)), own(2), full(vec.shape), pl.BlockSpec((None, *prob.shape[1:]), lambda p: (p, 0, 0, 0))],
        out_specs=[own(3 * PAIR), full(pay), full(pay)],
        out_shape=[pltpu.HBM((2, 3 * PAIR, seq), BF), jax.ShapeDtypeStruct(pay, BF), jax.ShapeDtypeStruct(pay, BF)],
        scratch_shapes=[pltpu.VMEM(pay, BF), pltpu.VMEM((PAIR, seq), F32)],
        compiler_params=params(12),
        cost_estimate=cost(11),
        name="attn_bwd",
    )(xt, qkv, att, do, gb, inv, vec, prob)


def attn_bwd_both_kernel(scale, xt_ref, qkv_ref, att_all_ref, do_ref, gb_ref, inv_ref, vec_ref, prob_ref, g_all_ref, other_ref, mine_ref, dq_ref):
    width, seq = xt_ref.shape
    step = pl.program_id(0)
    att_ref, g_ref = att_all_ref.at[step], g_all_ref.at[step]
    dq_ref[...] = jnp.zeros_like(dq_ref)
    for h in range(2):
        head = lambda i: slice(i * PAIR + 64 * h, i * PAIR + 64 * h + 64)
        own = head(0)
        values = qkv_ref[head(2), :].T
        scaled = do_ref[own, :].astype(F32) * inv_ref[h:h + 1, :]
        delta = jnp.sum(scaled * att_ref[own, :].astype(F32), axis=0, keepdims=True)
        scaled = scaled.astype(BF)
        for kb in range(seq // BLK):
            rows = slice(kb * BLK, (kb + 1) * BLK)
            lo = kb * BLK
            q, dout = qkv_ref[own, lo:], scaled[:, lo:]
            p = jnp.concatenate([prob_ref[h, :, block_at(kb, qb)] for qb in range(kb, seq // BLK)], axis=1)
            ds = (p.astype(F32) * (nn(values[rows], dout) - delta[:, lo:])).astype(BF)
            g_ref[head(2), rows] = nt(dout, p).astype(BF)
            g_ref[head(1), rows] = (nt(q, ds) * scale).astype(BF)
            dq_ref[own, lo:] += nn(qkv_ref[head(1), rows], ds)
    g_ref[0:PAIR, :] = (dq_ref[...] * scale).astype(BF)

    @pl.when(step == 1)
    def _():
        grads = nt(xt_ref[...], jnp.concatenate([g_all_ref[0], g_all_ref[1]], axis=0)).astype(BF)
        out = nt(gb_ref[...], jnp.concatenate([att_all_ref[0], att_all_ref[1]], axis=0)).astype(BF)
        vec = jnp.concatenate([vec_ref[...], jnp.zeros((EXTRA - 8, 4 * PAIR), F32)], axis=0).astype(BF)
        for i, ref in enumerate((other_ref, mine_ref)):
            ref[0:width, 0:3 * PAIR] = grads[:, 3 * PAIR * i:3 * PAIR * (i + 1)]
            ref[0:width, 3 * PAIR:] = out[:, PAIR * i:PAIR * (i + 1)]
            ref[width:, :] = vec


def attn_bwd_both(xt, qkv, att, do, gb, inv, vec, prob, scale):
    width, seq = xt.shape
    full = lambda shape: pl.BlockSpec(shape, lambda p: (0,) * len(shape))
    own = lambda rows: pl.BlockSpec((None, rows, seq), lambda p: (p, 0, 0))
    pay = (width + EXTRA, 4 * PAIR)
    return pl.pallas_call(
        functools.partial(attn_bwd_both_kernel, scale),
        grid=(2,),
        in_specs=[full((width, seq)), own(3 * PAIR), full((2, PAIR, seq)), own(PAIR), full((width, seq)), own(2), full(vec.shape), pl.BlockSpec((None, *prob.shape[1:]), lambda p: (p, 0, 0, 0))],
        out_specs=[full((2, 3 * PAIR, seq)), full(pay), full(pay)],
        out_shape=[jax.ShapeDtypeStruct((2, 3 * PAIR, seq), BF), jax.ShapeDtypeStruct(pay, BF), jax.ShapeDtypeStruct(pay, BF)],
        scratch_shapes=[pltpu.VMEM((PAIR, seq), F32)],
        compiler_params=params(12),
        cost_estimate=cost(11),
        name="attn_bwd_both",
    )(xt, qkv, att, do, gb, inv, vec, prob)


def gelu_parts(h):
    phi = 0.5 * lax.erf(h * math.sqrt(0.5)) + 0.5
    slope = jnp.exp2(h * h * (-0.5 * LOG2E)) * (1.0 / math.sqrt(2.0 * math.pi))
    return h * phi, phi + h * slope


def mean_of(v):
    return jnp.sum(v, axis=-1, keepdims=True) * (1.0 / v.shape[-1])


def normed(z):
    c = z - mean_of(z)
    rstd = lax.rsqrt(mean_of(c * c) + 1e-5)
    return c * rstd, rstd


def norm_back(w, zhat, rstd):
    return rstd * (w - mean_of(w) - zhat * mean_of(w * zhat))


def row_specs(blk):
    row = lambda w: pl.BlockSpec((blk, w), lambda p: (p, 0))
    full = lambda shape: pl.BlockSpec(shape, lambda p: (0,) * len(shape))
    return row, full


def column(rows, blk):
    return pl.BlockSpec((2, rows, blk), lambda p: (0, 0, p))


def joined(refs):
    return jnp.concatenate([ref[i] for ref in refs for i in range(2)], axis=0)


def out_spec(width):
    return pl.BlockSpec((PAIR, width), lambda p: (3, 0))


def first_kernel(pairs, pieces, x_ref, y_ref, *refs):
    att, refs = refs[:pairs // 2], refs[pairs // 2:]
    wo, refs = refs[:pairs], refs[pairs:]
    ffw, refs = refs[:pieces], refs[pieces:]
    g1_ref, b1_ref, low_ref, act_ref, der_ref, zhat_ref, rstd_ref, sum_ref, dual_ref = refs
    branch = nn(joined(att).T, jnp.concatenate([w[...] for w in wo], axis=0))
    zhat, rstd = normed(x_ref[...].astype(F32) + branch)
    zhat_ref[...] = zhat.astype(BF)
    rstd_ref[...] = jnp.broadcast_to(rstd, rstd_ref.shape)
    first = zhat * g1_ref[...] + b1_ref[...]
    low = first.astype(BF)
    low_ref[...] = low
    acts = []
    at = 0
    for w in ffw:
        n = w.shape[1]
        val, der = gelu_parts(nt(low, w[0]))
        acts.append(val.astype(BF))
        act_ref[:, at:at + n] = acts[-1]
        der_ref[:, at:at + n] = der.astype(BF)
        at += n
    ffn = nn(jnp.concatenate(acts, axis=1), jnp.concatenate([w[1] for w in ffw], axis=0))
    sum_ref[...] = first + ffn
    dual_ref[...] = y_ref[...].astype(F32) + branch + ffn


def first_part(x, y, att, wo, ffw, g1, b1, blk=512):
    seq, width = x.shape
    ff = sum(w.shape[1] for w in ffw)
    row, full = row_specs(blk)
    sd = lambda w, t: jax.ShapeDtypeStruct((seq, w), t)
    return pl.pallas_call(
        functools.partial(first_kernel, len(wo), len(ffw)),
        grid=(seq // blk,),
        in_specs=[row(width)] * 2 + [column(PAIR, blk)] * len(att) + [out_spec(width)] * len(wo) + [full(w.shape) for w in ffw] + [full((1, width))] * 2,
        out_specs=[row(width), row(ff), row(ff), row(width), row(PAIR), row(width), row(width)],
        out_shape=[sd(width, BF), sd(ff, BF), sd(ff, BF), sd(width, BF), sd(PAIR, F32), sd(width, F32), sd(width, F32)],
        compiler_params=params(12),
        cost_estimate=cost(8),
        name="first_part",
    )(x, y, *att, *wo, *ffw, g1, b1)


def second_rows(rows, wo, ffa, ffb, gs_ref, gd_ref, low_ref, der_a_ref, zhat_ref, rstd_ref, sum_ref, dual_ref,
                g1_ref, g2_ref, b2_ref, ns_ref, nd_ref, act_ref, dh_ref, gf_ref, gm_ref, gb_ref, *rest):
    do, vec_ref = rest[:-1], rest[-1]
    low = low_ref[rows, :]
    ders, acts = [], []
    at = 0
    for w in ffa:
        ders.append(der_a_ref[rows, at:at + w.shape[1]])
        at += w.shape[1]
    at = 0
    for w in ffb:
        n = w.shape[1]
        val, der = gelu_parts(nt(low, w[0]))
        acts.append(val.astype(BF))
        ders.append(der.astype(BF))
        act_ref[rows, at:at + n] = acts[-1]
        at += n
        yield True
    ffn = nn(jnp.concatenate(acts, axis=1), jnp.concatenate([w[1] for w in ffb], axis=0))
    yield True
    zhat2, rstd2 = normed(sum_ref[rows, :] + ffn)
    ns_ref[rows, :] = (zhat2 * g2_ref[...] + b2_ref[...]).astype(BF)
    nd_ref[rows, :] = (dual_ref[rows, :] + ffn).astype(BF)
    u = gs_ref[rows, :].astype(F32)
    second = norm_back(u * g2_ref[...], zhat2, rstd2)
    gd = gd_ref[rows, :].astype(F32)
    gf = (second + gd).astype(BF)
    gf_ref[rows, :] = gf
    fold = lambda v: jnp.sum(v, axis=0, keepdims=True)
    vec = [fold(u * zhat2), fold(u)]
    yield True
    dhs = []
    at = 0
    for w, der in zip(ffa + ffb, ders):
        n = w.shape[1]
        dhs.append((nt(gf, w[1]) * der.astype(F32)).astype(BF))
        dh_ref[rows, at:at + n] = dhs[-1]
        at += n
        yield True
    gfirst = second + nn(jnp.concatenate(dhs, axis=1), jnp.concatenate([w[0] for w in ffa + ffb], axis=0))
    yield True
    zhat1 = zhat_ref[rows, :].astype(F32)
    gm = norm_back(gfirst * g1_ref[...], zhat1, rstd_ref[rows, :1])
    gm_ref[rows, :] = gm
    gb = (gm + gd).astype(BF)
    gb_ref[:, rows] = gb.T
    vec_ref[...] += jnp.concatenate([fold(gfirst * zhat1), fold(gfirst), *vec, jnp.zeros((4, u.shape[1]), F32)], axis=0)
    yield True
    dout = nt(gb, wo).astype(BF).T
    for i in range(2 * len(do)):
        do[i // 2][i % 2, :, rows] = dout[i * PAIR:(i + 1) * PAIR]
    yield True


def interleave(streams):
    waiting, running = list(streams), []
    while waiting or running:
        if waiting:
            running.append(waiting.pop(0))
        for stream in running[:]:
            if next(stream, None) is None:
                running.remove(stream)


def second_kernel(pairs, pa, pb, *refs):
    data, refs = refs[:8], refs[8:]
    wo, refs = refs[:pairs], refs[pairs:]
    ffa, refs = refs[:pa], refs[pa:]
    ffb, refs = refs[:pb], refs[pb:]
    vec_ref = refs[-1]

    @pl.when(pl.program_id(0) == 0)
    def _():
        vec_ref[...] = jnp.zeros_like(vec_ref)

    wo = jnp.concatenate([w[...] for w in wo], axis=0)
    rows = data[0].shape[0]
    interleave(second_rows(slice(lo, lo + STREAM), wo, ffa, ffb, *data, *refs) for lo in range(0, rows, STREAM))


def second_part(gs, gd, low, der, zhat, rstd, total, dual, wo, ffa, ffb, g1, g2, b2, blk=512):
    seq, width = gs.shape
    fa, fb = sum(w.shape[1] for w in ffa), sum(w.shape[1] for w in ffb)
    row, full = row_specs(blk)
    sd = lambda w, t: jax.ShapeDtypeStruct((seq, w), t)
    return pl.pallas_call(
        functools.partial(second_kernel, len(wo), len(ffa), len(ffb)),
        grid=(seq // blk,),
        in_specs=[row(width)] * 3 + [row(fa), row(width), row(PAIR), row(width), row(width)] + [out_spec(width)] * len(wo) + [full(w.shape) for w in (*ffa, *ffb)] + [full((1, width))] * 3,
        out_specs=[row(width), row(width), row(fb), row(fa + fb), row(width), row(width), pl.BlockSpec((width, blk), lambda p: (0, p))] + [column(PAIR, blk)] * (len(wo) // 2) + [full((8, width))],
        out_shape=[sd(width, BF), sd(width, BF), sd(fb, BF), sd(fa + fb, BF), sd(width, BF), pltpu.HBM((seq, width), F32), jax.ShapeDtypeStruct((width, seq), BF)] + [jax.ShapeDtypeStruct((2, PAIR, seq), BF)] * (len(wo) // 2) + [jax.ShapeDtypeStruct((8, width), F32)],
        compiler_params=params(12),
        cost_estimate=cost(18),
        name="second_part",
    )(gs, gd, low, der, zhat, rstd, total, dual, *wo, *ffa, *ffb, g1, g2, b2)


def wgrad_kernel(which, act_a_ref, act_b_ref, dh_ref, gf_ref, low_ref, out_ref):
    piece = act_a_ref.shape[1] // 2
    for side, act_ref in enumerate((act_a_ref, act_b_ref)):
        at = (2 * side + which) * piece
        out_ref[side, 0] = tn(dh_ref[:, at:at + piece], low_ref[...]).astype(BF)
        out_ref[side, 1] = tn(act_ref[:, which * piece:(which + 1) * piece], gf_ref[...]).astype(BF)


def wgrad(act_a, act_b, dh, gf, low, which):
    width = gf.shape[1]
    return pl.pallas_call(
        functools.partial(wgrad_kernel, which),
        out_shape=jax.ShapeDtypeStruct((2, 2, act_a.shape[1] // 2, width), BF),
        compiler_params=params(12),
        cost_estimate=cost(6),
        name="wgrad",
    )(act_a, act_b, dh, gf, low)


def sgrad_kernel(pairs, gm_ref, *refs):
    g, refs = refs[:pairs // 2], refs[pairs // 2:]
    w, (out_ref,) = refs[:pairs], refs[pairs:]
    left = joined(g).T
    out_ref[...] = gm_ref[...] + nn(left, jnp.concatenate([a[...] for a in w], axis=0))


def sgrad(gm, g, w, blk=256):
    seq, width = gm.shape
    row, full = row_specs(blk)
    return pl.pallas_call(
        functools.partial(sgrad_kernel, len(w)),
        grid=(seq // blk,),
        in_specs=[row(width)] + [column(3 * PAIR, blk)] * len(g) + [full((3 * PAIR, width))] * len(w),
        out_specs=row(width),
        out_shape=jax.ShapeDtypeStruct((seq, width), F32),
        compiler_params=params(8),
        cost_estimate=cost(4),
        name="sgrad",
    )(gm, *g, *w)


def prep_kernel(place_ref, wq_ref, wk_ref, wv_ref, wo_ref, up_ref, down_ref, mine_ref, other_ref, ffw_ref):
    ffw_ref[0] = up_ref[...]
    ffw_ref[1] = down_ref[...]
    for out_ref, which in ((mine_ref, place_ref[0]), (other_ref, 1 - place_ref[0])):
        part = pl.ds(pl.multiple_of(which * PAIR, PAIR), PAIR)
        for i, ref in enumerate((wq_ref, wk_ref, wv_ref)):
            out_ref[i * PAIR:(i + 1) * PAIR, :] = ref[:, part].T
        out_ref[3 * PAIR:, :] = wo_ref[part, :]


def prep(core, wq, wk, wv, wo, up, down):
    width = wq.shape[0]
    sd = lambda *shape: jax.ShapeDtypeStruct(shape, BF)
    here = lambda v: pltpu.with_memory_space_constraint(v, pltpu.HBM)
    vmem = pl.BlockSpec()
    return pl.pallas_call(
        prep_kernel,
        in_specs=[pl.BlockSpec(memory_space=pltpu.SMEM)] + [vmem] * 6,
        out_shape=[sd(4 * PAIR, width), sd(4 * PAIR, width), sd(2, *up.shape)],
        compiler_params=params(8),
        cost_estimate=cost(2),
        name="prep",
    )(core.reshape(1), *map(here, (wq, wk, wv, wo, up, down)))


def finish_kernel(core_ref, mine_ref, other_ref, dq_ref, dk_ref, dv_ref, og_ref, *refs):
    width = dq_ref.shape[0]
    own = core_ref[0] == 0
    mine, other = mine_ref[...].astype(F32), other_ref[...].astype(F32)
    left, right = jnp.where(own, mine, other), jnp.where(own, other, mine)
    for i, ref in enumerate((dq_ref, dk_ref, dv_ref)):
        cols = slice(i * PAIR, (i + 1) * PAIR)
        ref[:, :PAIR] = left[:width, cols]
        ref[:, PAIR:] = right[:width, cols]
    og_ref[:PAIR, :] = left[:width, 3 * PAIR:].T
    og_ref[PAIR:, :] = right[:width, 3 * PAIR:].T
    for i in range(4):
        refs[i][...] = mine[width + i:width + i + 1]


def finish(core, mine, other):
    width = mine.shape[1]
    sd = lambda *shape: jax.ShapeDtypeStruct(shape, F32)
    vmem = pl.BlockSpec(memory_space=pltpu.VMEM)
    *dw, og, v0, v1, v2, v3 = pl.pallas_call(
        finish_kernel,
        in_specs=[pl.BlockSpec(memory_space=pltpu.SMEM)] + [vmem] * 2,
        out_shape=[sd(width, 2 * PAIR)] * 3 + [sd(2 * PAIR, width)] + [sd(1, width)] * 4,
        compiler_params=params(8),
        cost_estimate=cost(3),
        name="finish",
    )(core.reshape(1), mine, other)
    return dw, og, [v.reshape(width) for v in (v0, v1, v2, v3)]


def after(value, *earlier):
    return lax.optimization_barrier((value, earlier))[0]


def body(
    dp_size,
    head_size,
    stream_x,
    stream_y,
    segments,
    keep_mask,
    query_weight,
    key_weight,
    value_weight,
    output_weight,
    first_gain,
    first_shift,
    up_weight,
    down_weight,
    second_gain,
    second_shift,
    grad_stream,
    grad_dual,
):
    seq, width = stream_x.shape
    cols = query_weight.shape[1]
    scale = 1.0 / math.sqrt(width // HEADS)
    total = dp_size * head_size
    core_step = head_size
    head_steps = [1 << b for b in range(head_size.bit_length() - 1)]
    chip_steps = [core_step << b for b in range(1, dp_size.bit_length() - 1)]
    fast = cols == 2 * PAIR and head_size == 2

    def swap(value, even_step, odd_step=None):
        odd_step = even_step if odd_step is None else odd_step
        pairs = [
            (i, i ^ (odd_step if i // core_step % 2 else even_step)) for i in range(total)
        ]
        return lax.ppermute(value, ("dp", "head"), pairs)

    def pick(low, first, second):
        return jnp.where(low, first, second)

    index = lax.axis_index("dp") * head_size + lax.axis_index("head")
    bit_of = lambda step: (index >> (step.bit_length() - 1)) & 1
    core = bit_of(core_step)
    row = lambda vec: vec.reshape(1, width)
    g1, b1, g2, b2 = row(first_gain), row(first_shift), row(second_gain), row(second_shift)

    even = [chip_steps[-1]] + chip_steps[:-1] + head_steps
    odd = [chip_steps[-1]] + chip_steps[1:-1] + head_steps + chip_steps[:1]
    steps = list(zip(even, odd))

    tokens = lambda v: lax.dynamic_slice_in_dim(v.reshape(-1, 128), lax.axis_index("head") * (seq // 128), seq // 128)
    mask, xt = make_mask(stream_x, tokens(segments), tokens(keep_mask))
    fwd = functools.partial(attn_fwd, xt, mask=mask, scale=scale)

    if fast:
        s0, s1, s2 = chip_steps
        bit0, bit1 = bit_of(s0), bit_of(s1)
        core, first_low, second_low = lax.optimization_barrier((core, pick(core == 0, bit0, bit1) == 0, pick(core == 0, bit1, bit0) == 0))
        mine, other, ffw = prep(core, query_weight, key_weight, value_weight, output_weight, up_weight, down_weight)
        far_mine = swap(mine, head_steps[0])
        got = swap(ffw, *steps[0])
        near = fwd(mine, slot=1)
        ffw = jnp.concatenate([ffw, after(got, near[1])], axis=1)
        got = swap(ffw, *steps[1])
        near = fwd(after(other, ffw), slot=0, held=near)
        ffw = jnp.concatenate([ffw, after(got, near[1])], axis=1)
        got = swap(ffw, *steps[2])
        far_mine = after(far_mine, near[1])
        far_other = swap(far_mine, core_step)
        far = fwd(after(far_mine, ffw), slot=1)
        ffw = jnp.concatenate([ffw, after(got, far[1])], axis=1)
        got = swap(ffw, *steps[3])
        part = swap(ffw, core_step)
        far = fwd(after(far_other, ffw), slot=0, held=far)
        weights = [other, mine, far_other, far_mine]
        side_a = [ffw, part]
    else:
        ffw = jnp.stack([up_weight, down_weight])
        stacked = jnp.stack([query_weight.T, key_weight.T, value_weight.T, output_weight])
        for step in head_steps:
            stacked = jnp.concatenate([stacked, swap(stacked, step)], axis=1)
        weights = [stacked[:, i:i + PAIR].reshape(4 * PAIR, width) for i in range(0, width, PAIR)]
        near = fwd(weights[1], slot=1, held=fwd(weights[0], slot=0))
        far = fwd(weights[3], slot=1, held=fwd(weights[2], slot=0))
        for a, b in steps[:-1]:
            ffw = jnp.concatenate([ffw, swap(ffw, a, b)], axis=1)
        got = swap(ffw, *steps[-1])
        side_a = [ffw, swap(ffw, core_step)]

    low, act_a, der_a, *kept = first_part(stream_x, stream_y, [near[1], far[1]], weights, side_a, g1, b1)
    got = after(got, low)
    side_b = [got, swap(got, core_step)]
    ns, nd, act_b, dh, gf, gm, gb, do_near, do_far, vec = second_part(
        grad_stream, grad_dual, low, der_a, *kept, weights, side_a, side_b, g1, g2, b2
    )

    ffgrad = lambda which, *earlier: wgrad(act_a, act_b, after(dh, *earlier), gf, low, which)

    def bwd(group, do, *earlier, run=attn_bwd):
        qkv, att, inv, prob = group
        return run(xt, qkv, att, after(do, *earlier), gb, inv, vec, prob, scale)

    def halves(own, received, groups=1):
        pairs, rows, _ = own.shape
        cut = lambda v: v.reshape(pairs, groups, 2, -1, width)
        own, received = cut(own), cut(received)
        both = [(own[:, :, i] + received[:, :, i]).reshape(pairs, rows // 2, width) for i in range(2)]
        return both[1], both[0]

    g_far, pay_far_other, pay_far = bwd(far, do_far, run=attn_bwd_both)
    if fast:
        crossed_pay = swap(pay_far_other, core_step)
        theirs = ffgrad(1, pay_far)
        crossed = swap(theirs, core_step)
        pay_far = pay_far + after(crossed_pay, theirs)
        from_head = swap(pay_far, head_steps[0])
        g_near, pay_other, pay_mine = bwd(near, do_near, pay_far)
        crossed_pay = swap(pay_other, core_step)
        ours = ffgrad(0, pay_mine)
        part_b = ours[1] + crossed[1]
        recv = swap(part_b, *steps[3])
        part = ours[0] + crossed[0]
        crossed_pay, from_head = after((crossed_pay, from_head), part_b)
        whole = pay_mine + crossed_pay + from_head
        whole = jnp.concatenate([whole[:width], pay_far[width:] + from_head[width:]], axis=0)

        def split(low, value):
            n = value.shape[0] // 2
            return pick(low, value[n:], value[:n]), pick(low, value[:n], value[n:])

        def merge(low, own, received):
            return pick(low, jnp.concatenate([own, received]), jnp.concatenate([received, own]))

        sent, kept = split(first_low, whole)
        got = swap(sent, s0, s1)
        sg = sgrad(gm, [g_near, after(g_far, sent)], weights)
        sent, kept = split(second_low, kept + after(got, part, sg))
        got = swap(sent, s1, s0)
        sent, part = halves(part, after(recv, sent), 2)
        recv = swap(sent, *steps[1])
        whole = kept + after(got, sent)
        got = swap(whole, s2)
        sent, part = halves(part, after(recv, sent))
        recv = swap(sent, *steps[2])
        whole = whole + after(got, sent)
        got = swap(whole, s1, s0)
        whole = merge(second_low, whole, got)
        got = swap(whole, s0, s1)
        sent, part = halves(part, after(recv, whole))
        recv = swap(sent, *steps[0])
        whole = merge(first_low, whole, after(got, sent))
        got = swap(whole, core_step)
        part = part.astype(F32) + recv.astype(F32)
        dw, out_grad, vec = finish(core, whole, got)
    else:
        g_near, pay_near_other, pay_near = bwd(near, do_near)
        crossed = swap(ffgrad(1), core_step)
        ours = ffgrad(0)
        part = ours[0] + crossed[0] + swap(ours[1] + crossed[1], *steps[-1])
        for a, b in steps[-2::-1]:
            n = part.shape[1] // 2
            recv = swap(part[:, n:], a, b)
            part = part[:, :n].astype(F32) + recv.astype(F32)
            part = part.astype(BF) if n > up_weight.shape[0] else part
        pays = [pay_near_other, pay_near, pay_far_other, pay_far]
        low_vec = pay_near[width:]
        pays = jnp.stack([pay[:width] for pay in pays]).reshape(len(pays), width, 4, PAIR)
        pays = pays.transpose(2, 1, 0, 3).reshape(4, width, width)
        for step in head_steps[::-1]:
            n = pays.shape[2] // 2
            pays = pays[:, :, :n] + swap(pays[:, :, n:], step)
            low_vec = low_vec + swap(low_vec, step)
        for step in [core_step] + chip_steps:
            pays = pays + swap(pays, step)
            low_vec = low_vec + swap(low_vec, step)
        pays = pays.astype(F32)
        dw, out_grad = [pays[0], pays[1], pays[2]], pays[3].T
        vec = low_vec[:4].astype(F32)
        sg = sgrad(gm, [g_near, g_far], weights)

    return (
        ns, nd, sg, dw[0], dw[1], dw[2], out_grad,
        vec[0], vec[1], part[0], part[1], vec[2], vec[3],
    )


def solution(mesh):
    both = ("dp", "head")
    rows, cols, whole = P(both, None), P(None, "head"), P()
    in_specs = (
        rows, rows, P("dp"), P("dp"), cols, cols, cols, P("head", None),
        whole, whole, rows, rows, whole, whole, rows, rows,
    )
    out_specs = (
        rows, rows, rows, cols, cols, cols, P("head", None),
        whole, whole, rows, rows, whole, whole,
    )
    inner = functools.partial(body, mesh.shape["dp"], mesh.shape["head"])
    return jax.shard_map(inner, mesh=mesh, in_specs=in_specs, out_specs=out_specs, check_vma=False)
```
